32 devices in a mesh: dp: 8 (over y, x, core), tensor: 4 (over z).
Axes of the slice: x: 2, y: 2, z: 4, core: 2. Of those that a mesh axis runs over, the one named last changes fastest.
Arguments:
- tokens_in: bfloat16 [8192, 2048], P(('dp', 'tensor')), may hold values from -6 to 6
- segment_ids: int32 [8192], P('dp'), may hold values from 0 to 26, never falling along the last dimension, each value on 1 to 800 neighbouring positions
- cotangent: bfloat16 [8192, 2048], P(('dp', 'tensor')), may hold values from -6 to 6
- norm_first: bfloat16 [2048], P('dp'), may hold values from 0.5 to 1.5
- query_weight: bfloat16 [2048, 1024], P('dp', 'tensor'), may hold values from -0.125 to 0.125
- key_value_weight: bfloat16 [2048, 512], P('dp'), may hold values from -0.125 to 0.125
- output_weight: bfloat16 [1024, 2048], P('tensor', 'dp'), may hold values from -1.5 to 1.5
- inner_weight: bfloat16 [2048, 2, 3072], P('dp', None, 'tensor'), may hold values from -0.125 to 0.125
- state_weight: bfloat16 [2048, 512], P('dp'), may hold values from -0.125 to 0.125
- step_weight: bfloat16 [2048, 48], P('dp', 'tensor'), may hold values from -0.125 to 0.125
- conv_inner: bfloat16 [5, 48, 64], P(None, 'tensor'), may hold values from -0.5 to 0.5
- conv_state: bfloat16 [5, 512], replicated, may hold values from -0.5 to 0.5
- head_params: float32 [3, 48], P(None, 'tensor'), may hold values from -7 to 3, as said below
- gate_gain: bfloat16 [48, 64], P('tensor'), may hold values from 0.5 to 1.5
- mamba_weight: bfloat16 [3072, 2048], P('tensor', 'dp'), may hold values from -0.109375 to 0.109375
- norm_second: bfloat16 [2048], P('dp'), may hold values from 0.5 to 1.5
- expand_weight: bfloat16 [2048, 2, 4096], P('dp', None, 'tensor'), may hold values from -0.125 to 0.125
- shrink_weight: bfloat16 [4096, 2048], P('tensor', 'dp'), may hold values from -0.09375 to 0.09375
Outputs:
- block_out: bfloat16 [8192, 2048], P(('dp', 'tensor'))
- grad_tokens: float32 [8192, 2048], P(('dp', 'tensor'))
- grad_norm_first: float32 [2048], P(('dp', 'tensor'))
- grad_query: float32 [2048, 1024], P('dp', 'tensor')
- grad_keyval: float32 [2048, 512], P(('dp', 'tensor'))
- grad_output: float32 [1024, 2048], P('tensor', 'dp')
- grad_inner: float32 [2048, 2, 3072], P('dp', None, 'tensor')
- grad_state: float32 [2048, 512], P(('dp', 'tensor'))
- grad_step: float32 [2048, 48], P('dp', 'tensor')
- grad_conv_inner: float32 [5, 48, 64], P(None, 'tensor', 'dp')
- grad_conv_state: float32 [5, 512], P(None, ('dp', 'tensor'))
- grad_head_params: float32 [3, 48], P(None, 'tensor')
- grad_gate_gain: float32 [48, 64], P('tensor', 'dp')
- grad_mamba: float32 [3072, 2048], P('tensor', 'dp')
- grad_norm_second: float32 [2048], P(('dp', 'tensor'))
- grad_expand: float32 [2048, 2, 4096], P('dp', None, 'tensor')
- grad_shrink: float32 [4096, 2048], P('tensor', 'dp')
The draws below stay inside these ranges and needn't reach their ends.
Inputs may be any that keep to these rules, and one draw needn't show every extreme that they name: `segment_ids`: ids never fall along the tokens; each id covers 1 to 800 consecutive tokens and one covers exactly 800. `head_params`: row 0 lies in [0, log 16], row 1 is the inverse softplus of a value in [0.001, 0.1], row 2 lies in [0.5, 1.5].
All inputs are finite; a program needn't handle non-finite values.
Results may differ from the reference program's by a relative error of at most 0.025.
Values may be sent and summed in bfloat16 or wider, within the bound.
A program may use at most 320 MiB of HBM per device.

```python
import math
import jax
import jax.numpy as jnp
import numpy as np
from jax import lax

MODEL_DIM = 2048
QUERY_HEADS = 8
KEY_HEADS = 2
HEAD_SIZE = 128
HM = 48
PM = 64
NS = 256
KC = 4
FF = 4096
SEQ_LEN = 1024
DOC_MOST = 800
DOC_MEAN = 300
DSSM = 3072
TOKENS = 8192


def draw_head_params(key, part):
    key = jax.random.fold_in(key, 11)
    key_rate, key_bias, key_skip = jax.random.split(key, 3)
    log_rate = jax.random.uniform(key_rate, (HM,), jnp.float32, 0.0, math.log(16.0))
    step_base = jnp.exp(jax.random.uniform(key_bias, (HM,), jnp.float32, math.log(0.001), math.log(0.1)))
    bias_row = step_base + jnp.log(-jnp.expm1(-step_base))
    skip_row = jax.random.uniform(key_skip, (HM,), jnp.float32, 0.5, 1.5)
    return jnp.stack([log_rate, bias_row, skip_row])


def block_levels(own_key, shape, cuts, smallest, high):
    gain, own = 1.0, jax.random.fold_in(own_key, 6)
    for dim, parts in cuts:
        heights = jnp.exp(jax.random.uniform(jax.random.fold_in(own, dim), (parts,), jnp.float32, smallest / len(cuts), high / len(cuts)))
        gain = gain * jnp.repeat(heights, shape[dim] // parts).reshape([-1 if axis == dim else 1 for axis in range(len(shape))])
    return gain


def split_up(number_of, total, bound, slope):
    loads = [(1 << 20) // math.isqrt(rank ** slope) + 1 for rank in range(2, number_of + 1)]
    rest, counts = total - bound - (number_of - 1), [1] * (number_of - 1)
    while rest > 0:
        movable = [i for i in range(number_of - 1) if counts[i] < bound]
        whole, left = sum([loads[i] for i in movable]), rest
        for i in movable:
            more = min(bound - counts[i], max(1, left * loads[i] // whole), rest)
            counts[i] = counts[i] + more
            rest = rest - more
    return np.array([bound] + counts)


def uneven(stream_key, count, total, limit, slope):
    if count == 2:
        one = jax.random.randint(stream_key, (), max(1, total - limit), min(limit, total - 1) + 1)
        return jnp.stack([one, total - one])
    sizes = jnp.asarray(split_up(count, total, limit, slope), jnp.int32)
    couples = (count - 1) // 2
    giver, taker = sizes[1:1 + 2 * couples:2], sizes[2:2 + 2 * couples:2]
    margin = jnp.minimum(giver - 1, limit - taker)
    moved = jax.random.randint(jax.random.fold_in(stream_key, 1), (couples,), 0, 1 << 20) % (margin + 1)
    sizes = sizes.at[1:1 + 2 * couples:2].set(giver - moved).at[2:2 + 2 * couples:2].set(taker + moved)
    return sizes[jax.random.permutation(jax.random.fold_in(stream_key, 2), count)]


def centred(stream_key, dims, deviation, most, pieces=(), held_as=jnp.bfloat16):
    loudness = block_levels(stream_key, dims, pieces, -0.22, 0.18) if pieces else 1.0
    entries = jax.random.normal(stream_key, dims, jnp.float32) * deviation * loudness
    return jnp.minimum(jnp.maximum(entries, -most), most).astype(held_as)


def setup_inputs(seed: int = 0) -> dict:
    key_list = jax.random.split(jax.random.key(seed), 19)
    return {
        "tokens_in": centred(key_list[0], (TOKENS, MODEL_DIM), 1.0, 6.0, ((0, 32),)),
        "segment_ids": jnp.searchsorted(jnp.cumsum(uneven(key_list[1], TOKENS // DOC_MEAN, TOKENS, DOC_MOST, 0)), jnp.arange(TOKENS), side="right").astype(jnp.int32),
        "cotangent": centred(key_list[2], (TOKENS, MODEL_DIM), 1.0, 6.0, ((0, 32),)),
        "norm_first": jnp.clip(1.0 + 0.1 * jax.random.normal(key_list[3], (MODEL_DIM,), jnp.float32), 0.5, 1.5).astype(jnp.bfloat16),
        "query_weight": centred(key_list[4], (MODEL_DIM, QUERY_HEADS * HEAD_SIZE), MODEL_DIM ** -0.5, 0.125, ((0, 8), (1, 4))),
        "key_value_weight": centred(key_list[5], (MODEL_DIM, 2 * KEY_HEADS * HEAD_SIZE), MODEL_DIM ** -0.5, 0.125, ((0, 8),)),
        "output_weight": centred(key_list[6], (QUERY_HEADS * HEAD_SIZE, MODEL_DIM), (QUERY_HEADS * HEAD_SIZE // 64) ** -0.5, 1.5, ((0, 4), (1, 8))),
        "inner_weight": centred(key_list[7], (MODEL_DIM, 2, DSSM), MODEL_DIM ** -0.5, 0.125, ((0, 8), (2, 4))),
        "state_weight": centred(key_list[8], (MODEL_DIM, 2 * NS), MODEL_DIM ** -0.5, 0.125, ((0, 8),)),
        "step_weight": centred(key_list[9], (MODEL_DIM, HM), MODEL_DIM ** -0.5, 0.125, ((0, 8), (1, 4))),
        "conv_inner": jnp.clip(jax.random.uniform(key_list[10], (KC + 1, HM, PM), jnp.float32, -0.5, 0.5) * block_levels(key_list[10], (KC + 1, HM, PM), ((1, 4),), -0.4, 0.0), -0.5, 0.5).astype(jnp.bfloat16),
        "conv_state": jnp.clip(jax.random.uniform(key_list[11], (KC + 1, 2 * NS), jnp.float32, -0.5, 0.5), -0.5, 0.5).astype(jnp.bfloat16),
        "head_params": draw_head_params(jax.random.fold_in(key_list[18], 71), 0),
        "gate_gain": jnp.clip(1.0 + 0.1 * jax.random.normal(key_list[13], (HM, PM), jnp.float32), 0.5, 1.5).astype(jnp.bfloat16),
        "mamba_weight": centred(key_list[14], (DSSM, MODEL_DIM), DSSM ** -0.5, 0.109375, ((0, 4), (1, 8))),
        "norm_second": jnp.clip(1.0 + 0.1 * jax.random.normal(key_list[15], (MODEL_DIM,), jnp.float32), 0.5, 1.5).astype(jnp.bfloat16),
        "expand_weight": centred(key_list[16], (MODEL_DIM, 2, FF), MODEL_DIM ** -0.5, 0.125, ((0, 8), (2, 4))),
        "shrink_weight": centred(key_list[17], (FF, MODEL_DIM), FF ** -0.5, 0.09375, ((0, 4), (1, 8))),
    }


EPS = 1e-05
THETA = 100000000000.0
PRECISION_HIGH = lax.Precision.HIGHEST

@jax.custom_vjp
def low(v):
    return lax.optimization_barrier(v.astype(jnp.bfloat16)).astype(jnp.float32)

@jax.custom_vjp
def low_back(v):
    return v

def low_keep(v):
    return (low(v), None)

def low_pass(kept, grad):
    return (grad,)

def back_keep(v):
    return (v, None)

def back_low(kept, grad):
    return (low(grad),)
low.defvjp(low_keep, low_pass)
low_back.defvjp(back_keep, back_low)

def rms_norm(values, gain_vec):
    return values * lax.rsqrt(lax.optimization_barrier(jnp.mean(values * values, -1, keepdims=True)) + EPS) * gain_vec

def rotate(values, angles):
    halfway = values.shape[-1] // 2
    frequency = jnp.exp(jnp.arange(halfway).astype(jnp.float32) * (-2.0 * math.log(THETA) / values.shape[-1]))
    turned = angles[:, None] * frequency[None, :]
    cosine = jnp.cos(turned)[:, None, :]
    sine_part = jnp.sin(turned)[:, None, :]
    front_half = values[..., :halfway]
    back_half = values[..., halfway:]
    return jnp.concatenate([front_half * cosine - back_half * sine_part, back_half * cosine + front_half * sine_part], -1)

def short_conv(inputs, conv_weight, seg_ids, position):
    taps = conv_weight.shape[0] - 1
    segment_length = inputs.shape[0]
    result = conv_weight[taps] + conv_weight[taps - 1] * inputs
    for lag_steps in range(1, taps):
        moved = jnp.concatenate([jnp.zeros((lag_steps, inputs.shape[1]), inputs.dtype), inputs[:segment_length - lag_steps]], 0)
        earlier = jnp.concatenate([jnp.full((lag_steps,), -1, jnp.int32), seg_ids[:segment_length - lag_steps]], 0)
        keep_mask = ((earlier == seg_ids) & (position >= lag_steps)).astype(inputs.dtype)
        result = result + conv_weight[taps - 1 - lag_steps] * moved * keep_mask[:, None]
    return result

def prepare(lin_x, lin_bc, lin_dt, conv_weight, heads_vec, seg_ids, position):
    mixed = jax.nn.silu(short_conv(jnp.concatenate([lin_x, lin_bc], 1), conv_weight, seg_ids, position))
    step_size = jax.nn.softplus(lin_dt + heads_vec[1])
    return (mixed, step_size, -step_size * jnp.exp(heads_vec[0]))

def state_space(inner_x, state_b, state_c, step_size, log_decay, skip_gain, seg_ids):
    segment_length = inner_x.shape[0]
    index = jnp.arange(segment_length)
    allowed = (index[:, None] >= index[None, :]) & (seg_ids[:, None] == seg_ids[None, :])
    running = jnp.cumsum(log_decay, 0).T
    decay_gap = running[:, :, None] - running[:, None, :]
    decay = jnp.where(allowed[None], jnp.exp(jnp.where(allowed[None], decay_gap, 0.0)), 0.0)
    gram_mat = jnp.dot(state_c, state_b.T, precision=PRECISION_HIGH)
    mixing = gram_mat[None] * decay * step_size.T[:, None, :]
    return jnp.einsum('hts,shp->thp', mixing, inner_x, precision=PRECISION_HIGH) + skip_gain[None, :, None] * inner_x

def attention(query_rows, key_rows, value_rows, seg_ids):
    segment_length = query_rows.shape[0]
    repeat_factor = QUERY_HEADS // KEY_HEADS
    key_rows = jnp.repeat(key_rows, repeat_factor, axis=1)
    value_rows = jnp.repeat(value_rows, repeat_factor, axis=1)
    scores = low_back(jnp.einsum('thd,shd->hts', query_rows, key_rows, precision=PRECISION_HIGH) / math.sqrt(HEAD_SIZE))
    index = jnp.arange(segment_length)
    allowed = (index[:, None] >= index[None, :]) & (seg_ids[:, None] == seg_ids[None, :])
    scores = jnp.where(allowed[None], scores, -1e+30)
    row_top = lax.optimization_barrier(jnp.max(scores, -1, keepdims=True))
    shifted = jnp.exp(scores - row_top)
    weights_low = low(shifted / lax.optimization_barrier(jnp.sum(shifted, -1, keepdims=True)))
    return jnp.einsum('hts,shd->thd', weights_low, value_rows, precision=PRECISION_HIGH).reshape(segment_length, QUERY_HEADS * HEAD_SIZE)

def layer(params, tokens_seq, seg_ids):
    norm_first, query_weight, key_value_weight, output_weight, inner_weight, state_weight, step_weight, conv_inner, conv_state, head_params, gate_gain, mamba_weight, norm_second, expand_weight, shrink_weight = params
    segment_length = tokens_seq.shape[0]
    position = jnp.arange(segment_length).astype(jnp.int32)
    angles = position.astype(jnp.float32)
    first_norm_rows = low(rms_norm(tokens_seq, norm_first))
    query_lin = low_back(jnp.dot(first_norm_rows, query_weight, precision=PRECISION_HIGH)).reshape(segment_length, QUERY_HEADS, HEAD_SIZE)
    query_rows = low(rotate(query_lin, angles))
    pair_list = low_back(jnp.dot(first_norm_rows, key_value_weight, precision=PRECISION_HIGH)).reshape(segment_length, 2, KEY_HEADS, HEAD_SIZE)
    key_rows = low(rotate(pair_list[:, 0], angles))
    value_rows = low(pair_list[:, 1])
    attended = low(low_back(attention(query_rows, key_rows, value_rows, seg_ids)))
    inner_lin = low_back(jnp.dot(first_norm_rows, inner_weight.reshape(MODEL_DIM, 2 * DSSM), precision=PRECISION_HIGH))
    gate_lin = inner_lin[:, :DSSM]
    state_lin = low_back(jnp.dot(first_norm_rows, state_weight, precision=PRECISION_HIGH))
    step_lin = low_back(jnp.dot(first_norm_rows, step_weight, precision=PRECISION_HIGH))
    conv_weight = jnp.concatenate([conv_inner.reshape(KC + 1, DSSM), conv_state], 1)
    mixed, step_size, log_decay = prepare(inner_lin[:, DSSM:], state_lin, step_lin, conv_weight, head_params, seg_ids, position)
    mixed = low(mixed)
    ssm_out = state_space(mixed[:, :DSSM].reshape(segment_length, HM, PM), mixed[:, DSSM:DSSM + NS], mixed[:, DSSM + NS:], step_size, log_decay, head_params[2], seg_ids)
    gated = ssm_out.reshape(segment_length, DSSM) * jax.nn.silu(gate_lin)
    normed = low(rms_norm(gated, gate_gain.reshape(DSSM)))
    mix_sum = low_back(jnp.dot(attended, output_weight, precision=PRECISION_HIGH) + jnp.dot(normed, mamba_weight, precision=PRECISION_HIGH))
    middle = tokens_seq + mix_sum
    second = low(rms_norm(middle, norm_second))
    hidden_lin = low_back(jnp.dot(second, expand_weight.reshape(MODEL_DIM, 2 * FF), precision=PRECISION_HIGH))
    activated = low(jax.nn.silu(hidden_lin[:, :FF]) * hidden_lin[:, FF:])
    return middle + jnp.dot(activated, shrink_weight, precision=PRECISION_HIGH)

def reference(tokens_in, segment_ids, cotangent, norm_first, query_weight, key_value_weight, output_weight, inner_weight, state_weight, step_weight, conv_inner, conv_state, head_params, gate_gain, mamba_weight, norm_second, expand_weight, shrink_weight):
    params = tuple((weight_arr.astype(jnp.float32) for weight_arr in (norm_first, query_weight, key_value_weight, output_weight, inner_weight, state_weight, step_weight, conv_inner, conv_state, head_params, gate_gain, mamba_weight, norm_second, expand_weight, shrink_weight)))
    seq_total = tokens_in.shape[0] // SEQ_LEN
    tokens_seqs = tokens_in.astype(jnp.float32).reshape(seq_total, SEQ_LEN, MODEL_DIM)
    seg_seqs = segment_ids.reshape(seq_total, SEQ_LEN)
    layer_step = jax.checkpoint(layer)

    def whole(tokens_all, weights_all):

        def scan_step(carry, seq_items):
            return (carry, layer_step(weights_all, seq_items[0], seq_items[1]))
        return lax.scan(scan_step, jnp.zeros((), jnp.float32), (tokens_all, seg_seqs))[1]
    result, pullback = jax.vjp(whole, tokens_seqs, params)
    grad_seqs, grads = pullback(cotangent.astype(jnp.float32).reshape(seq_total, SEQ_LEN, MODEL_DIM))
    g_norm_first, g_query, g_keyval, g_output, g_inner, g_state, g_step, g_conv_inner, g_conv_state, g_heads, g_gate_gain, g_mamba, g_norm_second, g_expand, g_shrink = grads
    return (result.reshape(-1, MODEL_DIM).astype(jnp.bfloat16), grad_seqs.reshape(-1, MODEL_DIM), g_norm_first, g_query, g_keyval, g_output, g_inner, g_state, g_step, g_conv_inner, g_conv_state, g_heads, g_gate_gain, g_mamba, g_norm_second, g_expand, g_shrink)
```

```python
import functools
import math

import jax
import jax.numpy as jnp
from jax import lax
from jax.experimental import pallas as pl
from jax.experimental.pallas import tpu as pltpu
from jax.sharding import PartitionSpec as P

QUERY_HEADS = 8
KEY_HEADS = 2
HEAD_SIZE = 128
PM = 64
NS = 256
KC = 4
SEQ_LEN = 1024
DSSM = 3072
LANES = 128
CHUNK = 128
FAR = -1e30


EPS = 1e-05
THETA = 100000000000.0
HIGH = lax.Precision.HIGHEST
F32 = jnp.float32
BF16 = jnp.bfloat16


def mat(left_side, right_side):
    return jnp.dot(left_side, right_side, preferred_element_type=F32)


def mat_nt(left_side, right_side):
    return lax.dot_general(
        left_side, right_side, (((1,), (1,)), ((), ())), preferred_element_type=F32
    )


def mat_tn(left_side, right_side):
    return lax.dot_general(
        left_side, right_side, (((0,), (0,)), ((), ())), preferred_element_type=F32
    )


def iota(shape, dim):
    return lax.broadcasted_iota(jnp.int32, shape, dim)


def halves(value):
    high = value.astype(BF16)
    return high, (value - high.astype(F32)).astype(BF16)


def spread(value, heads_map):
    high, rest = halves(value)
    return mat(high, heads_map) + mat(rest, heads_map)


def gather_heads(value, heads_map):
    high, rest = halves(value)
    return mat_nt(high, heads_map) + mat_nt(rest, heads_map)


def sigmoid(value):
    return 1.0 / (1.0 + jnp.exp(-value))


def softplus(value):
    return jnp.maximum(value, 0.0) + jnp.log(1.0 + jnp.exp(-jnp.abs(value)))


def conv_rows(inputs, before, seg, seg_before, weight):
    rows = inputs.shape[0]
    longer = jnp.concatenate([before, inputs], 0)
    seg_longer = jnp.concatenate([seg_before, seg], 0)
    result = weight[KC : KC + 1] + weight[KC - 1 : KC] * inputs
    moved_list = []
    for lag in range(1, KC):
        keep = seg_longer[8 - lag : 8 - lag + rows] == seg
        moved = jnp.where(keep, longer[8 - lag : 8 - lag + rows], 0.0)
        moved_list.append(moved)
        result = result + weight[KC - 1 - lag : KC - lag] * moved
    return result, moved_list


def chunk_decay(step_lin, heads_vec, heads, seg, seg_last_before):
    rows = step_lin.shape[0]
    head_lane = iota((1, LANES), 1) < heads
    shifted = step_lin + heads_vec[1:2]
    step = jnp.where(head_lane, softplus(shifted), 0.0)
    rate = jnp.exp(heads_vec[0:1])
    log_decay = -step * rate
    lower = (iota((rows, rows), 0) >= iota((rows, rows), 1)).astype(F32)
    running = jnp.dot(lower, log_decay, precision=HIGH, preferred_element_type=F32)
    last = running[rows - 1 : rows]
    seg_last = seg[rows - 1 : rows]
    into = jnp.where(seg == seg_last_before, jnp.exp(running), 0.0)
    out = jnp.where(seg == seg_last, jnp.exp(last - running), 0.0)
    across = jnp.where(seg_last == seg_last_before, jnp.exp(last), 0.0)
    return shifted, step, rate, log_decay, running, into, out, across


def two_heads(pair):
    front = iota(pair.shape, 1) < PM
    nothing = jnp.zeros_like(pair)
    return jnp.concatenate(
        [jnp.where(front, pair, nothing), jnp.where(front, nothing, pair)], 0
    )


def pair_decay(running, running_t, bias, index):
    parts = []
    for head in (2 * index, 2 * index + 1):
        gap = running[:, head : head + 1] - running_t[head : head + 1, :] + bias
        parts.append(jnp.exp(gap))
    return parts


def as_column(row):
    return jnp.broadcast_to(row, (8, row.shape[1])).T[:, 0:1]


def row_sums_as_row(values):
    return jnp.sum(values.T, 0, keepdims=True)


def chunk_bias(seg, seg_row):
    rows = seg.shape[0]
    allowed = (iota((rows, rows), 0) >= iota((rows, rows), 1)) & (seg == seg_row)
    return jnp.where(allowed, 0.0, FAR)


def mixer_forward_kernel(
    heads, lin_ref, seg_ref, segr_ref, conv_ref, hp_ref, map_ref,
    ssm_ref, mixed_ref, sums_ref, states_ref, state, tail, seg_tail,
):
    channels = heads * PM
    rows = lin_ref.shape[0]

    @pl.when(lax.rem(pl.program_id(0), SEQ_LEN // CHUNK) == 0)
    def _():
        state[...] = jnp.zeros_like(state)
        tail[...] = jnp.zeros_like(tail)
        seg_tail[...] = jnp.full_like(seg_tail, -1)

    heads_map = map_ref[...]
    seg = seg_ref[...]
    seg_before = seg_tail[...]
    inputs = lin_ref[:, channels : 2 * channels + 2 * NS]
    conv, _ = conv_rows(inputs, tail[...], seg, seg_before, conv_ref[...])
    mixed = (conv * sigmoid(conv)).astype(BF16)
    mixed_ref[...] = mixed
    tail[...] = inputs[rows - 8 :]
    seg_tail[...] = seg[rows - 8 :]

    step_lin = lin_ref[:, 2 * channels + 2 * NS :]
    _, step, _, _, running, into, out, across = chunk_decay(
        step_lin, hp_ref[...], heads, seg, seg_before[7:8]
    )
    inner = mixed[:, :channels].astype(F32)
    state_b = mixed[:, channels : channels + NS]
    state_c = mixed[:, channels + NS :]
    few = jnp.concatenate([across, hp_ref[2:3], jnp.zeros((6, LANES), F32)], 0)
    wide = spread(jnp.concatenate([step, into, out, few], 0), heads_map)
    stepped = (inner * wide[:rows]).astype(BF16)
    leaving = (stepped.astype(F32) * wide[2 * rows : 3 * rows]).astype(BF16)
    held = state[...]
    held_low = held.astype(BF16)
    states_ref[0] = held_low
    base = wide[rows : 2 * rows] * mat(state_c, held_low) + wide[3 * rows + 1 : 3 * rows + 2] * inner
    state[...] = wide[3 * rows : 3 * rows + 1] * held + mat_tn(state_b, leaving)

    gram = mat_nt(state_c, state_b)
    bias = chunk_bias(seg, segr_ref[...])
    running_t = running.T
    total = jnp.zeros((rows, LANES), F32)
    for index in range(heads // 2):
        cols = slice(index * LANES, (index + 1) * LANES)
        first, second = pair_decay(running, running_t, bias, index)
        mixing = jnp.concatenate([first * gram, second * gram], 1).astype(BF16)
        outcome = mat(mixing, two_heads(stepped[:, cols])) + base[:, cols]
        ssm_ref[:, cols] = outcome
        gate = lin_ref[:, cols]
        gated = outcome * gate * sigmoid(gate)
        total = total + gated * gated
    sums_ref[0] = row_sums_as_row(total)


def mixer_backward_kernel(
    heads, lin_ref, before_ref, seg_ref, segb_ref, segr_ref, conv_ref, hp_ref, map_ref, gain_ref,
    gn_ref, inv_ref, cross_ref, ssm_ref, mixed_ref, states_ref,
    dlin_ref, dconv_ref, dhp_ref, dgain_ref, dstate, dnext, seg_next,
):
    channels = heads * PM
    rows = lin_ref.shape[0]
    chunks = SEQ_LEN // CHUNK
    chunk = pl.num_programs(0) - 1 - pl.program_id(0)
    place = lax.rem(chunk, chunks)

    @pl.when(pl.program_id(0) == 0)
    def _():
        dconv_ref[...] = jnp.zeros_like(dconv_ref)
        dhp_ref[...] = jnp.zeros_like(dhp_ref)
        dgain_ref[...] = jnp.zeros_like(dgain_ref)

    @pl.when(place == chunks - 1)
    def _():
        dstate[...] = jnp.zeros_like(dstate)
        dnext[...] = jnp.zeros_like(dnext)
        seg_next[...] = jnp.full_like(seg_next, -1)

    heads_map = map_ref[...]
    seg = seg_ref[...]
    seg_before = jnp.where(place == 0, -1, segb_ref[...])

    gate = lin_ref[:, :channels]
    sig = sigmoid(gate)
    silu = gate * sig
    ssm = ssm_ref[...]
    gated = ssm * silu
    grad_normed = gn_ref[...]
    inverse = as_column(inv_ref[0])
    dgain_ref[0:1] += jnp.sum(gated * inverse * grad_normed, 0, keepdims=True)
    cube = inverse * inverse * inverse * (as_column(cross_ref[0]) * (1.0 / DSSM))
    grad_gated = inverse * (grad_normed * gain_ref[...]) - gated * cube
    grad_out = grad_gated * silu
    grad_gate = grad_gated * ssm * (sig * (1.0 + gate * (1.0 - sig)))
    dlin_ref[:, :channels] = grad_gate.astype(BF16)
    grad_low = grad_out.astype(BF16)

    step_lin = lin_ref[:, 2 * channels + 2 * NS :]
    shifted, step, rate, log_decay, running, into, out, across = chunk_decay(
        step_lin, hp_ref[...], heads, seg, seg_before[7:8]
    )
    mixed = mixed_ref[...]
    inner = mixed[:, :channels].astype(F32)
    state_b = mixed[:, channels : channels + NS]
    state_c = mixed[:, channels + NS :]
    few = jnp.concatenate([across, hp_ref[2:3], jnp.zeros((6, LANES), F32)], 0)
    wide = spread(jnp.concatenate([step, into, out, few], 0), heads_map)
    step_wide = wide[:rows]
    out_wide = wide[2 * rows : 3 * rows]
    skip_wide = wide[3 * rows + 1 : 3 * rows + 2]
    stepped = (inner * step_wide).astype(BF16)
    stepped_wide = stepped.astype(F32)
    leaving = (stepped_wide * out_wide).astype(BF16)

    held = states_ref[0]
    grad_state = dstate[...]
    grad_state_low = grad_state.astype(BF16)
    grad_leaving = mat(state_b, grad_state_low)
    grad_b = mat_nt(leaving, grad_state_low)
    entering = wide[rows : 2 * rows] * grad_out
    entering_low = entering.astype(BF16)
    grad_c = mat_nt(entering_low, held)
    carried = mat(state_c, held)
    dstate[...] = wide[3 * rows : 3 * rows + 1] * grad_state + mat_tn(state_c, entering_low)
    grad_across = jnp.sum(grad_state * held.astype(F32), 0, keepdims=True)

    gram = mat_nt(state_c, state_b)
    bias = chunk_bias(seg, segr_ref[...])
    running_t = running.T
    head_lane = iota((1, LANES), 1)
    head_row = iota((LANES, 1), 0)
    grad_gram = jnp.zeros((rows, rows), F32)
    row_sums = jnp.zeros((rows, LANES), F32)
    column_sums = jnp.zeros((LANES, rows), F32)
    grad_stepped = []
    for index in range(heads // 2):
        cols = slice(index * LANES, (index + 1) * LANES)
        grads = mat_nt(grad_low[:, cols], two_heads(stepped[:, cols]))
        mixings = []
        for side, decay in enumerate(pair_decay(running, running_t, bias, index)):
            part = grads[:, side * rows : (side + 1) * rows] * decay
            grad_gram = grad_gram + part
            part = part * gram
            head = 2 * index + side
            row_sums = jnp.where(head_lane == head, jnp.sum(part, 1, keepdims=True), row_sums)
            column_sums = jnp.where(head_row == head, jnp.sum(part, 0, keepdims=True), column_sums)
            mixings.append((decay * gram).astype(BF16))
        both = mat_tn(jnp.concatenate(mixings, 1), grad_low[:, cols])
        front = iota((rows, LANES), 1) < PM
        grad_stepped.append(jnp.where(front, both[:rows], both[rows:]))
    grad_gram_low = grad_gram.astype(BF16)
    grad_c = grad_c + mat(grad_gram_low, state_b)
    grad_b = grad_b + mat_tn(grad_gram_low, state_c)
    grad_stepped = jnp.concatenate(grad_stepped, 1) + out_wide * grad_leaving
    grad_inner = grad_stepped * step_wide + skip_wide * grad_out

    few = jnp.concatenate([grad_across, jnp.zeros((7, channels), F32)], 0)
    sums = gather_heads(
        jnp.concatenate(
            [stepped_wide * grad_leaving, entering * carried, grad_stepped * inner, grad_out * inner, few], 0
        ),
        heads_map,
    )
    leave = sums[:rows] * out
    grad_running = row_sums - column_sums.T + sums[rows : 2 * rows] - leave
    grad_last = jnp.sum(leave, 0, keepdims=True) + sums[4 * rows : 4 * rows + 1] * across
    grad_running = grad_running + jnp.where(iota((rows, 1), 0) == rows - 1, grad_last, 0.0)
    upper = (iota((rows, rows), 0) <= iota((rows, rows), 1)).astype(F32)
    grad_log = jnp.dot(upper, grad_running, precision=HIGH, preferred_element_type=F32)
    grad_step = sums[2 * rows : 3 * rows] - grad_log * rate
    grad_shifted = jnp.where(head_lane < heads, grad_step * sigmoid(shifted), 0.0)
    first_spare = 2 * channels + 2 * NS + LANES
    dlin_ref[:, first_spare - LANES : first_spare] = grad_shifted.astype(BF16)
    dlin_ref[:, first_spare:] = jnp.zeros((rows, dlin_ref.shape[1] - first_spare), BF16)
    dhp_ref[0:1] += jnp.sum(grad_log * log_decay, 0, keepdims=True)
    dhp_ref[1:2] += jnp.sum(grad_shifted, 0, keepdims=True)
    dhp_ref[2:3] += jnp.sum(sums[3 * rows : 4 * rows], 0, keepdims=True)

    grad_mixed = jnp.concatenate([grad_inner, grad_b, grad_c], 1)
    weight = conv_ref[...]
    inputs = lin_ref[:, channels : 2 * channels + 2 * NS]
    before = before_ref[:, channels : 2 * channels + 2 * NS]
    conv, moved_list = conv_rows(inputs, before, seg, seg_before, weight)
    sig = sigmoid(conv)
    grad_conv = grad_mixed * (sig * (1.0 + conv * (1.0 - sig)))
    dconv_ref[KC : KC + 1] += jnp.sum(grad_conv, 0, keepdims=True)
    dconv_ref[KC - 1 : KC] += jnp.sum(grad_conv * inputs, 0, keepdims=True)
    longer = jnp.concatenate([grad_conv, dnext[...]], 0)
    seg_longer = jnp.concatenate([seg, seg_next[...]], 0)
    grad_inputs = weight[KC - 1 : KC] * grad_conv
    for lag in range(1, KC):
        tap = slice(KC - 1 - lag, KC - lag)
        dconv_ref[tap] += jnp.sum(grad_conv * moved_list[lag - 1], 0, keepdims=True)
        keep = seg_longer[lag : lag + rows] == seg
        grad_inputs = grad_inputs + weight[tap] * jnp.where(keep, longer[lag : lag + rows], 0.0)
    dlin_ref[:, channels : 2 * channels + 2 * NS] = grad_inputs.astype(BF16)
    dnext[...] = grad_conv[:8]
    seg_next[...] = seg[:8]


def whole_block(array):
    return pl.BlockSpec(array.shape, lambda *_: (0,) * array.ndim)


def mixer_forward(lin, seg, conv_weight, heads_vec, heads_map, heads):
    total = lin.shape[0]
    channels = heads * PM
    width = 2 * channels + 2 * NS + LANES
    mixed_width = channels + 2 * NS
    steps = total // CHUNK
    by_rows = lambda cols: pl.BlockSpec((CHUNK, cols), lambda c: (c, 0))
    return pl.pallas_call(
        functools.partial(mixer_forward_kernel, heads),
        grid=(steps,),
        in_specs=[
            by_rows(width),
            by_rows(1),
            pl.BlockSpec((1, CHUNK), lambda c: (0, c)),
            whole_block(conv_weight),
            whole_block(heads_vec),
            whole_block(heads_map),
        ],
        out_specs=[
            by_rows(channels),
            by_rows(mixed_width),
            pl.BlockSpec((1, 1, CHUNK), lambda c: (c, 0, 0)),
            pl.BlockSpec((1, NS, channels), lambda c: (c, 0, 0)),
        ],
        out_shape=[
            jax.ShapeDtypeStruct((total, channels), F32),
            jax.ShapeDtypeStruct((total, mixed_width), BF16),
            jax.ShapeDtypeStruct((steps, 1, CHUNK), F32),
            jax.ShapeDtypeStruct((steps, NS, channels), BF16),
        ],
        scratch_shapes=[
            pltpu.VMEM((NS, channels), F32),
            pltpu.VMEM((8, mixed_width), F32),
            pltpu.VMEM((8, 1), jnp.int32),
        ],
        compiler_params=pltpu.CompilerParams(vmem_limit_bytes=48 << 20),
        name="mixer_forward",
    )(lin, seg.reshape(total, 1), seg.reshape(1, total), conv_weight, heads_vec, heads_map)


def mixer_backward(
    lin, seg, conv_weight, heads_vec, heads_map, gain, grad_normed, inverse, cross, ssm, mixed, states, heads, lead
):
    total = lin.shape[0]
    channels = heads * PM
    width = 2 * channels + 2 * NS + LANES
    mixed_width = channels + 2 * NS
    steps = total // CHUNK
    by_rows = lambda cols: pl.BlockSpec((CHUNK, cols), lambda c: (steps - 1 - c, 0))
    ahead = lambda cols: pl.BlockSpec(
        (8, cols), lambda c: (jnp.maximum((steps - 1 - c) * (CHUNK // 8) - 1, 0), 0)
    )
    seg_column = seg.reshape(total, 1)
    return pl.pallas_call(
        functools.partial(mixer_backward_kernel, heads),
        grid=(steps,),
        in_specs=[
            by_rows(width),
            ahead(width),
            by_rows(1),
            ahead(1),
            pl.BlockSpec((1, CHUNK), lambda c: (0, steps - 1 - c)),
            whole_block(conv_weight),
            whole_block(heads_vec),
            whole_block(heads_map),
            whole_block(gain),
            by_rows(channels),
            pl.BlockSpec((1, 1, CHUNK), lambda c: (steps - 1 - c, 0, 0)),
            pl.BlockSpec((1, 1, CHUNK), lambda c: (steps - 1 - c, 0, 0)),
            by_rows(channels),
            by_rows(mixed_width),
            pl.BlockSpec((1, NS, channels), lambda c: (steps - 1 - c, 0, 0)),
        ],
        out_specs=[
            by_rows(lead),
            pl.BlockSpec((8, mixed_width), lambda c: (0, 0)),
            pl.BlockSpec((8, LANES), lambda c: (0, 0)),
            pl.BlockSpec((8, channels), lambda c: (0, 0)),
        ],
        out_shape=[
            jax.ShapeDtypeStruct((total, lin.shape[1]), BF16),
            jax.ShapeDtypeStruct((8, mixed_width), F32),
            jax.ShapeDtypeStruct((8, LANES), F32),
            jax.ShapeDtypeStruct((8, channels), F32),
        ],
        scratch_shapes=[
            pltpu.VMEM((NS, channels), F32),
            pltpu.VMEM((8, mixed_width), F32),
            pltpu.VMEM((8, 1), jnp.int32),
        ],
        compiler_params=pltpu.CompilerParams(vmem_limit_bytes=48 << 20),
        name="mixer_backward",
    )(
        lin, lin, seg_column, seg_column, seg.reshape(1, total), conv_weight, heads_vec, heads_map, gain,
        grad_normed, inverse, cross, ssm, mixed, states,
    )


ROWS = 256


def turn(values, cosine, sine):
    return values * cosine + pltpu.roll(values, HEAD_SIZE // 2, 1) * sine


def attend_weights(query, keys, seg, seg_row, start):
    stop = start + ROWS
    scores = mat_nt(query, keys[:stop]) * (1.0 / math.sqrt(HEAD_SIZE))
    allowed = (iota((ROWS, stop), 0) + start >= iota((ROWS, stop), 1)) & (
        seg[start:stop] == seg_row[:, :stop]
    )
    scores = jnp.where(allowed, scores, FAR)
    shifted = jnp.exp(scores - jnp.max(scores, 1, keepdims=True))
    return shifted * (1.0 / jnp.sum(shifted, 1, keepdims=True))


def attend_forward_kernel(head_ref, q_ref, k_ref, v_ref, seg_ref, segr_ref, cos_ref, sin_ref, out_ref):
    cosine, sine = cos_ref[...], sin_ref[...]
    seg, seg_row = seg_ref[...], segr_ref[...]
    query = turn(q_ref[...], cosine, sine).astype(BF16)
    keys = turn(k_ref[...], cosine, sine).astype(BF16)
    values = v_ref[...].astype(BF16)
    for start in range(0, SEQ_LEN, ROWS):
        weights = attend_weights(query[start : start + ROWS], keys, seg, seg_row, start)
        out_ref[start : start + ROWS, :] = mat(
            weights.astype(BF16), values[: start + ROWS]
        ).astype(BF16)


def attend_backward_kernel(
    first_block, lead, head_ref, q_ref, k_ref, v_ref, seg_ref, segr_ref, cos_ref, sin_ref, do_ref, old_ref,
    dlin_ref, dkeys, dvalues, dq_ref, dkv_ref, sem,
):
    step = pl.program_id(1)
    here = pl.ds(pl.program_id(0) * SEQ_LEN, SEQ_LEN)
    cosine, sine = cos_ref[...], sin_ref[...]
    seg, seg_row = seg_ref[...], segr_ref[...]
    scale = 1.0 / math.sqrt(HEAD_SIZE)

    @pl.when(step == 0)
    def _():
        dkeys[...] = jnp.zeros_like(dkeys)
        dvalues[...] = jnp.zeros_like(dvalues)

    query = turn(q_ref[...], cosine, sine).astype(BF16)
    keys = turn(k_ref[...], cosine, sine).astype(BF16)
    values = v_ref[...].astype(BF16)
    for start in range(0, SEQ_LEN, ROWS):
        stop = start + ROWS
        rows = slice(start, stop)
        weights = attend_weights(query[rows], keys, seg, seg_row, start)
        grad_out = do_ref[rows, :]
        dvalues[:stop] += mat_tn(weights.astype(BF16), grad_out)
        grads = mat_nt(grad_out, values[:stop])
        inner = jnp.sum(grads * weights, 1, keepdims=True)
        scores = (weights * (grads - inner)).astype(BF16)
        dq = mat(scores, keys[:stop]) * scale
        dq_ref[rows, :] = turn(dq, cosine[rows], -sine[rows]).astype(BF16)
        dkeys[:stop] += mat_tn(scores, query[rows]) * scale
    place = pl.ds(pl.multiple_of((first_block + step) * HEAD_SIZE, HEAD_SIZE), HEAD_SIZE)
    out = pltpu.make_async_copy(dq_ref, dlin_ref.at[here, place], sem)
    out.start()
    out.wait()

    @pl.when(step == pl.num_programs(1) - 1)
    def _():
        mine = head_ref[0]
        grad_keys = turn(dkeys[...], cosine, -sine)
        grad_values = dvalues[...]
        for head in range(KEY_HEADS):
            same = mine == head
            cols = slice(head * HEAD_SIZE, (head + 1) * HEAD_SIZE)
            dkv_ref[:, cols] = jnp.where(same, grad_keys, 0.0).astype(BF16)
            cols = slice((KEY_HEADS + head) * HEAD_SIZE, (KEY_HEADS + head + 1) * HEAD_SIZE)
            dkv_ref[:, cols] = jnp.where(same, grad_values, 0.0).astype(BF16)
        both = pltpu.make_async_copy(dkv_ref, dlin_ref.at[here, pl.ds(lead, dkv_ref.shape[1])], sem)
        both.start()
        both.wait()


def attend_specs(first_block, lead):
    column = lambda first: pl.BlockSpec((SEQ_LEN, HEAD_SIZE), first)
    pair_block = lead // HEAD_SIZE
    return [
        column(lambda b, h, s: (b, first_block + h)),
        column(lambda b, h, s: (b, pair_block + s[0])),
        column(lambda b, h, s: (b, pair_block + KEY_HEADS + s[0])),
        pl.BlockSpec((SEQ_LEN, 1), lambda b, h, s: (b, 0)),
        pl.BlockSpec((1, SEQ_LEN), lambda b, h, s: (0, b)),
        pl.BlockSpec((SEQ_LEN, HEAD_SIZE), lambda b, h, s: (0, 0)),
        pl.BlockSpec((SEQ_LEN, HEAD_SIZE), lambda b, h, s: (0, 0)),
    ]


def attend_forward(lin, first_block, lead, heads, key_head, seg, cosine, sine):
    total = lin.shape[0]
    return pl.pallas_call(
        attend_forward_kernel,
        grid_spec=pltpu.PrefetchScalarGridSpec(
            num_scalar_prefetch=1,
            grid=(total // SEQ_LEN, heads),
            in_specs=attend_specs(first_block, lead),
            out_specs=pl.BlockSpec((SEQ_LEN, HEAD_SIZE), lambda b, h, s: (b, h)),
        ),
        out_shape=jax.ShapeDtypeStruct((total, heads * HEAD_SIZE), BF16),
        compiler_params=pltpu.CompilerParams(vmem_limit_bytes=48 << 20),
        name="attend_forward",
    )(key_head, lin, lin, lin, seg.reshape(total, 1), seg.reshape(1, total), cosine, sine)


def attend_backward(lin, first_block, lead, heads, key_head, seg, cosine, sine, grad_out, grad_lin):
    total = lin.shape[0]
    return pl.pallas_call(
        functools.partial(attend_backward_kernel, first_block, lead),
        grid_spec=pltpu.PrefetchScalarGridSpec(
            num_scalar_prefetch=1,
            grid=(total // SEQ_LEN, heads),
            in_specs=attend_specs(first_block, lead)
            + [
                pl.BlockSpec((SEQ_LEN, HEAD_SIZE), lambda b, h, s: (b, h)),
                pl.BlockSpec(memory_space=pl.ANY),
            ],
            out_specs=pl.BlockSpec(memory_space=pl.ANY),
            scratch_shapes=[
                pltpu.VMEM((SEQ_LEN, HEAD_SIZE), F32),
                pltpu.VMEM((SEQ_LEN, HEAD_SIZE), F32),
                pltpu.VMEM((SEQ_LEN, HEAD_SIZE), BF16),
                pltpu.VMEM((SEQ_LEN, 2 * KEY_HEADS * HEAD_SIZE), BF16),
                pltpu.SemaphoreType.DMA,
            ],
        ),
        out_shape=jax.ShapeDtypeStruct(grad_lin.shape, BF16),
        input_output_aliases={9: 0},
        compiler_params=pltpu.CompilerParams(vmem_limit_bytes=48 << 20),
        name="attend_backward",
    )(key_head, lin, lin, lin, seg.reshape(total, 1), seg.reshape(1, total), cosine, sine, grad_out, grad_lin)


def rms_rows(values):
    return lax.rsqrt(jnp.mean(values * values, -1, keepdims=True) + EPS)


def rms_back(values, inverse, gain, grad):
    scaled = grad * gain
    inner = jnp.mean(scaled * values, -1, keepdims=True)
    return inverse * scaled - values * (inverse * inverse * inverse * inner)


def angle_tables():
    half = HEAD_SIZE // 2
    frequency = jnp.exp(jnp.arange(half).astype(F32) * (-2.0 * math.log(THETA) / HEAD_SIZE))
    turned = jnp.arange(SEQ_LEN).astype(F32)[:, None] * frequency[None, :]
    cosine, sine = jnp.cos(turned), jnp.sin(turned)
    return jnp.concatenate([cosine, cosine], 1), jnp.concatenate([-sine, sine], 1)


MESH = pl.DeviceIdType.MESH
LINE_CHUNKS = 4


CORE, ACROSS, ALONG, CORNER = 1, 2, 4, 6
PLANE_PARTS = 4


def partner(index, bits):
    for bit in (CORE, ACROSS, ALONG):
        if bits & bit:
            index = index + jnp.where(lax.rem(index // bit, 2) == 0, bit, -bit)
    return index


def greet(place, group, owner, plane, everyone=False):
    barrier = pltpu.get_barrier_semaphore()
    if everyone:
        for hop in range(1, group):
            pl.semaphore_signal(
                barrier, inc=1, device_id={"tensor": lax.rem(place + hop, group)}, device_id_type=MESH
            )
        count = group - 1
    else:

        @pl.when(place > 0)
        def _():
            pl.semaphore_signal(barrier, inc=1, device_id={"tensor": place - 1}, device_id_type=MESH)

        @pl.when(place < group - 1)
        def _():
            pl.semaphore_signal(barrier, inc=1, device_id={"tensor": place + 1}, device_id_type=MESH)

        count = jnp.where((place > 0) & (place < group - 1), 2, 1)
    if plane:
        for bits in (CORE, ACROSS, ALONG):
            pl.semaphore_signal(barrier, inc=1, device_id={"dp": partner(owner, bits)}, device_id_type=MESH)
        count = count + 3
    pl.semaphore_wait(barrier, count)


def plane_gather_steps(own_ref, out_ref, local_sem, send_sem, recv_sem):
    owner = lax.axis_index("dp")
    share = own_ref.shape[0]
    parts = PLANE_PARTS
    rows = share // parts
    half = parts // 2

    def copy(slot, origin, to, part, own=False):
        block = out_ref.at[pl.ds(origin * share + part * rows, rows)]
        return pltpu.make_async_remote_copy(
            own_ref.at[pl.ds(part * rows, rows)] if own else block,
            block,
            send_sem.at[slot, part],
            recv_sem.at[slot, part],
            device_id={"dp": partner(owner, to)},
            device_id_type=MESH,
        )

    keep = pltpu.make_async_copy(own_ref, out_ref.at[pl.ds(owner * share, share)], local_sem)
    first = [
        copy(slot, owner, to, part, True)
        for part in range(parts)
        for slot, to in ((1, ACROSS), (2, ALONG), (0, CORE))
    ]
    later = []

    def begin():
        keep.start()
        for item in first:
            item.start()

    def go(item):
        item.start()
        later.append(item)

    def neighbours(part):
        copy(1, owner, ACROSS, part, True).wait_recv()
        if part < half:
            go(copy(3, partner(owner, ACROSS), ALONG, part))
        go(copy(4, partner(owner, ACROSS), CORE, part))
        other = (part + half) % parts
        copy(2, owner, ALONG, other, True).wait_recv()
        if other >= half:
            go(copy(3, partner(owner, ALONG), ACROSS, other))
        go(copy(5, partner(owner, ALONG), CORE, other))

    def corner(part):
        copy(3, partner(owner, ACROSS), ALONG if part < half else ACROSS, part).wait_recv()
        go(copy(6, partner(owner, CORNER), CORE, part))

    def end():
        for part in range(parts):
            for slot in (0, 4, 5, 6):
                copy(slot, owner, CORE, part).wait_recv()
        for item in first + later:
            item.wait_send()
        keep.wait()

    return begin, neighbours, corner, end


def entry_gather_kernel(
    group, parts, own_ref, weight_ref, out_ref, full_ref, local_sem, send_sem, recv_sem, keep_sem, plane_send, plane_recv
):
    place = lax.axis_index("tensor")
    rows = own_ref.shape[0] // parts
    greet(place, group, lax.axis_index("dp"), True)

    def copy(side, source, part, own=False):
        block = out_ref.at[source, pl.ds(part * rows, rows)]
        return pltpu.make_async_remote_copy(
            own_ref.at[pl.ds(part * rows, rows)] if own else block,
            block,
            send_sem.at[side, source, part],
            recv_sem.at[side, source, part],
            device_id={"tensor": place + 1 - 2 * side},
            device_id_type=MESH,
        )

    begin, neighbours, corner, end = plane_gather_steps(weight_ref, full_ref, keep_sem, plane_send, plane_recv)
    keep = pltpu.make_async_copy(own_ref, out_ref.at[place], local_sem)
    keep.start()
    more = (place < group - 1, place > 0)
    for part in range(parts):
        for side in (0, 1):

            @pl.when(more[side])
            def _():
                copy(side, place, part, True).start()

    begin()
    plane_steps = [functools.partial(neighbours, part) for part in range(PLANE_PARTS)] + [
        functools.partial(corner, part)
        for pair in range(PLANE_PARTS // 2)
        for part in (pair, pair + PLANE_PARTS // 2)
    ]
    line_steps = (group - 1) * parts
    done = 0
    for hop in range(1, group):
        for part in range(parts):
            for side in (0, 1):
                source = place - hop if side == 0 else place + hop

                @pl.when((source >= 0) & (source < group))
                def _():
                    copy(side, source, part).wait_recv()

                    @pl.when(more[side])
                    def _():
                        copy(side, source, part).start()

            index = (hop - 1) * parts + part + 1
            while done < len(plane_steps) * index // line_steps:
                plane_steps[done]()
                done += 1

    end()
    keep.wait()
    for hop in range(group):
        for part in range(parts):
            for side in (0, 1):
                source = place - hop if side == 0 else place + hop

                @pl.when((source >= 0) & (source < group) & more[side])
                def _():
                    copy(side, source, part, hop == 0).wait_send()


def line_gather_kernel(group, parts, own_ref, out_ref, local_sem, send_sem, recv_sem):
    place = lax.axis_index("tensor")
    rows = own_ref.shape[0] // parts
    greet(place, group, None, False)

    def copy(side, source, part, own=False):
        block = out_ref.at[source, pl.ds(part * rows, rows)]
        return pltpu.make_async_remote_copy(
            own_ref.at[pl.ds(part * rows, rows)] if own else block,
            block,
            send_sem.at[side, source, part],
            recv_sem.at[side, source, part],
            device_id={"tensor": place + 1 - 2 * side},
            device_id_type=MESH,
        )

    keep = pltpu.make_async_copy(own_ref, out_ref.at[place], local_sem)
    keep.start()
    more = (place < group - 1, place > 0)
    for part in range(parts):
        for side in (0, 1):

            @pl.when(more[side])
            def _():
                copy(side, place, part, True).start()

    for hop in range(1, group):
        for part in range(parts):
            for side in (0, 1):
                source = place - hop if side == 0 else place + hop

                @pl.when((source >= 0) & (source < group))
                def _():
                    copy(side, source, part).wait_recv()

                    @pl.when(more[side])
                    def _():
                        copy(side, source, part).start()

    keep.wait()
    for hop in range(group):
        for part in range(parts):
            for side in (0, 1):
                source = place - hop if side == 0 else place + hop

                @pl.when((source >= 0) & (source < group) & more[side])
                def _():
                    copy(side, source, part, hop == 0).wait_send()


def entry_gather(own, weight, dp_size, group, collective_id):
    rows, cols = own.shape
    parts = 2
    anywhere = pl.BlockSpec(memory_space=pl.ANY)
    line_sems = pltpu.SemaphoreType.DMA((2, group, parts))
    plane_sems = pltpu.SemaphoreType.DMA((7, PLANE_PARTS))
    if dp_size != 8:
        all_rows = pl.pallas_call(
            functools.partial(line_gather_kernel, group, parts),
            in_specs=[anywhere],
            out_specs=anywhere,
            out_shape=jax.ShapeDtypeStruct((group, rows, cols), own.dtype),
            scratch_shapes=[pltpu.SemaphoreType.DMA, line_sems, line_sems],
            compiler_params=pltpu.CompilerParams(collective_id=collective_id, has_side_effects=True),
            name="line_gather",
        )(own)
        return all_rows.reshape(group * rows, cols), gather(weight, "dp", 0)
    all_rows, full = pl.pallas_call(
        functools.partial(entry_gather_kernel, group, parts),
        in_specs=[anywhere] * 2,
        out_specs=[anywhere] * 2,
        out_shape=[
            jax.ShapeDtypeStruct((group, rows, cols), own.dtype),
            jax.ShapeDtypeStruct((dp_size * weight.shape[0], weight.shape[1]), weight.dtype),
        ],
        scratch_shapes=[
            pltpu.SemaphoreType.DMA, line_sems, line_sems, pltpu.SemaphoreType.DMA, plane_sems, plane_sems,
        ],
        compiler_params=pltpu.CompilerParams(collective_id=collective_id, has_side_effects=True),
        name="entry_gather",
    )(own, weight)
    return all_rows.reshape(group * rows, cols), full


def plane_scatter_steps(piece_refs, out_ref, got, staged, near_x, near_y, last, sems):
    owner = lax.axis_index("dp")
    share, width = out_ref.shape
    parts = LINE_CHUNKS
    half = share // 2
    rows = half // parts
    targets = (0, ACROSS, CORNER, ALONG)
    core_send, core_recv, stage_sem, x_send, x_recv, y_send, y_recv, last_send, last_recv = sems

    def block(piece_ref, target, side, part):
        return piece_ref.at[pl.ds(target * share + side * half + part * rows, rows)]

    def whole_core(part):
        return pltpu.make_async_remote_copy(
            got.at[part], got.at[part], core_send.at[part], core_recv.at[part],
            device_id={"dp": partner(owner, CORE)}, device_id_type=MESH,
        )

    def to_x(part):
        return pltpu.make_async_remote_copy(
            got.at[part, 0, pl.ds(1, 2)], near_x.at[part], x_send.at[part], x_recv.at[part],
            device_id={"dp": partner(owner, ACROSS)}, device_id_type=MESH,
        )

    def to_y(part):
        return pltpu.make_async_remote_copy(
            got.at[part, 1, pl.ds(2, 2)], near_y.at[part], y_send.at[part], y_recv.at[part],
            device_id={"dp": partner(owner, ALONG)}, device_id_type=MESH,
        )

    def on_to_y(part):
        return pltpu.make_async_remote_copy(
            near_x.at[part, 1], last.at[part, 0], last_send.at[0, part], last_recv.at[0, part],
            device_id={"dp": partner(owner, ALONG)}, device_id_type=MESH,
        )

    def on_to_x(part):
        return pltpu.make_async_remote_copy(
            near_y.at[part, 0], last.at[part, 1], last_send.at[1, part], last_recv.at[1, part],
            device_id={"dp": partner(owner, ACROSS)}, device_id_type=MESH,
        )

    def begin():
        def send(part, carry):
            for side in (0, 1):
                for index, bits in enumerate(targets):
                    first = 0
                    for piece_ref in piece_refs:
                        cols = pl.ds(first, piece_ref.shape[1])
                        first += piece_ref.shape[1]
                        pltpu.make_async_remote_copy(
                            block(piece_ref, partner(owner, bits | CORE), side, part),
                            got.at[part, side, index, :, cols],
                            core_send.at[part],
                            core_recv.at[part],
                            device_id={"dp": partner(owner, CORE)},
                            device_id_type=MESH,
                        ).start()
            return carry

        lax.fori_loop(0, parts, send, 0)
        stage(0)

    def stage(part):
        for side in (0, 1):
            for index, bits in enumerate(targets):
                first = 0
                for piece_ref in piece_refs:
                    cols = pl.ds(first, piece_ref.shape[1])
                    first += piece_ref.shape[1]
                    pltpu.make_async_copy(
                        block(piece_ref, partner(owner, bits), side, part), staged.at[side, index, :, cols], stage_sem
                    ).start()

    def add_core(part):
        whole_core(part).wait_recv()
        pltpu.make_async_copy(staged, staged, stage_sem).wait()

        def add(step, carry):
            side, index = step // 4, lax.rem(step, 4)
            total = got[part, side, index].astype(F32) + staged[side, index].astype(F32)
            got[part, side, index] = total.astype(BF16)
            return carry

        lax.fori_loop(0, 8, add, 0)
        to_x(part).start()
        to_y(part).start()

        @pl.when(part + 1 < parts)
        def _():
            stage(part + 1)

    def add_near(part):
        to_x(part).wait_recv()
        near_x[part, 1] = (near_x[part, 1].astype(F32) + got[part, 0, 3].astype(F32)).astype(BF16)
        on_to_y(part).start()
        to_y(part).wait_recv()
        near_y[part, 0] = (near_y[part, 0].astype(F32) + got[part, 1, 1].astype(F32)).astype(BF16)
        on_to_x(part).start()

    def add_last(part):
        for side, near, step in ((0, near_x.at[part, 0], on_to_y), (1, near_y.at[part, 1], on_to_x)):
            step(part).wait_recv()
            total = got[part, side, 0].astype(F32) + near[...].astype(F32)
            out_ref[pl.ds(side * half + part * rows, rows), :] = total + last[part, side].astype(F32)

    def end(part):
        whole_core(part).wait_send()
        to_x(part).wait_send()
        to_y(part).wait_send()
        on_to_y(part).wait_send()
        on_to_x(part).wait_send()

    return begin, add_core, add_near, add_last, end


def plane_scatter_scratch(share, width):
    rows = share // 2 // LINE_CHUNKS
    by_part = pltpu.SemaphoreType.DMA((LINE_CHUNKS,))
    by_side = pltpu.SemaphoreType.DMA((2, LINE_CHUNKS))
    return [
        pltpu.VMEM((LINE_CHUNKS, 2, 4, rows, width), BF16),
        pltpu.VMEM((2, 4, rows, width), BF16),
        pltpu.VMEM((LINE_CHUNKS, 2, rows, width), BF16),
        pltpu.VMEM((LINE_CHUNKS, 2, rows, width), BF16),
        pltpu.VMEM((LINE_CHUNKS, 2, rows, width), BF16),
        by_part, by_part, pltpu.SemaphoreType.DMA, by_part, by_part, by_part, by_part, by_side, by_side,
    ]


def common_sum(group, place, piece_out, weight_ref, lanes_ref, common_ref, outbox, inbox, send_sem, recv_sem, ranges):
    rows, width = common_ref.shape
    first = 0
    for start, count in ranges:
        outbox[:, first : first + count] = piece_out[:, start : start + count].astype(BF16)
        first += count
    lanes = lanes_ref[...]
    lane = iota(lanes.shape, 1)
    own = jnp.sum(weight_ref[...].astype(F32) * piece_out[:, : weight_ref.shape[1]], 1, keepdims=True)
    last = piece_out[:, piece_out.shape[1] - LANES :]
    last = jnp.where(lane == LANES - 2, own * lanes, jnp.where(lane == LANES - 1, lanes, last))
    outbox[:, first:] = last.astype(BF16)
    copies = []
    for hop in range(1, group):
        peer = lax.rem(place + hop, group)
        copies.append(
            pltpu.make_async_remote_copy(
                outbox.at[pl.ds(peer * rows, rows)], inbox.at[hop - 1], send_sem.at[hop - 1], recv_sem.at[hop - 1],
                device_id={"tensor": peer}, device_id_type=MESH,
            )
        )
    for copy in copies:
        copy.start()
    total = outbox[pl.ds(place * rows, rows), :].astype(F32)
    for hop, copy in enumerate(copies):
        copy.wait_recv()
        total = total + inbox[hop].astype(F32)
    common_ref[...] = total
    for copy in copies:
        copy.wait_send()


def common_plain(group, summed, weight, lanes, ranges):
    own = jnp.sum(weight.astype(F32) * summed[:, : weight.shape[1]], 1, keepdims=True)
    lane = jnp.arange(LANES)[None]
    last = summed[:, summed.shape[1] - LANES :]
    last = jnp.where(lane == LANES - 2, own * lanes, jnp.where(lane == LANES - 1, lanes, last))
    parts = [summed[:, start : start + count] for start, count in ranges] + [last]
    return scatter(jnp.concatenate(parts, 1).astype(BF16), "tensor", 0).astype(F32)


def line_sum_kernel(
    group, spread, dot, finish, own_count, side_count, piece_count, ranges, *refs,
):
    x_ref, w_ref, refs = refs[0], refs[1], refs[2:]
    own_refs, refs = refs[:own_count], refs[own_count:]
    piece_refs, refs = refs[:piece_count], refs[piece_count:]
    if ranges:
        weight_ref, lanes_ref, refs = refs[0], refs[1], refs[2:]
    out_ref, refs = refs[0], refs[1:]
    side_refs, refs = refs[:side_count], refs[side_count:]
    if piece_count:
        piece_out, refs = refs[0], refs[1:]
    if ranges:
        common_ref, refs = refs[0], refs[1:]
    held, part, sum_send, sum_recv, out_send, out_recv = refs[:6]
    place = lax.axis_index("tensor")
    away = group - 1 - place
    chunks = LINE_CHUNKS
    rows = x_ref.shape[1] // chunks
    few = rows // 2
    model = out_ref.shape[-1]
    tile = model // group
    more = (place < group - 1, place > 0)
    ahead = (place > 0, place < group - 1)
    greet(place, group, lax.axis_index("dp"), piece_count > 0, bool(ranges))
    if piece_count:
        begin, add_core, add_near, add_last, end = plane_scatter_steps(
            piece_refs, piece_out, *refs[6:11], refs[11:20]
        )
        begin()

    def multiply(chunk, index):
        left = x_ref[:, pl.ds(chunk * rows, rows), :].reshape(group * rows, x_ref.shape[2])
        cols = pl.ds(index * tile, tile)
        part[lax.rem(chunk, 2), :, :, cols] = dot(left, w_ref, cols).reshape(group, rows, tile)

    def sum_copy(side, chunk, share, half):
        block = held.at[chunk, share + 1 - side, pl.ds(half * few, few)]
        index = 2 * chunk + half
        return pltpu.make_async_remote_copy(
            block, block, sum_send.at[side, index, share], sum_recv.at[side, index, share],
            device_id={"tensor": place + 1 - 2 * side}, device_id_type=MESH,
        )

    def out_copy(side, chunk, source, half):
        block = out_ref.at[source, pl.ds(chunk * rows + half * few, few)]
        index = 2 * chunk + half
        return pltpu.make_async_remote_copy(
            block, block, out_send.at[side, index, source], out_recv.at[side, index, source],
            device_id={"tensor": place + 1 - 2 * side}, device_id_type=MESH,
        )

    for index in range(group):
        multiply(0, index)

    def pass_out(chunk, slot, half):
        for side in (0, 1):
            source = place - (slot + 1) if side == 0 else place + (slot + 1)

            @pl.when((chunk > 0) & (source >= 0) & (source < group))
            def _():
                out_copy(side, chunk - 1, source, half).wait_recv()

                @pl.when(more[side])
                def _():
                    out_copy(side, chunk - 1, source, half).start()

    def add_on(chunk, slot, half):
        local = pl.ds(half * few, few)
        for side in (0, 1):
            depth = place if side == 0 else away
            share = group - 1 - slot + place if side == 0 else slot - away

            @pl.when((chunk < chunks) & (depth <= slot))
            def _():
                mine = part[lax.rem(chunk, 2), share, local]
                spot = share + 1 - side

                @pl.when(ahead[side])
                def _():
                    sum_copy(side, chunk, share, half).wait_recv()
                    held[chunk, spot, local] = (held[chunk, spot, local].astype(F32) + mine).astype(BF16)

                @pl.when(jnp.logical_not(ahead[side]))
                def _():
                    held[chunk, spot, local] = mine.astype(BF16)

                sum_copy(side, chunk, share, half).start()

    def complete(chunk, half):
        local = pl.ds(half * few, few)

        @pl.when(chunk < chunks)
        def _():
            total = part.at[lax.rem(chunk, 2), place, local]
            for side in (0, 1):

                @pl.when(ahead[side])
                def _():
                    sum_copy(side, chunk, place, half).wait_recv()
                    total[...] += held[chunk, place + 1 - side, local].astype(F32)

            mine = pl.ds(chunk * rows + half * few, few)
            result = finish(total[...], mine, own_refs, side_refs)
            if spread:
                out_ref[place, mine, :] = result
                for side in (0, 1):

                    @pl.when(more[side])
                    def _():
                        out_copy(side, chunk, place, half).start()
            else:
                out_ref[mine, :] = result

    def one_chunk(chunk, carry):
        for slot in range(group):
            for half in (0, 1):
                if slot + 1 < group and spread:
                    pass_out(chunk, slot, half)
                if slot < group - 1:
                    add_on(chunk, slot, half)
                else:
                    complete(chunk, half)

            @pl.when(chunk + 1 < chunks)
            def _():
                multiply(chunk + 1, slot)

            if piece_count and slot == 0:

                @pl.when(chunk < chunks)
                def _():
                    add_core(chunk)

            if piece_count and slot == group // 2:

                @pl.when(chunk < chunks)
                def _():
                    add_near(chunk)

            if piece_count and slot == 1:

                @pl.when(chunk > 0)
                def _():
                    add_last(chunk - 1)

        return carry

    lax.fori_loop(0, chunks + 1 if spread or piece_count else chunks, one_chunk, 0)
    if ranges:
        common_sum(group, place, piece_out, weight_ref, lanes_ref, common_ref, *refs[20:], ranges)

    def finish_sends(chunk, carry):
        for half in (0, 1):
            for slot in range(group):
                for side in (0, 1):
                    depth = place if side == 0 else away
                    share = group - 1 - slot + place if side == 0 else slot - away
                    if slot < group - 1:

                        @pl.when(depth <= slot)
                        def _():
                            sum_copy(side, chunk, share, half).wait_send()

                    source = place - slot if side == 0 else place + slot
                    if spread:

                        @pl.when((source >= 0) & (source < group) & more[side])
                        def _():
                            out_copy(side, chunk, source, half).wait_send()

        if piece_count:
            end(chunk)
        return carry

    lax.fori_loop(0, chunks, finish_sends, 0)


def line_sum(
    x, w, own, dot, finish, side_shapes, group, model, collective_id, name, spread=True, pieces=(), dp_size=8, common=None
):
    total = x.shape[0]
    rows = total // group
    vmem = pl.BlockSpec(memory_space=pltpu.VMEM)
    anywhere = pl.BlockSpec(memory_space=pl.ANY)
    piece_rows = rows // LINE_CHUNKS
    sems = pltpu.SemaphoreType.DMA((2, 2 * LINE_CHUNKS, group))
    out_shape = [jax.ShapeDtypeStruct((group, rows, model), BF16) if spread else jax.ShapeDtypeStruct((rows, model), F32)]
    out_shape += side_shapes
    scratch = [
        pltpu.VMEM((LINE_CHUNKS, group + 1, piece_rows, model), BF16),
        pltpu.VMEM((2, group, piece_rows, model), F32),
        sems, sems, sems, sems,
    ]
    summed, ranges, last = None, (), []
    if pieces and dp_size != 8:
        summed = [jnp.concatenate([scatter(piece, "dp", 0) for piece in pieces], 1).astype(F32)]
        if common:
            summed.append(common_plain(group, summed[0], *common))
        pieces, common = (), None
    if pieces:
        share, width = pieces[0].shape[0] // dp_size, sum(piece.shape[1] for piece in pieces)
        out_shape += [jax.ShapeDtypeStruct((share, width), F32)]
        scratch += plane_scatter_scratch(share, width)
    if common:
        ranges, last = common[2], list(common[:2])
        common_width = sum(count for _, count in ranges) + LANES
        out_shape += [jax.ShapeDtypeStruct((share // group, common_width), F32)]
        scratch += [
            pltpu.VMEM((share, common_width), BF16),
            pltpu.VMEM((group - 1, share // group, common_width), BF16),
            pltpu.SemaphoreType.DMA((group - 1,)),
            pltpu.SemaphoreType.DMA((group - 1,)),
        ]
    results = pl.pallas_call(
        functools.partial(line_sum_kernel, group, spread, dot, finish, len(own), len(side_shapes), len(pieces), ranges),
        in_specs=[vmem] * (2 + len(own)) + [anywhere] * len(pieces) + [vmem] * len(last),
        out_specs=[vmem] * len(out_shape),
        out_shape=out_shape,
        scratch_shapes=scratch,
        compiler_params=pltpu.CompilerParams(
            collective_id=collective_id, has_side_effects=True, vmem_limit_bytes=60 << 20
        ),
        name=name,
    )(x.reshape(group, rows, x.shape[1]), w, *own, *pieces, *last)
    results = list(results)
    if spread:
        results[0] = results[0].reshape(total, model)
    return results if summed is None else results + summed


def project_kernel(tokens_ref, gains_ref, w_ref, lin_ref, first_ref, gain_rows_ref):
    @pl.when(pl.program_id(0) == 0)
    def _():
        picks = (iota((8, LANES), 0) + LANES - 2 == iota((8, LANES), 1)).astype(BF16)
        gain_rows_ref[...] = mat_nt(picks, gains_ref[...])
        gain = gain_rows_ref[0:1]

        def normalise(step, carry):
            rows = pl.ds(step * CHUNK, CHUNK)
            values = tokens_ref[rows, :].astype(F32)
            first_ref[rows, :] = (values * rms_rows(values) * gain).astype(BF16)
            return carry

        lax.fori_loop(0, tokens_ref.shape[0] // CHUNK, normalise, 0)

    lin_ref[...] = mat(first_ref[...], w_ref[...])


def project(tokens, weight, gain_block):
    total, model = tokens.shape
    cols = weight.shape[1]
    tile = 512
    return pl.pallas_call(
        project_kernel,
        grid=(cols // tile,),
        in_specs=[
            whole_block(tokens),
            pl.BlockSpec((model, LANES), lambda c: (0, gain_block)),
            pl.BlockSpec((model, tile), lambda c: (0, c)),
        ],
        out_specs=[
            pl.BlockSpec((total, tile), lambda c: (0, c)),
            pl.BlockSpec((total, model), lambda c: (0, 0)),
            pl.BlockSpec((8, model), lambda c: (0, 0)),
        ],
        out_shape=[
            jax.ShapeDtypeStruct((total, cols), F32),
            jax.ShapeDtypeStruct((total, model), BF16),
            jax.ShapeDtypeStruct((8, model), F32),
        ],
        compiler_params=pltpu.CompilerParams(vmem_limit_bytes=56 << 20),
        name="project",
    )(tokens, weight, weight)


def exchange_copies(group, own_ref, slots, send_sem, recv_sem):
    place = lax.axis_index("tensor")
    return [
        pltpu.make_async_remote_copy(
            own_ref, slots.at[hop - 1], send_sem.at[hop - 1], recv_sem.at[hop - 1],
            device_id={"tensor": lax.rem(place + hop, group)}, device_id_type=MESH,
        )
        for hop in range(1, group)
    ]


def exchange_scratch(group, shape):
    return [
        pltpu.VMEM((group - 1,) + shape, F32),
        pltpu.SemaphoreType.DMA((group - 1,)),
        pltpu.SemaphoreType.DMA((group - 1,)),
    ]


def gate_norm_kernel(
    group, square_ref, ssm_ref, gate_ref, gain_ref, attended_ref, mix_ref, inverse_ref, slots, send_sem, recv_sem
):
    greet(lax.axis_index("tensor"), group, None, False, True)
    copies = exchange_copies(group, square_ref, slots, send_sem, recv_sem)
    for copy in copies:
        copy.start()
    total = square_ref[...]
    for hop, copy in enumerate(copies):
        copy.wait_recv()
        total = total + slots[hop]
    inverse_ref[...] = lax.rsqrt(total * (1.0 / DSSM) + EPS)
    query_cols = attended_ref.shape[1]
    mix_ref[:, :query_cols] = attended_ref[...]

    def norm(step, carry):
        rows = pl.ds(step * CHUNK, CHUNK)
        gate = gate_ref[rows, :]
        gated = ssm_ref[rows, :] * gate * sigmoid(gate)
        mix_ref[rows, query_cols:] = (gated * as_column(inverse_ref[step]) * gain_ref[...]).astype(BF16)
        return carry

    lax.fori_loop(0, square_ref.shape[0], norm, 0)
    for copy in copies:
        copy.wait_send()


def gate_norm(square, ssm, lin, gain, attended, group, collective_id):
    total, channels = ssm.shape
    width = attended.shape[1] + channels
    return pl.pallas_call(
        functools.partial(gate_norm_kernel, group),
        grid=(1,),
        in_specs=[
            whole_block(square),
            whole_block(ssm),
            pl.BlockSpec((total, channels), lambda c: (0, 0)),
            whole_block(gain),
            whole_block(attended),
        ],
        out_specs=[pl.BlockSpec((total, width), lambda c: (0, 0)), whole_block(square)],
        out_shape=[jax.ShapeDtypeStruct((total, width), BF16), jax.ShapeDtypeStruct(square.shape, F32)],
        scratch_shapes=exchange_scratch(group, square.shape),
        compiler_params=pltpu.CompilerParams(
            collective_id=collective_id, has_side_effects=True, vmem_limit_bytes=56 << 20
        ),
        name="gate_norm",
    )(square, ssm, lin, gain, attended)


def gate_back_kernel(
    group, query_cols, mix_ref, w_ref, ssm_ref, gate_ref, gain_ref, attended_ref, normed_ref, cross_ref,
    own, slots, send_sem, recv_sem,
):
    step = pl.program_id(0)

    @pl.when(step == 0)
    def _():
        greet(lax.axis_index("tensor"), group, None, False, True)

    grads = mat_nt(mix_ref[...], w_ref[...])
    attended_ref[...] = grads[:, :query_cols].astype(BF16)
    grads = grads[:, query_cols:]
    normed_ref[...] = grads
    gate = gate_ref[...]
    products = ssm_ref[...] * gate * sigmoid(gate) * (grads * gain_ref[...])
    total = products[:, :LANES]
    for index in range(1, products.shape[1] // LANES):
        total = total + products[:, index * LANES : (index + 1) * LANES]
    per_step = ROWS // CHUNK
    for index in range(per_step):
        own[step * per_step + index] = row_sums_as_row(total[index * CHUNK : (index + 1) * CHUNK])

    @pl.when(step == pl.num_programs(0) - 1)
    def _():
        copies = exchange_copies(group, own, slots, send_sem, recv_sem)
        for copy in copies:
            copy.start()
        result = own[...]
        for hop, copy in enumerate(copies):
            copy.wait_recv()
            result = result + slots[hop]
        cross_ref[...] = result
        for copy in copies:
            copy.wait_send()


def gate_back(mix_all, weight_mix, ssm, lin, gain, query_cols, group, collective_id):
    total, channels = ssm.shape
    model = mix_all.shape[1]
    cross = (total // CHUNK, 1, CHUNK)
    by_rows = lambda cols: pl.BlockSpec((ROWS, cols), lambda c: (c, 0))
    return pl.pallas_call(
        functools.partial(gate_back_kernel, group, query_cols),
        grid=(total // ROWS,),
        in_specs=[by_rows(model), whole_block(weight_mix), by_rows(channels), by_rows(channels), whole_block(gain)],
        out_specs=[by_rows(query_cols), by_rows(channels), pl.BlockSpec(cross, lambda c: (0, 0, 0))],
        out_shape=[
            jax.ShapeDtypeStruct((total, query_cols), BF16),
            jax.ShapeDtypeStruct((total, channels), F32),
            jax.ShapeDtypeStruct(cross, F32),
        ],
        scratch_shapes=[pltpu.VMEM(cross, F32)] + exchange_scratch(group, cross),
        compiler_params=pltpu.CompilerParams(
            collective_id=collective_id, has_side_effects=True, vmem_limit_bytes=56 << 20
        ),
        name="gate_back",
    )(mix_all, weight_mix, ssm, lin, gain)


HIDDEN_TILE = 256


def feed_forward_kernel(second_ref, cot_ref, expand_ref, shrink_ref, act_ref, hidden_ref, out_ref, total):
    step = pl.program_id(0)
    expand = expand_ref[...]
    shrink = shrink_ref[...]
    for first in range(0, second_ref.shape[0], ROWS):
        rows = slice(first, first + ROWS)
        lin = mat(second_ref[rows, :], expand)
        gate, up = lin[:, :HIDDEN_TILE], lin[:, HIDDEN_TILE:]
        sig = sigmoid(gate)
        silu = gate * sig
        act = (silu * up).astype(BF16)
        act_ref[rows, :] = act
        grad = mat_nt(cot_ref[rows, :], shrink)
        hidden_ref[rows, :HIDDEN_TILE] = (grad * up * (sig * (1.0 + gate * (1.0 - sig)))).astype(BF16)
        hidden_ref[rows, HIDDEN_TILE:] = (grad * silu).astype(BF16)
        part = mat(act, shrink)

        @pl.when(step == 0)
        def _():
            total[rows, :] = part

        @pl.when(step > 0)
        def _():
            total[rows, :] += part

    @pl.when(step == pl.num_programs(0) - 1)
    def _():
        out_ref[...] = total[...].astype(BF16)


def feed_forward(second, cot, expand, shrink):
    total, model = second.shape
    hidden = shrink.shape[0]
    return pl.pallas_call(
        feed_forward_kernel,
        grid=(hidden // HIDDEN_TILE,),
        in_specs=[
            pl.BlockSpec(memory_space=pltpu.VMEM),
            pl.BlockSpec(memory_space=pltpu.VMEM),
            pl.BlockSpec((model, 2 * HIDDEN_TILE), lambda c: (0, c)),
            pl.BlockSpec((HIDDEN_TILE, model), lambda c: (c, 0)),
        ],
        out_specs=[
            pl.BlockSpec((total, HIDDEN_TILE), lambda c: (0, c)),
            pl.BlockSpec((total, 2 * HIDDEN_TILE), lambda c: (0, c)),
            pl.BlockSpec((total, model), lambda c: (0, 0)),
        ],
        out_shape=[
            jax.ShapeDtypeStruct((total, hidden), BF16),
            jax.ShapeDtypeStruct((total, 2 * hidden), BF16),
            jax.ShapeDtypeStruct((total, model), BF16),
        ],
        scratch_shapes=[pltpu.VMEM((total, model), F32)],
        compiler_params=pltpu.CompilerParams(vmem_limit_bytes=60 << 20),
        name="feed_forward",
    )(second, cot, expand, shrink)


def mix_finish(total, mine, own_refs, side_refs):
    tokens_ref, gain_ref = own_refs
    middle = tokens_ref[mine, :].astype(F32) + total
    side_refs[0][mine, :] = middle
    return (middle * rms_rows(middle) * gain_ref[...]).astype(BF16)


def second_finish(total, mine, own_refs, side_refs):
    cot_ref, middle_ref, gain_ref = own_refs
    middle = middle_ref[mine, :]
    grad = cot_ref[mine, :].astype(F32) + rms_back(middle, rms_rows(middle), gain_ref[...], total)
    side_refs[0][mine, :] = grad
    return grad.astype(BF16)


def first_finish(total, mine, own_refs, side_refs):
    tokens_ref, middle_ref, gain_ref = own_refs
    tokens = tokens_ref[mine, :].astype(F32)
    return middle_ref[mine, :] + rms_back(tokens, rms_rows(tokens), gain_ref[...], total)


def dot_columns(left, w_ref, cols):
    return mat(left, w_ref[:, cols])


def dot_rows(left, w_ref, cols):
    return mat_nt(left, w_ref[cols, :])


def gather(array, axis_name, axis):
    return lax.all_gather(array, axis_name, axis=axis, tiled=True)


def scatter(array, axis_name, axis):
    return lax.psum_scatter(array, axis_name, scatter_dimension=axis, tiled=True)


def per_device(
    tokens_in, segment_ids, cotangent, norm_first, query_weight, key_value_weight, output_weight,
    inner_weight, state_weight, step_weight, conv_inner, conv_state, head_params, gate_gain,
    mamba_weight, norm_second, expand_weight, shrink_weight,
):
    dp_size = lax.axis_size("dp")
    group = lax.axis_size("tensor")
    place = lax.axis_index("tensor")
    total = segment_ids.shape[0]
    own_rows, model = tokens_in.shape
    share = query_weight.shape[0]
    heads = step_weight.shape[1]
    channels = heads * PM
    query_cols = query_weight.shape[1]
    query_heads = query_cols // HEAD_SIZE
    pair_cols = key_value_weight.shape[1]
    hidden = shrink_weight.shape[0]
    state_cols = 2 * channels + 2 * NS
    mixer_cols = state_cols + LANES
    lead = -(-(mixer_cols + query_cols) // pair_cols) * pair_cols

    step_block = jnp.concatenate(
        [
            step_weight,
            jnp.zeros((share, LANES - 2 - heads), BF16),
            norm_first[:, None],
            norm_second[:, None],
        ],
        1,
    )
    spare = jnp.zeros((share, lead - mixer_cols - query_cols), BF16)
    weight_own = jnp.concatenate(
        [inner_weight.reshape(share, 2 * channels), state_weight, step_block, query_weight, spare, key_value_weight], 1
    )
    weight_mix = gather(jnp.concatenate([output_weight, mamba_weight], 0), "dp", 1)
    tokens_all, weight_in = entry_gather(tokens_in, weight_own, dp_size, group, 1)
    cot_mine, tokens_all, weight_in = lax.optimization_barrier((cotangent, tokens_all, weight_in))
    cot_all = gather(cot_mine, "tensor", 0)

    cosine, sine = angle_tables()
    key_head = (place * query_heads // (QUERY_HEADS // KEY_HEADS)).astype(jnp.int32).reshape(1)
    heads_map = (jnp.arange(channels)[None, :] // PM == jnp.arange(LANES)[:, None]).astype(BF16)
    conv_weight = jnp.concatenate(
        [conv_inner.reshape(KC + 1, channels), conv_state], 1
    ).astype(F32)
    conv_weight = jnp.pad(conv_weight, ((0, 8 - KC - 1), (0, 0)))
    heads_vec = jnp.pad(head_params, ((0, 5), (0, LANES - heads)))
    gate_row = gate_gain.astype(F32).reshape(1, channels)

    lin, first, gains = project(tokens_all, weight_in, mixer_cols // LANES - 1)
    gain_one, gain_two = gains[0:1], gains[1:2]
    query_block = mixer_cols // LANES
    ssm, mixed, square, states = mixer_forward(lin, segment_ids, conv_weight, heads_vec, heads_map, heads)
    attended = attend_forward(lin, query_block, lead, query_heads, key_head, segment_ids, cosine, sine)
    expand_own = jnp.moveaxis(expand_weight.reshape(share, 2, -1, HIDDEN_TILE), 1, 2).reshape(share, 2 * hidden)
    weight_expand = gather(expand_own, "dp", 0)
    weight_shrink = gather(shrink_weight, "dp", 1)
    mix_in, inverse = gate_norm(square, ssm, lin, gate_row, attended, group, 4)
    mix_in, cot_all = lax.optimization_barrier((mix_in, cot_all))
    second_all, middle = line_sum(
        mix_in, weight_mix, [tokens_in, gain_two], dot_columns, mix_finish,
        [jax.ShapeDtypeStruct((own_rows, model), F32)], group, model, 2, "mix_sum",
    )
    act, grad_hidden, ffn_part = feed_forward(second_all, cot_all, weight_expand, weight_shrink)
    grad_expand = mat_tn(second_all, grad_hidden).astype(BF16)
    grad_shrink = mat_tn(cot_all, act).astype(BF16)
    mix_all, grad_middle, ffn_sum = line_sum(
        grad_hidden, weight_expand, [cotangent, middle, gain_two], dot_rows, second_finish,
        [jax.ShapeDtypeStruct((own_rows, model), F32)], group, model, 3, "second_sum",
        pieces=[grad_expand, grad_shrink], dp_size=dp_size,
    )
    ffn_part, mix_all = lax.optimization_barrier((ffn_part, mix_all))
    ffn_out = scatter(ffn_part, "tensor", 0)

    grad_attended, grad_normed, cross = gate_back(mix_all, weight_mix, ssm, lin, gate_row, query_cols, group, 5)
    grad_mix_weight = mat_tn(mix_all, mix_in).astype(BF16)
    grad_lin, grad_conv, grad_heads, grad_gate_gain = mixer_backward(
        lin, segment_ids, conv_weight, heads_vec, heads_map, gate_row, grad_normed, inverse, cross,
        ssm, mixed, states, heads, lead,
    )
    grad_lin = attend_backward(
        lin, query_block, lead, query_heads, key_head, segment_ids, cosine, sine, grad_attended, grad_lin
    )
    piece = PM // dp_size
    by_owner = lambda array: jnp.moveaxis(array.reshape(array.shape[0], -1, dp_size, array.shape[-1] // dp_size), 2, 0)
    small = jnp.concatenate(
        [
            by_owner(grad_conv[: KC + 1, :channels].reshape(KC + 1, heads, PM)).reshape(dp_size, -1),
            by_owner(grad_gate_gain[0].reshape(1, heads, PM)).reshape(dp_size, -1),
            jnp.broadcast_to(grad_heads[None, :3, :heads], (dp_size, 3, heads)).reshape(dp_size, -1),
            by_owner(grad_conv[: KC + 1, channels:].reshape(KC + 1, 1, 2 * NS)).reshape(dp_size, -1),
        ],
        1,
    )
    conv_cut = (KC + 1) * heads * piece
    gain_cut = conv_cut + heads * piece
    head_cut = gain_cut + 3 * heads
    state_piece = 2 * NS // (dp_size * group)
    gain_piece = share // group
    small_cols = -(-head_cut // share)
    local = jnp.pad(small[:, :head_cut], ((0, 0), (0, small_cols * share - head_cut)))
    state_count = (KC + 1) * state_piece
    state_extra = -(-state_count // gain_piece)
    common = small[:, head_cut:].reshape(dp_size, KC + 1, group, state_piece).transpose(0, 2, 1, 3)
    common = jnp.pad(
        common.reshape(dp_size, group, state_count), ((0, 0), (0, 0), (0, state_extra * gain_piece - state_count))
    )
    small = jnp.concatenate(
        [
            local.reshape(model, small_cols),
            common.reshape(model, state_extra),
            jnp.zeros((model, LANES - small_cols - state_extra), F32),
        ],
        1,
    ).astype(BF16)
    gain_two_part = jnp.sum(
        expand_own.astype(F32) * ffn_sum[:, : 2 * hidden], 1
    ) / norm_second.astype(F32)
    gain_lanes = jnp.concatenate(
        [
            jnp.zeros((share, LANES - 2), F32),
            (1.0 / norm_first.astype(F32))[:, None],
            gain_two_part[:, None],
        ],
        1,
    )
    grad_in = mat_tn(first, grad_lin).astype(BF16)
    in_cols = weight_own.shape[1]
    grad_lin, ffn_out = lax.optimization_barrier((grad_lin, ffn_out))
    block_out = (middle + ffn_out.astype(F32)).astype(BF16)
    grad_tokens, in_sum, shared_sum = line_sum(
        grad_lin, weight_in, [tokens_in, grad_middle, gain_one], dot_rows, first_finish,
        [], group, model, 6, "first_sum", spread=False, pieces=[grad_in, grad_mix_weight, small], dp_size=dp_size,
        common=(weight_own, gain_lanes, ((2 * channels, 2 * NS), (lead, pair_cols))),
    )
    extra = in_sum[:, in_cols + query_cols + channels :][:, :small_cols].reshape(-1)
    rest = shared_sum[:, 2 * NS + pair_cols :]
    conv_inner_own = extra[:conv_cut].reshape(KC + 1, heads, piece)
    gate_gain_own = extra[conv_cut:gain_cut].reshape(heads, piece)
    head_own = extra[gain_cut:head_cut].reshape(3, heads)
    conv_state_own = (
        rest[:, small_cols : small_cols + state_extra].reshape(-1)[:state_count].reshape(KC + 1, state_piece)
    )
    mix_sum = in_sum[:, in_cols : in_cols + query_cols + channels].T
    return (
        block_out,
        grad_tokens,
        rest[:, LANES - 2],
        in_sum[:, mixer_cols : mixer_cols + query_cols],
        shared_sum[:, 2 * NS : 2 * NS + pair_cols],
        mix_sum[:query_cols],
        in_sum[:, : 2 * channels].reshape(share, 2, channels),
        shared_sum[:, : 2 * NS],
        in_sum[:, state_cols : state_cols + heads],
        conv_inner_own,
        conv_state_own,
        head_own,
        gate_gain_own,
        mix_sum[query_cols:],
        rest[:, LANES - 1],
        jnp.moveaxis(ffn_sum[:, : 2 * hidden].reshape(share, -1, 2, HIDDEN_TILE), 2, 1).reshape(share, 2, hidden),
        ffn_sum[:, 2 * hidden :].T,
    )


def solution(mesh):
    return jax.shard_map(
        per_device,
        mesh=mesh,
        in_specs=(
            P(("dp", "tensor"), None),
            P("dp"),
            P(("dp", "tensor"), None),
            P("dp"),
            P("dp", "tensor"),
            P("dp", None),
            P("tensor", "dp"),
            P("dp", None, "tensor"),
            P("dp", None),
            P("dp", "tensor"),
            P(None, "tensor", None),
            P(),
            P(None, "tensor"),
            P("tensor", None),
            P("tensor", "dp"),
            P("dp"),
            P("dp", None, "tensor"),
            P("tensor", "dp"),
        ),
        out_specs=(
            P(("dp", "tensor"), None),
            P(("dp", "tensor"), None),
            P(("dp", "tensor")),
            P("dp", "tensor"),
            P(("dp", "tensor"), None),
            P("tensor", "dp"),
            P("dp", None, "tensor"),
            P(("dp", "tensor"), None),
            P("dp", "tensor"),
            P(None, "tensor", "dp"),
            P(None, ("dp", "tensor")),
            P(None, "tensor"),
            P("tensor", "dp"),
            P("tensor", "dp"),
            P(("dp", "tensor")),
            P("dp", None, "tensor"),
            P("tensor", "dp"),
        ),
        check_vma=False,
    )
```

```python
import functools
import math

import jax
import jax.numpy as jnp
from jax import lax
from jax.experimental import pallas as pl
from jax.experimental.pallas import tpu as pltpu
from jax.sharding import PartitionSpec as P

QUERY_HEADS = 8
KEY_HEADS = 2
HEAD_SIZE = 128
PM = 64
NS = 256
KC = 4
SEQ_LEN = 1024
DSSM = 3072
LANES = 128
CHUNK = 128
FAR = -1e30


EPS = 1e-05
THETA = 100000000000.0
HIGH = lax.Precision.HIGHEST
F32 = jnp.float32
BF16 = jnp.bfloat16


def mat(left_side, right_side):
    return jnp.dot(left_side, right_side, preferred_element_type=F32)


def mat_nt(left_side, right_side):
    return lax.dot_general(
        left_side, right_side, (((1,), (1,)), ((), ())), preferred_element_type=F32
    )


def mat_tn(left_side, right_side):
    return lax.dot_general(
        left_side, right_side, (((0,), (0,)), ((), ())), preferred_element_type=F32
    )


def iota(shape, dim):
    return lax.broadcasted_iota(jnp.int32, shape, dim)


def halves(value):
    high = value.astype(BF16)
    return high, (value - high.astype(F32)).astype(BF16)


def spread(value, heads_map):
    high, rest = halves(value)
    return mat(high, heads_map) + mat(rest, heads_map)


def gather_heads(value, heads_map):
    high, rest = halves(value)
    return mat_nt(high, heads_map) + mat_nt(rest, heads_map)


def sigmoid(value):
    return 0.5 + 0.5 * jnp.tanh(0.5 * value)


def softplus(value):
    return jnp.maximum(value, 0.0) + jnp.log(1.0 + jnp.exp(-jnp.abs(value)))


def conv_rows(inputs, before, seg, seg_before, weight):
    rows = inputs.shape[0]
    longer = jnp.concatenate([before, inputs], 0)
    seg_longer = jnp.concatenate([seg_before, seg], 0)
    result = weight[KC : KC + 1] + weight[KC - 1 : KC] * inputs
    moved_list = []
    for lag in range(1, KC):
        keep = seg_longer[8 - lag : 8 - lag + rows] == seg
        moved = jnp.where(keep, longer[8 - lag : 8 - lag + rows], 0.0)
        moved_list.append(moved)
        result = result + weight[KC - 1 - lag : KC - lag] * moved
    return result, moved_list


def chunk_decay(step_lin, heads_vec, heads, seg, seg_last_before):
    rows = step_lin.shape[0]
    head_lane = iota((1, LANES), 1) < heads
    shifted = step_lin + heads_vec[1:2]
    step = jnp.where(head_lane, softplus(shifted), 0.0)
    rate = jnp.exp(heads_vec[0:1])
    log_decay = -step * rate
    lower = (iota((rows, rows), 0) >= iota((rows, rows), 1)).astype(F32)
    running = jnp.dot(lower, log_decay, precision=HIGH, preferred_element_type=F32)
    last = running[rows - 1 : rows]
    seg_last = seg[rows - 1 : rows]
    into = jnp.where(seg == seg_last_before, jnp.exp(running), 0.0)
    out = jnp.where(seg == seg_last, jnp.exp(last - running), 0.0)
    across = jnp.where(seg_last == seg_last_before, jnp.exp(last), 0.0)
    return shifted, step, rate, log_decay, running, into, out, across


def two_heads(pair):
    front = iota(pair.shape, 1) < PM
    nothing = jnp.zeros_like(pair)
    return jnp.concatenate(
        [jnp.where(front, pair, nothing), jnp.where(front, nothing, pair)], 0
    )


def pair_decay(running, running_t, bias, index):
    parts = []
    for head in (2 * index, 2 * index + 1):
        gap = running[:, head : head + 1] - running_t[head : head + 1, :] + bias
        parts.append(jnp.exp(gap))
    return parts


def as_column(row):
    return jnp.broadcast_to(row, (8, row.shape[1])).T[:, 0:1]


def row_sums_as_row(values):
    return jnp.sum(values.T, 0, keepdims=True)


def chunk_bias(seg, seg_row):
    rows = seg.shape[0]
    allowed = (iota((rows, rows), 0) >= iota((rows, rows), 1)) & (seg == seg_row)
    return jnp.where(allowed, 0.0, FAR)


def mixer_forward_kernel(
    heads, lin_ref, seg_ref, segr_ref, conv_ref, hp_ref, map_ref,
    ssm_ref, mixed_ref, sums_ref, states_ref, state, tail, seg_tail,
):
    channels = heads * PM
    rows = lin_ref.shape[0]

    @pl.when(lax.rem(pl.program_id(0), SEQ_LEN // CHUNK) == 0)
    def _():
        state[...] = jnp.zeros_like(state)
        tail[...] = jnp.zeros_like(tail)
        seg_tail[...] = jnp.full_like(seg_tail, -1)

    heads_map = map_ref[...]
    seg = seg_ref[...]
    seg_before = seg_tail[...]
    inputs = lin_ref[:, channels : 2 * channels + 2 * NS]
    conv, _ = conv_rows(inputs, tail[...], seg, seg_before, conv_ref[...])
    mixed = (conv * sigmoid(conv)).astype(BF16)
    mixed_ref[...] = mixed
    tail[...] = inputs[rows - 8 :]
    seg_tail[...] = seg[rows - 8 :]

    step_lin = lin_ref[:, 2 * channels + 2 * NS :]
    _, step, _, _, running, into, out, across = chunk_decay(
        step_lin, hp_ref[...], heads, seg, seg_before[7:8]
    )
    inner = mixed[:, :channels].astype(F32)
    state_b = mixed[:, channels : channels + NS]
    state_c = mixed[:, channels + NS :]
    few = jnp.concatenate([across, hp_ref[2:3], jnp.zeros((6, LANES), F32)], 0)
    wide = spread(jnp.concatenate([step, into, out, few], 0), heads_map)
    stepped = (inner * wide[:rows]).astype(BF16)
    leaving = (stepped.astype(F32) * wide[2 * rows : 3 * rows]).astype(BF16)
    held = state[...]
    held_low = held.astype(BF16)
    states_ref[0] = held_low
    base = wide[rows : 2 * rows] * mat(state_c, held_low) + wide[3 * rows + 1 : 3 * rows + 2] * inner
    state[...] = wide[3 * rows : 3 * rows + 1] * held + mat_tn(state_b, leaving)

    gram = mat_nt(state_c, state_b)
    bias = chunk_bias(seg, segr_ref[...])
    running_t = running.T
    total = jnp.zeros((rows, LANES), F32)
    for index in range(heads // 2):
        cols = slice(index * LANES, (index + 1) * LANES)
        first, second = pair_decay(running, running_t, bias, index)
        mixing = jnp.concatenate([first * gram, second * gram], 1).astype(BF16)
        outcome = mat(mixing, two_heads(stepped[:, cols])) + base[:, cols]
        ssm_ref[:, cols] = outcome
        gate = lin_ref[:, cols]
        gated = outcome * gate * sigmoid(gate)
        total = total + gated * gated
    sums_ref[0] = row_sums_as_row(total)


def mixer_backward_kernel(
    heads, lin_ref, before_ref, seg_ref, segb_ref, segr_ref, conv_ref, hp_ref, map_ref, gain_ref,
    gn_ref, inv_ref, cross_ref, ssm_ref, mixed_ref, states_ref,
    dlin_ref, small_ref, dstate, dnext, seg_next, dconv_ref, dhp_ref, dgain_ref,
):
    channels = heads * PM
    rows = lin_ref.shape[0]
    chunks = SEQ_LEN // CHUNK
    chunk = pl.num_programs(0) - 1 - pl.program_id(0)
    place = lax.rem(chunk, chunks)

    @pl.when(pl.program_id(0) == 0)
    def _():
        dconv_ref[...] = jnp.zeros_like(dconv_ref)
        dhp_ref[...] = jnp.zeros_like(dhp_ref)
        dgain_ref[...] = jnp.zeros_like(dgain_ref)

    @pl.when(place == chunks - 1)
    def _():
        dstate[...] = jnp.zeros_like(dstate)
        dnext[...] = jnp.zeros_like(dnext)
        seg_next[...] = jnp.full_like(seg_next, -1)

    heads_map = map_ref[...]
    seg = seg_ref[...]
    seg_before = jnp.where(place == 0, -1, segb_ref[...])

    gate = lin_ref[:, :channels]
    sig = sigmoid(gate)
    silu = gate * sig
    ssm = ssm_ref[...]
    gated = ssm * silu
    grad_normed = gn_ref[...]
    inverse = as_column(inv_ref[0])
    dgain_ref[0:1] += jnp.sum(gated * inverse * grad_normed, 0, keepdims=True)
    cube = inverse * inverse * inverse * (as_column(cross_ref[0]) * (1.0 / DSSM))
    grad_gated = inverse * (grad_normed * gain_ref[...]) - gated * cube
    grad_out = grad_gated * silu
    grad_gate = grad_gated * ssm * (sig * (1.0 + gate * (1.0 - sig)))
    dlin_ref[:, :channels] = grad_gate.astype(BF16)
    grad_low = grad_out.astype(BF16)

    step_lin = lin_ref[:, 2 * channels + 2 * NS :]
    shifted, step, rate, log_decay, running, into, out, across = chunk_decay(
        step_lin, hp_ref[...], heads, seg, seg_before[7:8]
    )
    mixed = mixed_ref[...]
    inner = mixed[:, :channels].astype(F32)
    state_b = mixed[:, channels : channels + NS]
    state_c = mixed[:, channels + NS :]
    few = jnp.concatenate([across, hp_ref[2:3], jnp.zeros((6, LANES), F32)], 0)
    wide = spread(jnp.concatenate([step, into, out, few], 0), heads_map)
    step_wide = wide[:rows]
    out_wide = wide[2 * rows : 3 * rows]
    skip_wide = wide[3 * rows + 1 : 3 * rows + 2]
    stepped = (inner * step_wide).astype(BF16)
    stepped_wide = stepped.astype(F32)
    leaving = (stepped_wide * out_wide).astype(BF16)

    held = states_ref[0]
    grad_state = dstate[...]
    grad_state_low = grad_state.astype(BF16)
    grad_leaving = mat(state_b, grad_state_low)
    grad_b = mat_nt(leaving, grad_state_low)
    entering = wide[rows : 2 * rows] * grad_out
    entering_low = entering.astype(BF16)
    grad_c = mat_nt(entering_low, held)
    carried = mat(state_c, held)
    dstate[...] = wide[3 * rows : 3 * rows + 1] * grad_state + mat_tn(state_c, entering_low)
    grad_across = jnp.sum(grad_state * held.astype(F32), 0, keepdims=True)

    gram = mat_nt(state_c, state_b)
    bias = chunk_bias(seg, segr_ref[...])
    running_t = running.T
    head_lane = iota((1, LANES), 1)
    head_row = iota((LANES, 1), 0)
    grad_gram = jnp.zeros((rows, rows), F32)
    row_sums = jnp.zeros((rows, LANES), F32)
    column_sums = jnp.zeros((LANES, rows), F32)
    grad_stepped = []
    for index in range(heads // 2):
        cols = slice(index * LANES, (index + 1) * LANES)
        grads = mat_nt(grad_low[:, cols], two_heads(stepped[:, cols]))
        mixings = []
        for side, decay in enumerate(pair_decay(running, running_t, bias, index)):
            part = grads[:, side * rows : (side + 1) * rows] * decay
            grad_gram = grad_gram + part
            part = part * gram
            head = 2 * index + side
            row_sums = jnp.where(head_lane == head, jnp.sum(part, 1, keepdims=True), row_sums)
            column_sums = jnp.where(head_row == head, jnp.sum(part, 0, keepdims=True), column_sums)
            mixings.append((decay * gram).astype(BF16))
        both = mat_tn(jnp.concatenate(mixings, 1), grad_low[:, cols])
        front = iota((rows, LANES), 1) < PM
        grad_stepped.append(jnp.where(front, both[:rows], both[rows:]))
    grad_gram_low = grad_gram.astype(BF16)
    grad_c = grad_c + mat(grad_gram_low, state_b)
    grad_b = grad_b + mat_tn(grad_gram_low, state_c)
    grad_stepped = jnp.concatenate(grad_stepped, 1) + out_wide * grad_leaving
    grad_inner = grad_stepped * step_wide + skip_wide * grad_out

    few = jnp.concatenate([grad_across, jnp.zeros((7, channels), F32)], 0)
    sums = gather_heads(
        jnp.concatenate(
            [stepped_wide * grad_leaving, entering * carried, grad_stepped * inner, grad_out * inner, few], 0
        ),
        heads_map,
    )
    leave = sums[:rows] * out
    grad_running = row_sums - column_sums.T + sums[rows : 2 * rows] - leave
    grad_last = jnp.sum(leave, 0, keepdims=True) + sums[4 * rows : 4 * rows + 1] * across
    grad_running = grad_running + jnp.where(iota((rows, 1), 0) == rows - 1, grad_last, 0.0)
    upper = (iota((rows, rows), 0) <= iota((rows, rows), 1)).astype(F32)
    grad_log = jnp.dot(upper, grad_running, precision=HIGH, preferred_element_type=F32)
    grad_step = sums[2 * rows : 3 * rows] - grad_log * rate
    grad_shifted = jnp.where(head_lane < heads, grad_step * sigmoid(shifted), 0.0)
    first_spare = 2 * channels + 2 * NS + LANES
    dlin_ref[:, first_spare - LANES : first_spare] = grad_shifted.astype(BF16)
    dlin_ref[:, first_spare:] = jnp.zeros((rows, dlin_ref.shape[1] - first_spare), BF16)
    dhp_ref[0:1] += jnp.sum(grad_log * log_decay, 0, keepdims=True)
    dhp_ref[1:2] += jnp.sum(grad_shifted, 0, keepdims=True)
    dhp_ref[2:3] += jnp.sum(sums[3 * rows : 4 * rows], 0, keepdims=True)

    grad_mixed = jnp.concatenate([grad_inner, grad_b, grad_c], 1)
    weight = conv_ref[...]
    inputs = lin_ref[:, channels : 2 * channels + 2 * NS]
    before = before_ref[:, channels : 2 * channels + 2 * NS]
    conv, moved_list = conv_rows(inputs, before, seg, seg_before, weight)
    sig = sigmoid(conv)
    grad_conv = grad_mixed * (sig * (1.0 + conv * (1.0 - sig)))
    dconv_ref[KC : KC + 1] += jnp.sum(grad_conv, 0, keepdims=True)
    dconv_ref[KC - 1 : KC] += jnp.sum(grad_conv * inputs, 0, keepdims=True)
    longer = jnp.concatenate([grad_conv, dnext[...]], 0)
    seg_longer = jnp.concatenate([seg, seg_next[...]], 0)
    grad_inputs = weight[KC - 1 : KC] * grad_conv
    for lag in range(1, KC):
        tap = slice(KC - 1 - lag, KC - lag)
        dconv_ref[tap] += jnp.sum(grad_conv * moved_list[lag - 1], 0, keepdims=True)
        keep = seg_longer[lag : lag + rows] == seg
        grad_inputs = grad_inputs + weight[tap] * jnp.where(keep, longer[lag : lag + rows], 0.0)
    dlin_ref[:, channels : 2 * channels + 2 * NS] = grad_inputs.astype(BF16)
    dnext[...] = grad_conv[:8]
    seg_next[...] = seg[:8]

    @pl.when(pl.program_id(0) == pl.num_programs(0) - 1)
    def _():
        small_ref[...] = jnp.zeros_like(small_ref)
        row = 0
        for array in (dconv_ref, dhp_ref, dgain_ref):
            for first in range(0, array.shape[1], LANES):
                small_ref[row : row + 8, :] = array[:, first : first + LANES]
                row += 8


def whole_block(array):
    return pl.BlockSpec(array.shape, lambda *_: (0,) * array.ndim)


def mixer_forward(lin, seg, conv_weight, heads_vec, heads_map, heads):
    total = lin.shape[0]
    channels = heads * PM
    width = 2 * channels + 2 * NS + LANES
    mixed_width = channels + 2 * NS
    steps = total // CHUNK
    by_rows = lambda cols: pl.BlockSpec((CHUNK, cols), lambda c: (c, 0))
    return pl.pallas_call(
        functools.partial(mixer_forward_kernel, heads),
        grid=(steps,),
        in_specs=[
            by_rows(width),
            by_rows(1),
            pl.BlockSpec((1, CHUNK), lambda c: (0, c)),
            whole_block(conv_weight),
            whole_block(heads_vec),
            whole_block(heads_map),
        ],
        out_specs=[
            by_rows(channels),
            by_rows(mixed_width),
            pl.BlockSpec((1, 1, CHUNK), lambda c: (c, 0, 0)),
            pl.BlockSpec((1, NS, channels), lambda c: (c, 0, 0)),
        ],
        out_shape=[
            jax.ShapeDtypeStruct((total, channels), F32),
            jax.ShapeDtypeStruct((total, mixed_width), BF16),
            jax.ShapeDtypeStruct((steps, 1, CHUNK), F32),
            jax.ShapeDtypeStruct((steps, NS, channels), BF16),
        ],
        scratch_shapes=[
            pltpu.VMEM((NS, channels), F32),
            pltpu.VMEM((8, mixed_width), F32),
            pltpu.VMEM((8, 1), jnp.int32),
        ],
        compiler_params=pltpu.CompilerParams(vmem_limit_bytes=48 << 20),
        name="mixer_forward",
    )(lin, seg.reshape(total, 1), seg.reshape(1, total), conv_weight, heads_vec, heads_map)


def mixer_backward(
    lin, seg, conv_weight, heads_vec, heads_map, gain, grad_normed, inverse, cross, ssm, mixed, states, heads, lead, share
):
    total = lin.shape[0]
    channels = heads * PM
    width = 2 * channels + 2 * NS + LANES
    mixed_width = channels + 2 * NS
    steps = total // CHUNK
    by_rows = lambda cols: pl.BlockSpec((CHUNK, cols), lambda c: (steps - 1 - c, 0))
    ahead = lambda cols: pl.BlockSpec(
        (8, cols), lambda c: (jnp.maximum((steps - 1 - c) * (CHUNK // 8) - 1, 0), 0)
    )
    seg_column = seg.reshape(total, 1)
    return pl.pallas_call(
        functools.partial(mixer_backward_kernel, heads),
        grid=(steps,),
        in_specs=[
            by_rows(width),
            ahead(width),
            by_rows(1),
            ahead(1),
            pl.BlockSpec((1, CHUNK), lambda c: (0, steps - 1 - c)),
            whole_block(conv_weight),
            whole_block(heads_vec),
            whole_block(heads_map),
            whole_block(gain),
            by_rows(channels),
            pl.BlockSpec((1, 1, CHUNK), lambda c: (steps - 1 - c, 0, 0)),
            pl.BlockSpec((1, 1, CHUNK), lambda c: (steps - 1 - c, 0, 0)),
            by_rows(channels),
            by_rows(mixed_width),
            pl.BlockSpec((1, NS, channels), lambda c: (steps - 1 - c, 0, 0)),
        ],
        out_specs=[
            by_rows(lead),
            pl.BlockSpec((share, LANES), lambda c: (0, 0)),
        ],
        out_shape=[
            jax.ShapeDtypeStruct((total, lin.shape[1]), BF16),
            jax.ShapeDtypeStruct((share, LANES), F32),
        ],
        scratch_shapes=[
            pltpu.VMEM((NS, channels), F32),
            pltpu.VMEM((8, mixed_width), F32),
            pltpu.VMEM((8, 1), jnp.int32),
            pltpu.VMEM((8, mixed_width), F32),
            pltpu.VMEM((8, LANES), F32),
            pltpu.VMEM((8, channels), F32),
        ],
        compiler_params=pltpu.CompilerParams(vmem_limit_bytes=48 << 20),
        name="mixer_backward",
    )(
        lin, lin, seg_column, seg_column, seg.reshape(1, total), conv_weight, heads_vec, heads_map, gain,
        grad_normed, inverse, cross, ssm, mixed, states,
    )


ROWS = 256


def turn(values, cosine, sine):
    return values * cosine + pltpu.roll(values, HEAD_SIZE // 2, 1) * sine


def attend_weights(query, keys, seg, seg_row, start):
    stop = start + ROWS
    scores = mat_nt(query, keys[:stop]) * (1.0 / math.sqrt(HEAD_SIZE))
    allowed = (iota((ROWS, stop), 0) + start >= iota((ROWS, stop), 1)) & (
        seg[start:stop] == seg_row[:, :stop]
    )
    scores = jnp.where(allowed, scores, FAR)
    shifted = jnp.exp(scores - jnp.max(scores, 1, keepdims=True))
    return shifted * (1.0 / jnp.sum(shifted, 1, keepdims=True))


def attend_forward_kernel(head_ref, q_ref, k_ref, v_ref, seg_ref, segr_ref, cos_ref, sin_ref, out_ref):
    cosine, sine = cos_ref[...], sin_ref[...]
    seg, seg_row = seg_ref[...], segr_ref[...]
    query = turn(q_ref[...], cosine, sine).astype(BF16)
    keys = turn(k_ref[...], cosine, sine).astype(BF16)
    values = v_ref[...].astype(BF16)
    for start in range(0, SEQ_LEN, ROWS):
        weights = attend_weights(query[start : start + ROWS], keys, seg, seg_row, start)
        out_ref[start : start + ROWS, :] = mat(
            weights.astype(BF16), values[: start + ROWS]
        ).astype(BF16)


def attend_backward_kernel(
    first_block, lead, head_ref, q_ref, k_ref, v_ref, seg_ref, segr_ref, cos_ref, sin_ref, do_ref, old_ref,
    dlin_ref, dkeys, dvalues, dq_ref, dkv_ref, sem,
):
    step = pl.program_id(1)
    here = pl.ds(pl.program_id(0) * SEQ_LEN, SEQ_LEN)
    cosine, sine = cos_ref[...], sin_ref[...]
    seg, seg_row = seg_ref[...], segr_ref[...]
    scale = 1.0 / math.sqrt(HEAD_SIZE)

    @pl.when(step == 0)
    def _():
        dkeys[...] = jnp.zeros_like(dkeys)
        dvalues[...] = jnp.zeros_like(dvalues)

    query = turn(q_ref[...], cosine, sine).astype(BF16)
    keys = turn(k_ref[...], cosine, sine).astype(BF16)
    values = v_ref[...].astype(BF16)
    for start in range(0, SEQ_LEN, ROWS):
        stop = start + ROWS
        rows = slice(start, stop)
        weights = attend_weights(query[rows], keys, seg, seg_row, start)
        grad_out = do_ref[rows, :]
        dvalues[:stop] += mat_tn(weights.astype(BF16), grad_out)
        grads = mat_nt(grad_out, values[:stop])
        inner = jnp.sum(grads * weights, 1, keepdims=True)
        scores = (weights * (grads - inner)).astype(BF16)
        dq = mat(scores, keys[:stop]) * scale
        dq_ref[rows, :] = turn(dq, cosine[rows], -sine[rows]).astype(BF16)
        dkeys[:stop] += mat_tn(scores, query[rows]) * scale
    place = pl.ds(pl.multiple_of((first_block + step) * HEAD_SIZE, HEAD_SIZE), HEAD_SIZE)
    out = pltpu.make_async_copy(dq_ref, dlin_ref.at[here, place], sem)
    out.start()
    out.wait()

    @pl.when(step == pl.num_programs(1) - 1)
    def _():
        mine = head_ref[0]
        grad_keys = turn(dkeys[...], cosine, -sine)
        grad_values = dvalues[...]
        for head in range(KEY_HEADS):
            same = mine == head
            cols = slice(head * HEAD_SIZE, (head + 1) * HEAD_SIZE)
            dkv_ref[:, cols] = jnp.where(same, grad_keys, 0.0).astype(BF16)
            cols = slice((KEY_HEADS + head) * HEAD_SIZE, (KEY_HEADS + head + 1) * HEAD_SIZE)
            dkv_ref[:, cols] = jnp.where(same, grad_values, 0.0).astype(BF16)
        both = pltpu.make_async_copy(dkv_ref, dlin_ref.at[here, pl.ds(lead, dkv_ref.shape[1])], sem)
        both.start()
        both.wait()


def attend_specs(first_block, lead):
    column = lambda first: pl.BlockSpec((SEQ_LEN, HEAD_SIZE), first)
    pair_block = lead // HEAD_SIZE
    return [
        column(lambda b, h, s: (b, first_block + h)),
        column(lambda b, h, s: (b, pair_block + s[0])),
        column(lambda b, h, s: (b, pair_block + KEY_HEADS + s[0])),
        pl.BlockSpec((SEQ_LEN, 1), lambda b, h, s: (b, 0)),
        pl.BlockSpec((1, SEQ_LEN), lambda b, h, s: (0, b)),
        pl.BlockSpec((SEQ_LEN, HEAD_SIZE), lambda b, h, s: (0, 0)),
        pl.BlockSpec((SEQ_LEN, HEAD_SIZE), lambda b, h, s: (0, 0)),
    ]


def attend_forward(lin, first_block, lead, heads, key_head, seg, cosine, sine):
    total = lin.shape[0]
    return pl.pallas_call(
        attend_forward_kernel,
        grid_spec=pltpu.PrefetchScalarGridSpec(
            num_scalar_prefetch=1,
            grid=(total // SEQ_LEN, heads),
            in_specs=attend_specs(first_block, lead),
            out_specs=pl.BlockSpec((SEQ_LEN, HEAD_SIZE), lambda b, h, s: (b, h)),
        ),
        out_shape=jax.ShapeDtypeStruct((total, heads * HEAD_SIZE), BF16),
        compiler_params=pltpu.CompilerParams(vmem_limit_bytes=48 << 20),
        name="attend_forward",
    )(key_head, lin, lin, lin, seg.reshape(total, 1), seg.reshape(1, total), cosine, sine)


def attend_backward(lin, first_block, lead, heads, key_head, seg, cosine, sine, grad_out, grad_lin):
    total = lin.shape[0]
    return pl.pallas_call(
        functools.partial(attend_backward_kernel, first_block, lead),
        grid_spec=pltpu.PrefetchScalarGridSpec(
            num_scalar_prefetch=1,
            grid=(total // SEQ_LEN, heads),
            in_specs=attend_specs(first_block, lead)
            + [
                pl.BlockSpec((SEQ_LEN, HEAD_SIZE), lambda b, h, s: (b, h)),
                pl.BlockSpec(memory_space=pl.ANY),
            ],
            out_specs=pl.BlockSpec(memory_space=pl.ANY),
            scratch_shapes=[
                pltpu.VMEM((SEQ_LEN, HEAD_SIZE), F32),
                pltpu.VMEM((SEQ_LEN, HEAD_SIZE), F32),
                pltpu.VMEM((SEQ_LEN, HEAD_SIZE), BF16),
                pltpu.VMEM((SEQ_LEN, 2 * KEY_HEADS * HEAD_SIZE), BF16),
                pltpu.SemaphoreType.DMA,
            ],
        ),
        out_shape=jax.ShapeDtypeStruct(grad_lin.shape, BF16),
        input_output_aliases={9: 0},
        compiler_params=pltpu.CompilerParams(vmem_limit_bytes=48 << 20),
        name="attend_backward",
    )(key_head, lin, lin, lin, seg.reshape(total, 1), seg.reshape(1, total), cosine, sine, grad_out, grad_lin)


def rms_rows(values):
    return lax.rsqrt(jnp.mean(values * values, -1, keepdims=True) + EPS)


def rms_back(values, inverse, gain, grad):
    scaled = grad * gain
    inner = jnp.mean(scaled * values, -1, keepdims=True)
    return inverse * scaled - values * (inverse * inverse * inverse * inner)


def angle_tables():
    half = HEAD_SIZE // 2
    frequency = jnp.exp(jnp.arange(half).astype(F32) * (-2.0 * math.log(THETA) / HEAD_SIZE))
    turned = jnp.arange(SEQ_LEN).astype(F32)[:, None] * frequency[None, :]
    cosine, sine = jnp.cos(turned), jnp.sin(turned)
    return jnp.concatenate([cosine, cosine], 1), jnp.concatenate([-sine, sine], 1)


MESH = pl.DeviceIdType.MESH
LINE_CHUNKS = 4


CORE, ACROSS, ALONG, CORNER = 1, 2, 4, 6
PLANE_PARTS = 4


def partner(index, bits):
    for bit in (CORE, ACROSS, ALONG):
        if bits & bit:
            index = index + jnp.where(lax.rem(index // bit, 2) == 0, bit, -bit)
    return index


def greet(place, group, owner, plane, everyone=False):
    barrier = pltpu.get_barrier_semaphore()
    if everyone:
        for hop in range(1, group):
            pl.semaphore_signal(
                barrier, inc=1, device_id={"tensor": lax.rem(place + hop, group)}, device_id_type=MESH
            )
        count = group - 1
    else:

        @pl.when(place > 0)
        def _():
            pl.semaphore_signal(barrier, inc=1, device_id={"tensor": place - 1}, device_id_type=MESH)

        @pl.when(place < group - 1)
        def _():
            pl.semaphore_signal(barrier, inc=1, device_id={"tensor": place + 1}, device_id_type=MESH)

        count = jnp.where((place > 0) & (place < group - 1), 2, 1)
    if plane:
        for bits in (CORE, ACROSS, ALONG):
            pl.semaphore_signal(barrier, inc=1, device_id={"dp": partner(owner, bits)}, device_id_type=MESH)
        count = count + 3
    pl.semaphore_wait(barrier, count)


def plane_gather_steps(pieces, local_sem, send_sem, recv_sem):
    owner = lax.axis_index("dp")
    parts = PLANE_PARTS
    half = parts // 2

    def copies(slot, origin, to, part, own=False):
        result = []
        for index, (own_ref, full_ref, by_rows) in enumerate(pieces):
            share, cols = own_ref.shape
            rows = share // parts
            if by_rows:
                block = full_ref.at[pl.ds(origin * share + part * rows, rows)]
            else:
                block = full_ref.at[pl.ds(part * rows, rows), pl.ds(pl.multiple_of(origin * cols, cols), cols)]
            result.append(
                pltpu.make_async_remote_copy(
                    own_ref.at[pl.ds(part * rows, rows)] if own else block,
                    block,
                    send_sem.at[index, slot, part],
                    recv_sem.at[index, slot, part],
                    device_id={"dp": partner(owner, to)},
                    device_id_type=MESH,
                )
            )
        return result

    def start(*args):
        for item in copies(*args):
            item.start()

    def arrive(*args):
        for item in copies(*args):
            item.wait_recv()

    def keeps():
        result = []
        for index, (own_ref, full_ref, by_rows) in enumerate(pieces):
            share, cols = own_ref.shape
            if by_rows:
                block = full_ref.at[pl.ds(owner * share, share)]
            else:
                block = full_ref.at[:, pl.ds(pl.multiple_of(owner * cols, cols), cols)]
            result.append(pltpu.make_async_copy(own_ref, block, local_sem.at[index]))
        return result

    def begin():
        for part in range(parts):
            start(1, owner, ACROSS, part, True)
            start(2, owner, ALONG, (part + half) % parts, True)
            start(0, owner, CORE, part, True)
        for item in keeps():
            item.start()

    def neighbours(part):
        arrive(1, owner, ACROSS, part, True)

        @pl.when(part < half)
        def _():
            start(3, partner(owner, ACROSS), ALONG, part)

        start(4, partner(owner, ACROSS), CORE, part)
        other = (part + half) % parts
        arrive(2, owner, ALONG, other, True)

        @pl.when(part < half)
        def _():
            start(3, partner(owner, ALONG), ACROSS, other)

        start(5, partner(owner, ALONG), CORE, other)

    def corner(step):
        for part in (step, step + half):
            arrive(3, partner(owner, CORNER), ALONG, part)
            start(6, partner(owner, CORNER), CORE, part)

    def end():
        for part in range(parts):
            for slot in (0, 4, 5, 6):
                arrive(slot, owner, CORE, part)
            for slot in range(7):
                for item in copies(slot, owner, CORE, part):
                    item.wait_send()
        for item in keeps():
            item.wait()

    return begin, neighbours, corner, end


def plane_gather_scratch(count):
    return [
        pltpu.SemaphoreType.DMA((count,)),
        pltpu.SemaphoreType.DMA((count, 7, PLANE_PARTS)),
        pltpu.SemaphoreType.DMA((count, 7, PLANE_PARTS)),
    ]


def plane_gather_plain(array, by_rows):
    return gather(array, "dp", 0 if by_rows else 1)


def entry_gather_kernel(
    group, parts, own_ref, weight_ref, out_ref, full_ref,
    local_sem, send_sem, recv_sem, keep_sem, plane_send, plane_recv,
):
    place = lax.axis_index("tensor")
    rows = own_ref.shape[0] // parts
    greet(place, group, lax.axis_index("dp"), True)

    def copy(side, source, part, own=False):
        block = out_ref.at[source, pl.ds(part * rows, rows)]
        return pltpu.make_async_remote_copy(
            own_ref.at[pl.ds(part * rows, rows)] if own else block,
            block,
            send_sem.at[side, source, part],
            recv_sem.at[side, source, part],
            device_id={"tensor": place + 1 - 2 * side},
            device_id_type=MESH,
        )

    begin, neighbours, corner, end = plane_gather_steps(
        [(weight_ref, full_ref, True)], keep_sem, plane_send, plane_recv
    )
    more = (place < group - 1, place > 0)
    for part in range(parts):
        for side in (0, 1):

            @pl.when(more[side])
            def _():
                copy(side, place, part, True).start()

    begin()
    keep = pltpu.make_async_copy(own_ref, out_ref.at[place], local_sem)
    keep.start()
    plane_steps = [functools.partial(neighbours, part) for part in range(PLANE_PARTS)] + [
        functools.partial(corner, step) for step in range(PLANE_PARTS // 2)
    ]
    line_steps = (group - 1) * parts
    done = 0
    for hop in range(1, group):
        for part in range(parts):
            for side in (0, 1):
                source = place - hop if side == 0 else place + hop

                @pl.when((source >= 0) & (source < group))
                def _():
                    copy(side, source, part).wait_recv()

                    @pl.when(more[side])
                    def _():
                        copy(side, source, part).start()

            index = (hop - 1) * parts + part + 1
            while done < len(plane_steps) * index // line_steps:
                plane_steps[done]()
                done += 1

    end()
    keep.wait()
    for hop in range(group):
        for part in range(parts):
            for side in (0, 1):
                source = place - hop if side == 0 else place + hop

                @pl.when((source >= 0) & (source < group) & more[side])
                def _():
                    copy(side, source, part, hop == 0).wait_send()


def line_gather_kernel(group, parts, own_ref, out_ref, local_sem, send_sem, recv_sem):
    place = lax.axis_index("tensor")
    rows = own_ref.shape[0] // parts
    greet(place, group, None, False)

    def copy(side, source, part, own=False):
        block = out_ref.at[source, pl.ds(part * rows, rows)]
        return pltpu.make_async_remote_copy(
            own_ref.at[pl.ds(part * rows, rows)] if own else block,
            block,
            send_sem.at[side, source, part],
            recv_sem.at[side, source, part],
            device_id={"tensor": place + 1 - 2 * side},
            device_id_type=MESH,
        )

    keep = pltpu.make_async_copy(own_ref, out_ref.at[place], local_sem)
    keep.start()
    more = (place < group - 1, place > 0)
    for part in range(parts):
        for side in (0, 1):

            @pl.when(more[side])
            def _():
                copy(side, place, part, True).start()

    for hop in range(1, group):
        for part in range(parts):
            for side in (0, 1):
                source = place - hop if side == 0 else place + hop

                @pl.when((source >= 0) & (source < group))
                def _():
                    copy(side, source, part).wait_recv()

                    @pl.when(more[side])
                    def _():
                        copy(side, source, part).start()

    keep.wait()
    for hop in range(group):
        for part in range(parts):
            for side in (0, 1):
                source = place - hop if side == 0 else place + hop

                @pl.when((source >= 0) & (source < group) & more[side])
                def _():
                    copy(side, source, part, hop == 0).wait_send()


def entry_gather(own, weight, dp_size, group, collective_id):
    rows, cols = own.shape
    parts = 2
    anywhere = pl.BlockSpec(memory_space=pl.ANY)
    line_sems = pltpu.SemaphoreType.DMA((2, group, parts))
    if dp_size != 8:
        all_rows = pl.pallas_call(
            functools.partial(line_gather_kernel, group, parts),
            in_specs=[anywhere],
            out_specs=anywhere,
            out_shape=jax.ShapeDtypeStruct((group, rows, cols), own.dtype),
            scratch_shapes=[pltpu.SemaphoreType.DMA, line_sems, line_sems],
            compiler_params=pltpu.CompilerParams(collective_id=collective_id, has_side_effects=True),
            name="line_gather",
        )(own)
        return all_rows.reshape(group * rows, cols), plane_gather_plain(weight, True)
    all_rows, full = pl.pallas_call(
        functools.partial(entry_gather_kernel, group, parts),
        in_specs=[anywhere] * 2,
        out_specs=[anywhere] * 2,
        out_shape=[
            jax.ShapeDtypeStruct((group, rows, cols), own.dtype),
            jax.ShapeDtypeStruct((dp_size * weight.shape[0], weight.shape[1]), BF16),
        ],
        scratch_shapes=[pltpu.SemaphoreType.DMA, line_sems, line_sems] + plane_gather_scratch(1),
        compiler_params=pltpu.CompilerParams(collective_id=collective_id, has_side_effects=True),
        name="entry_gather",
    )(own, weight)
    return all_rows.reshape(group * rows, cols), full


def plane_scatter_steps(piece_refs, out_ref, got, staged, near_x, near_y, last, sems):
    owner = lax.axis_index("dp")
    share, width = out_ref.shape
    parts = LINE_CHUNKS
    half = share // 2
    rows = half // parts
    targets = (0, ACROSS, CORNER, ALONG)
    core_send, core_recv, stage_sem, x_send, x_recv, y_send, y_recv, last_send, last_recv = sems

    def block(piece_ref, target, side, part):
        first = 0 if piece_ref.shape[0] == share else target * share
        return piece_ref.at[pl.ds(first + side * half + part * rows, rows)]

    def whole_core(part):
        return pltpu.make_async_remote_copy(
            got.at[part], got.at[part], core_send.at[part], core_recv.at[part],
            device_id={"dp": partner(owner, CORE)}, device_id_type=MESH,
        )

    def to_x(part):
        return pltpu.make_async_remote_copy(
            got.at[part, 0, pl.ds(1, 2)], near_x.at[part], x_send.at[part], x_recv.at[part],
            device_id={"dp": partner(owner, ACROSS)}, device_id_type=MESH,
        )

    def to_y(part):
        return pltpu.make_async_remote_copy(
            got.at[part, 1, pl.ds(2, 2)], near_y.at[part], y_send.at[part], y_recv.at[part],
            device_id={"dp": partner(owner, ALONG)}, device_id_type=MESH,
        )

    def on_to_y(part):
        return pltpu.make_async_remote_copy(
            near_x.at[part, 1], last.at[part, 0], last_send.at[0, part], last_recv.at[0, part],
            device_id={"dp": partner(owner, ALONG)}, device_id_type=MESH,
        )

    def on_to_x(part):
        return pltpu.make_async_remote_copy(
            near_y.at[part, 0], last.at[part, 1], last_send.at[1, part], last_recv.at[1, part],
            device_id={"dp": partner(owner, ACROSS)}, device_id_type=MESH,
        )

    def begin():
        def send(part, carry):
            for side in (0, 1):
                for index, bits in enumerate(targets):
                    first = 0
                    for piece_ref in piece_refs:
                        cols = pl.ds(first, piece_ref.shape[1])
                        first += piece_ref.shape[1]
                        pltpu.make_async_remote_copy(
                            block(piece_ref, partner(owner, bits | CORE), side, part),
                            got.at[part, side, index, :, cols],
                            core_send.at[part],
                            core_recv.at[part],
                            device_id={"dp": partner(owner, CORE)},
                            device_id_type=MESH,
                        ).start()
            return carry

        lax.fori_loop(0, parts, send, 0)
        stage(0)

    def stage(part):
        for side in (0, 1):
            for index, bits in enumerate(targets):
                first = 0
                for piece_ref in piece_refs:
                    cols = pl.ds(first, piece_ref.shape[1])
                    first += piece_ref.shape[1]
                    pltpu.make_async_copy(
                        block(piece_ref, partner(owner, bits), side, part), staged.at[side, index, :, cols], stage_sem
                    ).start()

    def add_core(part):
        whole_core(part).wait_recv()
        pltpu.make_async_copy(staged, staged, stage_sem).wait()

        def add(step, carry):
            side, index = step // 4, lax.rem(step, 4)
            total = got[part, side, index].astype(F32) + staged[side, index].astype(F32)
            got[part, side, index] = total.astype(BF16)
            return carry

        lax.fori_loop(0, 8, add, 0)
        to_x(part).start()
        to_y(part).start()

        @pl.when(part + 1 < parts)
        def _():
            stage(part + 1)

    def add_near(part):
        to_x(part).wait_recv()
        near_x[part, 1] = (near_x[part, 1].astype(F32) + got[part, 0, 3].astype(F32)).astype(BF16)
        on_to_y(part).start()
        to_y(part).wait_recv()
        near_y[part, 0] = (near_y[part, 0].astype(F32) + got[part, 1, 1].astype(F32)).astype(BF16)
        on_to_x(part).start()

    def add_last(part):
        for side, near, step in ((0, near_x.at[part, 0], on_to_y), (1, near_y.at[part, 1], on_to_x)):
            step(part).wait_recv()
            total = got[part, side, 0].astype(F32) + near[...].astype(F32)
            out_ref[pl.ds(side * half + part * rows, rows), :] = total + last[part, side].astype(F32)

    def end(part):
        whole_core(part).wait_send()
        to_x(part).wait_send()
        to_y(part).wait_send()
        on_to_y(part).wait_send()
        on_to_x(part).wait_send()

    return begin, add_core, add_near, add_last, end


def plane_scatter_scratch(share, width):
    rows = share // 2 // LINE_CHUNKS
    by_part = pltpu.SemaphoreType.DMA((LINE_CHUNKS,))
    by_side = pltpu.SemaphoreType.DMA((2, LINE_CHUNKS))
    return [
        pltpu.VMEM((LINE_CHUNKS, 2, 4, rows, width), BF16),
        pltpu.VMEM((2, 4, rows, width), BF16),
        pltpu.VMEM((LINE_CHUNKS, 2, rows, width), BF16),
        pltpu.VMEM((LINE_CHUNKS, 2, rows, width), BF16),
        pltpu.VMEM((LINE_CHUNKS, 2, rows, width), BF16),
        by_part, by_part, pltpu.SemaphoreType.DMA, by_part, by_part, by_part, by_part, by_side, by_side,
    ]


def gain_lanes(lanes, weight, summed, index):
    own = jnp.sum(weight.astype(F32) * summed, 1, keepdims=True)
    return jnp.where(iota(lanes.shape, 1) == index, own * lanes, lanes)


def common_sum(group, place, ranges, state_rows, piece_out, lanes, refs):
    common_ref, state_ref, gains_ref, outbox, inbox, send_sem, recv_sem = refs
    rows, width = common_ref.shape
    start, stop = state_rows
    first = 0
    for column, count in ranges:
        outbox[:, first : first + count] = piece_out[:, column : column + count].astype(BF16)
        first += count
    state = piece_out[start:stop, piece_out.shape[1] - LANES :]
    for peer in range(group):
        outbox[peer * rows : peer * rows + stop - start, width : width + LANES] = state.astype(BF16)
    outbox[:, width + LANES :] = lanes.astype(BF16)
    copies = []
    for hop in range(1, group):
        peer = lax.rem(place + hop, group)
        copies.append(
            pltpu.make_async_remote_copy(
                outbox.at[pl.ds(peer * rows, rows)], inbox.at[hop - 1], send_sem.at[hop - 1], recv_sem.at[hop - 1],
                device_id={"tensor": peer}, device_id_type=MESH,
            )
        )
    for copy in copies:
        copy.start()
    total = outbox[pl.ds(place * rows, rows), :].astype(F32)
    for hop, copy in enumerate(copies):
        copy.wait_recv()
        total = total + inbox[hop].astype(F32)
    common_ref[...] = total[:, :width]
    state_ref[...] = total[: stop - start, width : width + LANES]
    gains_ref[...] = total[:, width + LANES :]
    for copy in copies:
        copy.wait_send()


PRODUCT_TURNS = (
    (0, 2, 0, 0), (0, 2, 1, 1), (1, 2, 2, 0), (0, 2, 3, 2), (1, 3, 0, 1), (2, 3, 0, 0), (0, 3, 1, 3), (1, 3, 2, 2),
    (2, 3, 2, 1), (1, 4, 0, 3), (2, 4, 0, 2), (2, 4, 3, 3),
)


def product_steps(left_refs, x_held, right_ref, piece_refs, left_held, made, left_sem, made_sem):
    total, share = left_held.shape[2:]
    owners = piece_refs[0].shape[0] // share
    widths = [ref.shape[1] for ref in piece_refs]

    def left_copy(tile, which):
        cols = pl.ds(pl.multiple_of(tile * share, share), share)
        slot = lax.rem(tile, 2)
        return pltpu.make_async_copy(left_refs[which].at[:, cols], left_held.at[slot, which], left_sem.at[slot, which])

    def made_copy(tile, which):
        slot = lax.rem(tile, 2)
        first = sum(widths[:which])
        return pltpu.make_async_copy(
            made.at[slot, :, pl.ds(first, widths[which])],
            piece_refs[which].at[pl.ds(tile * share, share)],
            made_sem.at[slot, which],
        )

    def load_left(tile):
        left_copy(tile, 0).start()
        left_copy(tile, 1).start()

    def product(tile):
        slot = lax.rem(tile, 2)

        @pl.when(tile + 1 < owners)
        def _():
            load_left(tile + 1)

        @pl.when(tile >= 2)
        def _():
            made_copy(tile - 2, 0).wait()
            made_copy(tile - 2, 1).wait()

        step = 512
        for which in (0, 1):
            left_copy(tile, which).wait()
            left = left_held[slot, which]
            first = sum(widths[:which])
            for col in range(0, widths[which], step):
                if which == 0:
                    right = x_held[:, :, col : col + step].reshape(total, step)
                else:
                    right = right_ref[:, col : col + step]
                made[slot, :, first + col : first + col + step] = mat_tn(left, right).astype(BF16)
            made_copy(tile, which).start()

    def end():
        for tile in (owners - 2, owners - 1):
            made_copy(tile, 0).wait()
            made_copy(tile, 1).wait()

    return load_left, product, end


def line_sum_kernel(
    group, spread, by_rows, finish, own_count, side_count, piece_count, products, gather_rows, gain_index, ranges,
    state_rows, *refs,
):
    def take(count):
        nonlocal refs
        taken, refs = refs[:count], refs[count:]
        return taken

    x_ref, w_ref = take(2)
    own_refs = take(own_count)
    if products:
        left_refs, (right_ref,) = take(2), take(1)
    else:
        piece_refs = take(piece_count)
    gather_refs = take(len(gather_rows))
    if piece_count:
        weight_ref, lanes_ref = take(2)
    (out_ref,) = take(1)
    side_refs = take(side_count)
    if products:
        piece_refs = take(piece_count)
    if piece_count:
        (piece_out,) = take(1)
        common_refs = take(3 if ranges else 1)
    full_refs = take(len(gather_rows))
    x_held, w_held, load_sem, held, part, sum_send, sum_recv, out_send, out_recv = take(9)
    place = lax.axis_index("tensor")
    away = group - 1 - place
    chunks = LINE_CHUNKS
    rows = x_ref.shape[1] // chunks
    few = rows // 2
    model = out_ref.shape[-1]
    tile = model // group
    more = (place < group - 1, place > 0)
    ahead = (place > 0, place < group - 1)

    def load_x():
        return pltpu.make_async_copy(x_ref, x_held, load_sem.at[group])

    def load_w(index):
        cols = pl.ds(index * tile, tile)
        if by_rows:
            return pltpu.make_async_copy(w_ref.at[cols], w_held.at[cols], load_sem.at[index])
        return pltpu.make_async_copy(w_ref.at[:, cols], w_held.at[:, cols], load_sem.at[index])

    load_x().start()
    for index in range(group):
        load_w(index).start()
    greet(place, group, lax.axis_index("dp"), piece_count + len(gather_rows) > 0, bool(ranges))
    if piece_count:
        begin, add_core, add_near, add_last, end = plane_scatter_steps(piece_refs, piece_out, *take(5), take(9))
        if products:
            load_left, product, product_end = product_steps(left_refs, x_held, right_ref, piece_refs, *take(4))
            load_left(0)
        else:
            begin()
    if gather_rows:
        pieces = list(zip(gather_refs, full_refs, gather_rows))
        begin, neighbours, corner, end = plane_gather_steps(pieces, *take(3))
        begin()

    def multiply(chunk, index):
        left = x_held[:, pl.ds(chunk * rows, rows), :].reshape(group * rows, x_ref.shape[2])
        cols = pl.ds(index * tile, tile)
        product = mat_nt(left, w_held[cols, :]) if by_rows else mat(left, w_held[:, cols])
        part[lax.rem(chunk, 2), :, :, cols] = product.reshape(group, rows, tile)

    def sum_copy(side, chunk, share, half):
        block = held.at[chunk, share + 1 - side, pl.ds(half * few, few)]
        index = 2 * chunk + half
        return pltpu.make_async_remote_copy(
            block, block, sum_send.at[side, index, share], sum_recv.at[side, index, share],
            device_id={"tensor": place + 1 - 2 * side}, device_id_type=MESH,
        )

    def out_copy(side, chunk, source, half):
        block = out_ref.at[source, pl.ds(chunk * rows + half * few, few)]
        index = 2 * chunk + half
        return pltpu.make_async_remote_copy(
            block, block, out_send.at[side, index, source], out_recv.at[side, index, source],
            device_id={"tensor": place + 1 - 2 * side}, device_id_type=MESH,
        )

    load_x().wait()
    for index in range(group):
        load_w(index).wait()
        multiply(0, index)

    def pass_out(chunk, slot, half):
        for side in (0, 1):
            source = place - (slot + 1) if side == 0 else place + (slot + 1)

            @pl.when((chunk > 0) & (source >= 0) & (source < group))
            def _():
                out_copy(side, chunk - 1, source, half).wait_recv()

                @pl.when(more[side])
                def _():
                    out_copy(side, chunk - 1, source, half).start()

    def add_on(chunk, slot, half):
        local = pl.ds(half * few, few)
        for side in (0, 1):
            depth = place if side == 0 else away
            share = group - 1 - slot + place if side == 0 else slot - away

            @pl.when((chunk < chunks) & (depth <= slot))
            def _():
                mine = part[lax.rem(chunk, 2), share, local]
                spot = share + 1 - side

                @pl.when(ahead[side])
                def _():
                    sum_copy(side, chunk, share, half).wait_recv()
                    held[chunk, spot, local] = (held[chunk, spot, local].astype(F32) + mine).astype(BF16)

                @pl.when(jnp.logical_not(ahead[side]))
                def _():
                    held[chunk, spot, local] = mine.astype(BF16)

                sum_copy(side, chunk, share, half).start()

    def complete(chunk, half):
        local = pl.ds(half * few, few)

        @pl.when(chunk < chunks)
        def _():
            total = part.at[lax.rem(chunk, 2), place, local]
            for side in (0, 1):

                @pl.when(ahead[side])
                def _():
                    sum_copy(side, chunk, place, half).wait_recv()
                    total[...] += held[chunk, place + 1 - side, local].astype(F32)

            mine = pl.ds(chunk * rows + half * few, few)
            result = finish(total[...], mine, own_refs, side_refs)
            if spread:
                out_ref[place, mine, :] = result
                for side in (0, 1):

                    @pl.when(more[side])
                    def _():
                        out_copy(side, chunk, place, half).start()
            else:
                out_ref[mine, :] = result

    def one_chunk(chunk, carry):
        for slot in range(group):
            for half in (0, 1):
                if slot + 1 < group and spread:
                    pass_out(chunk, slot, half)
                if slot < group - 1:
                    add_on(chunk, slot, half)
                else:
                    complete(chunk, half)

            @pl.when(chunk + 1 < chunks)
            def _():
                multiply(chunk + 1, slot)

            if products:

                @pl.when(chunk < 2)
                def _():
                    product(chunk * group + slot)

                if slot == group - 1:

                    @pl.when(chunk == 1)
                    def _():
                        product_end()
                        begin()

                for step, turn_chunk, turn_slot, index in PRODUCT_TURNS:
                    if turn_slot == slot:

                        @pl.when(chunk == turn_chunk)
                        def _():
                            (add_core, add_near, add_last)[step](index)

            if piece_count and not products and slot == 0:

                @pl.when(chunk < chunks)
                def _():
                    add_core(chunk)

            if piece_count and not products and slot == group // 2:

                @pl.when(chunk < chunks)
                def _():
                    add_near(chunk)

            if piece_count and not products and slot == 1:

                @pl.when(chunk > 0)
                def _():
                    add_last(chunk - 1)

            if gather_rows and slot == 1:

                @pl.when(chunk < PLANE_PARTS)
                def _():
                    neighbours(chunk)

            if gather_rows and slot == group // 2:

                @pl.when((chunk >= PLANE_PARTS // 2) & (chunk < PLANE_PARTS))
                def _():
                    corner(chunk - PLANE_PARTS // 2)

        return carry

    lax.fori_loop(0, chunks + 1 if spread or piece_count else chunks, one_chunk, 0)
    if piece_count:
        lanes = gain_lanes(lanes_ref[...], weight_ref[...], piece_out[:, : weight_ref.shape[1]], gain_index)
        if ranges:
            common_sum(group, place, ranges, state_rows, piece_out, lanes, common_refs + take(4))
        else:
            common_refs[0][...] = lanes

    def finish_sends(chunk, carry):
        for half in (0, 1):
            for slot in range(group):
                for side in (0, 1):
                    depth = place if side == 0 else away
                    share = group - 1 - slot + place if side == 0 else slot - away
                    if slot < group - 1:

                        @pl.when(depth <= slot)
                        def _():
                            sum_copy(side, chunk, share, half).wait_send()

                    source = place - slot if side == 0 else place + slot
                    if spread:

                        @pl.when((source >= 0) & (source < group) & more[side])
                        def _():
                            out_copy(side, chunk, source, half).wait_send()

        if piece_count:
            end(chunk)
        return carry

    lax.fori_loop(0, chunks, finish_sends, 0)
    if gather_rows:
        end()


def line_sum(
    x, w, own, by_rows, finish, side_shapes, group, model, collective_id, name, dp_size,
    spread=True, pieces=(), products=(), gains=None, ranges=(), state_rows=None, gathers=(),
):
    total = x.shape[0]
    rows = total // group
    vmem = pl.BlockSpec(memory_space=pltpu.VMEM)
    anywhere = pl.BlockSpec(memory_space=pl.ANY)
    piece_rows = rows // LINE_CHUNKS
    sems = pltpu.SemaphoreType.DMA((2, 2 * LINE_CHUNKS, group))
    out_shape = [jax.ShapeDtypeStruct((group, rows, model), BF16) if spread else jax.ShapeDtypeStruct((rows, model), F32)]
    out_shape += side_shapes
    scratch = [
        pltpu.VMEM((group, rows, x.shape[1]), BF16),
        pltpu.VMEM(w.shape, BF16),
        pltpu.SemaphoreType.DMA((group + 1,)),
        pltpu.VMEM((LINE_CHUNKS, group + 1, piece_rows, model), BF16),
        pltpu.VMEM((2, group, piece_rows, model), F32),
        sems, sems, sems, sems,
    ]
    late = []
    if products and (dp_size != 8 or group != 4):
        lefts, right = products[:2], products[2]
        pieces = [mat_tn(lefts[0], x).astype(BF16), mat_tn(lefts[1], right).astype(BF16)]
        products = ()
    if dp_size != 8:
        if pieces:
            share = pieces[0].shape[0] // dp_size
            parts = [scatter(piece, "dp", 0) if piece.shape[0] > share else lax.psum(piece, "dp") for piece in pieces]
            late = [jnp.concatenate(parts, 1).astype(F32)]
            weight, lanes, gain_index = gains
            lanes = gain_lanes(lanes, weight, late[0][:, : weight.shape[1]], gain_index)
            if ranges:
                columns = [late[0][:, start : start + count] for start, count in ranges]
                late += [
                    scatter(jnp.concatenate(columns, 1).astype(BF16), "tensor", 0).astype(F32),
                    lax.psum(late[0][state_rows[0] : state_rows[1], late[0].shape[1] - LANES :], "tensor"),
                    scatter(lanes, "tensor", 0),
                ]
            else:
                late += [lanes]
        late += [plane_gather_plain(array, kind) for array, kind in gathers]
        pieces, ranges, gathers = (), (), ()
    outs = [vmem] * len(out_shape)
    last, gain_index = [], 0
    piece_inputs, piece_specs = list(pieces), [anywhere] * len(pieces)
    if products:
        pieces = [jax.ShapeDtypeStruct((model, x.shape[1]), BF16), jax.ShapeDtypeStruct((model, products[2].shape[1]), BF16)]
        piece_inputs, piece_specs = list(products), [anywhere, anywhere, vmem]
        out_shape += pieces
        outs += [anywhere] * 2
    if pieces:
        share, width = pieces[0].shape[0] // dp_size, sum(piece.shape[1] for piece in pieces)
        last, gain_index = list(gains[:2]), gains[2]
        out_shape += [jax.ShapeDtypeStruct((share, width), F32)]
        scratch += plane_scatter_scratch(share, width)
        if products:
            scratch += [
                pltpu.VMEM((2, 2, total, share), BF16),
                pltpu.VMEM((2, share, width), BF16),
                pltpu.SemaphoreType.DMA((2, 2)),
                pltpu.SemaphoreType.DMA((2, 2)),
            ]
        if ranges:
            common_width = sum(count for _, count in ranges)
            out_shape += [
                jax.ShapeDtypeStruct((share // group, common_width), F32),
                jax.ShapeDtypeStruct((state_rows[1] - state_rows[0], LANES), F32),
                jax.ShapeDtypeStruct((share // group, LANES), F32),
            ]
            scratch += [
                pltpu.VMEM((share, common_width + 2 * LANES), BF16),
                pltpu.VMEM((group - 1, share // group, common_width + 2 * LANES), BF16),
                pltpu.SemaphoreType.DMA((group - 1,)),
                pltpu.SemaphoreType.DMA((group - 1,)),
            ]
        else:
            out_shape += [jax.ShapeDtypeStruct((share, LANES), F32)]
        outs += [vmem] * (len(out_shape) - len(outs))
    if gathers:
        for array, kind in gathers:
            shape = (dp_size * array.shape[0], array.shape[1]) if kind else (array.shape[0], dp_size * array.shape[1])
            out_shape += [jax.ShapeDtypeStruct(shape, BF16)]
            outs += [anywhere]
        scratch += plane_gather_scratch(len(gathers))
    results = pl.pallas_call(
        functools.partial(
            line_sum_kernel, group, spread, by_rows, finish, len(own), len(side_shapes), len(pieces), bool(products),
            tuple(kind for _, kind in gathers), gain_index, ranges, state_rows,
        ),
        in_specs=[anywhere] * 2 + [vmem] * len(own) + piece_specs + [anywhere] * len(gathers) + [vmem] * len(last),
        out_specs=outs,
        out_shape=out_shape,
        scratch_shapes=scratch,
        compiler_params=pltpu.CompilerParams(
            collective_id=collective_id, has_side_effects=True, vmem_limit_bytes=62 << 20
        ),
        name=name,
    )(x.reshape(group, rows, x.shape[1]), w, *own, *piece_inputs, *[array for array, _ in gathers], *last)
    results = list(results)
    if spread:
        results[0] = results[0].reshape(total, model)
    if products:
        del results[1 + len(side_shapes) : 3 + len(side_shapes)]
    return results + late


def unpack_kernel(
    heads, query_cols, first_query, dp_size, group, in_ref, ffn_ref, common_ref, state_ref, gains_ref,
    gain_one, query, pair, output, inner, state, step, conv_inner, conv_state, head, gate_gain, mamba, gain_two,
    expand, shrink,
):
    owner, place = lax.axis_index("dp"), lax.axis_index("tensor")
    channels = heads * PM
    hidden = shrink.shape[0]
    state_cols = 2 * channels + 2 * NS
    inner[:, 0, :] = in_ref[:, :channels]
    inner[:, 1, :] = in_ref[:, channels : 2 * channels]
    step[...] = in_ref[:, state_cols : state_cols + heads]
    query[...] = in_ref[:, first_query : first_query + query_cols]
    first = in_ref.shape[1] - LANES - query_cols - channels
    for row in range(0, query_cols, LANES):
        output[row : row + LANES, :] = in_ref[:, first + row : first + row + LANES].T
    first += query_cols
    for row in range(0, channels, LANES):
        mamba[row : row + LANES, :] = in_ref[:, first + row : first + row + LANES].T
    for tile in range(hidden // HIDDEN_TILE):
        cols = slice(tile * HIDDEN_TILE, (tile + 1) * HIDDEN_TILE)
        for kind in (0, 1):
            start = (2 * tile + kind) * HIDDEN_TILE
            expand[:, kind, cols] = ffn_ref[:, start : start + HIDDEN_TILE]
    for row in range(0, hidden, LANES):
        shrink[row : row + LANES, :] = ffn_ref[:, 2 * hidden + row : 2 * hidden + row + LANES].T
    state[...] = common_ref[:, : 2 * NS]
    pair[...] = common_ref[:, 2 * NS :]
    for lane, gain in ((0, gain_one), (1, gain_two)):
        column = gains_ref[:, lane : lane + 1]
        rows = column.shape[0]
        gain[...] = jnp.sum(jnp.where(iota((rows, rows), 0) == iota((rows, rows), 1), column, 0.0), 0, keepdims=True)
    piece = PM // dp_size
    last = in_ref.shape[1] - LANES
    gate_first = (channels + 2 * NS) // LANES * 8 + 8
    head[...] = in_ref[gate_first - 8 : gate_first - 5, last : last + heads]
    for index in range(heads // 2):
        for start, rows, target in ((0, KC + 1, conv_inner), (gate_first, 1, gate_gain)):
            block = in_ref[start + 8 * index : start + 8 * index + 8, last:]
            block = pltpu.roll(block, lax.rem(LANES - owner * piece, LANES), 1)
            for side in (0, 1):
                values = block[:rows, side * PM : side * PM + piece]
                if rows == 1:
                    target[2 * index + side : 2 * index + side + 1, :] = values
                else:
                    target[:, 2 * index + side, :] = values
    width = conv_state.shape[1]
    column = (owner * group + place) * width
    block = state_ref[pl.ds(pl.multiple_of(column // LANES * 8, 8), 8), :]
    block = pltpu.roll(block, lax.rem(LANES - lax.rem(column, LANES), LANES), 1)
    conv_state[...] = block[: KC + 1, :width]


def unpack(in_sum, ffn_sum, common, state, gains, heads, query_cols, first_query, hidden, dp_size, group):
    share, rows, channels, own_cols = in_sum.shape[0], common.shape[0], heads * PM, in_sum.shape[0]
    vmem = pl.BlockSpec(memory_space=pltpu.VMEM)
    shapes = [
        (1, rows), (share, query_cols), (rows, common.shape[1] - 2 * NS), (query_cols, own_cols), (share, 2, channels),
        (rows, 2 * NS), (share, heads), (KC + 1, heads, PM // dp_size), (KC + 1, 2 * NS // (dp_size * group)),
        (3, heads), (heads, PM // dp_size), (channels, own_cols), (1, rows), (share, 2, hidden), (hidden, own_cols),
    ]
    results = list(
        pl.pallas_call(
            functools.partial(unpack_kernel, heads, query_cols, first_query, dp_size, group),
            in_specs=[vmem] * 5,
            out_specs=[vmem] * len(shapes),
            out_shape=[jax.ShapeDtypeStruct(shape, F32) for shape in shapes],
            compiler_params=pltpu.CompilerParams(vmem_limit_bytes=48 << 20),
            name="unpack",
        )(in_sum, ffn_sum, common, state, gains)
    )
    results[0], results[12] = results[0].reshape(rows), results[12].reshape(rows)
    return results


def project_kernel(tokens_ref, gains_ref, w_ref, lin_ref, first_ref, gain_rows_ref):
    @pl.when(pl.program_id(0) == 0)
    def _():
        picks = (iota((8, LANES), 0) + LANES - 2 == iota((8, LANES), 1)).astype(BF16)
        gain_rows_ref[...] = mat_nt(picks, gains_ref[...])
        gain = gain_rows_ref[0:1]

        def normalise(step, carry):
            rows = pl.ds(step * CHUNK, CHUNK)
            values = tokens_ref[rows, :].astype(F32)
            first_ref[rows, :] = (values * rms_rows(values) * gain).astype(BF16)
            return carry

        lax.fori_loop(0, tokens_ref.shape[0] // CHUNK, normalise, 0)

    lin_ref[...] = mat(first_ref[...], w_ref[...])


def project(tokens, weight, gain_block):
    total, model = tokens.shape
    cols = weight.shape[1]
    tile = 512
    return pl.pallas_call(
        project_kernel,
        grid=(cols // tile,),
        in_specs=[
            whole_block(tokens),
            pl.BlockSpec((model, LANES), lambda c: (0, gain_block)),
            pl.BlockSpec((model, tile), lambda c: (0, c)),
        ],
        out_specs=[
            pl.BlockSpec((total, tile), lambda c: (0, c)),
            pl.BlockSpec((total, model), lambda c: (0, 0)),
            pl.BlockSpec((8, model), lambda c: (0, 0)),
        ],
        out_shape=[
            jax.ShapeDtypeStruct((total, cols), F32),
            jax.ShapeDtypeStruct((total, model), BF16),
            jax.ShapeDtypeStruct((8, model), F32),
        ],
        compiler_params=pltpu.CompilerParams(vmem_limit_bytes=56 << 20),
        name="project",
    )(tokens, weight, weight)


def exchange_copies(group, own_ref, slots, send_sem, recv_sem):
    place = lax.axis_index("tensor")
    return [
        pltpu.make_async_remote_copy(
            own_ref, slots.at[hop - 1], send_sem.at[hop - 1], recv_sem.at[hop - 1],
            device_id={"tensor": lax.rem(place + hop, group)}, device_id_type=MESH,
        )
        for hop in range(1, group)
    ]


def exchange_scratch(group, shape):
    return [
        pltpu.VMEM((group - 1,) + shape, F32),
        pltpu.SemaphoreType.DMA((group - 1,)),
        pltpu.SemaphoreType.DMA((group - 1,)),
    ]


def gate_norm_kernel(
    group, square_ref, ssm_ref, gate_ref, gain_ref, attended_ref, mix_ref, inverse_ref, slots, send_sem, recv_sem
):
    greet(lax.axis_index("tensor"), group, None, False, True)
    copies = exchange_copies(group, square_ref, slots, send_sem, recv_sem)
    for copy in copies:
        copy.start()
    total = square_ref[...]
    for hop, copy in enumerate(copies):
        copy.wait_recv()
        total = total + slots[hop]
    inverse_ref[...] = lax.rsqrt(total * (1.0 / DSSM) + EPS)
    query_cols = attended_ref.shape[1]
    mix_ref[:, :query_cols] = attended_ref[...]

    def norm(step, carry):
        rows = pl.ds(step * CHUNK, CHUNK)
        gate = gate_ref[rows, :]
        gated = ssm_ref[rows, :] * gate * sigmoid(gate)
        mix_ref[rows, query_cols:] = (gated * as_column(inverse_ref[step]) * gain_ref[...]).astype(BF16)
        return carry

    lax.fori_loop(0, square_ref.shape[0], norm, 0)
    for copy in copies:
        copy.wait_send()


def gate_norm(square, ssm, lin, gain, attended, group, collective_id):
    total, channels = ssm.shape
    width = attended.shape[1] + channels
    return pl.pallas_call(
        functools.partial(gate_norm_kernel, group),
        grid=(1,),
        in_specs=[
            whole_block(square),
            whole_block(ssm),
            pl.BlockSpec((total, channels), lambda c: (0, 0)),
            whole_block(gain),
            whole_block(attended),
        ],
        out_specs=[pl.BlockSpec((total, width), lambda c: (0, 0)), whole_block(square)],
        out_shape=[jax.ShapeDtypeStruct((total, width), BF16), jax.ShapeDtypeStruct(square.shape, F32)],
        scratch_shapes=exchange_scratch(group, square.shape),
        compiler_params=pltpu.CompilerParams(
            collective_id=collective_id, has_side_effects=True, vmem_limit_bytes=56 << 20
        ),
        name="gate_norm",
    )(square, ssm, lin, gain, attended)


def gate_back_kernel(
    group, query_cols, mix_ref, w_ref, ssm_ref, gate_ref, gain_ref, attended_ref, normed_ref, cross_ref,
    own, slots, send_sem, recv_sem,
):
    step = pl.program_id(0)

    @pl.when(step == 0)
    def _():
        greet(lax.axis_index("tensor"), group, None, False, True)

    grads = mat_nt(mix_ref[...], w_ref[...])
    attended_ref[...] = grads[:, :query_cols].astype(BF16)
    grads = grads[:, query_cols:]
    normed_ref[...] = grads
    gate = gate_ref[...]
    products = ssm_ref[...] * gate * sigmoid(gate) * (grads * gain_ref[...])
    total = products[:, :LANES]
    for index in range(1, products.shape[1] // LANES):
        total = total + products[:, index * LANES : (index + 1) * LANES]
    per_step = ROWS // CHUNK
    for index in range(per_step):
        own[step * per_step + index] = row_sums_as_row(total[index * CHUNK : (index + 1) * CHUNK])

    @pl.when(step == pl.num_programs(0) - 1)
    def _():
        copies = exchange_copies(group, own, slots, send_sem, recv_sem)
        for copy in copies:
            copy.start()
        result = own[...]
        for hop, copy in enumerate(copies):
            copy.wait_recv()
            result = result + slots[hop]
        cross_ref[...] = result
        for copy in copies:
            copy.wait_send()


def gate_back(mix_all, weight_mix, ssm, lin, gain, query_cols, group, collective_id):
    total, channels = ssm.shape
    model = mix_all.shape[1]
    cross = (total // CHUNK, 1, CHUNK)
    by_rows = lambda cols: pl.BlockSpec((ROWS, cols), lambda c: (c, 0))
    return pl.pallas_call(
        functools.partial(gate_back_kernel, group, query_cols),
        grid=(total // ROWS,),
        in_specs=[by_rows(model), whole_block(weight_mix), by_rows(channels), by_rows(channels), whole_block(gain)],
        out_specs=[by_rows(query_cols), by_rows(channels), pl.BlockSpec(cross, lambda c: (0, 0, 0))],
        out_shape=[
            jax.ShapeDtypeStruct((total, query_cols), BF16),
            jax.ShapeDtypeStruct((total, channels), F32),
            jax.ShapeDtypeStruct(cross, F32),
        ],
        scratch_shapes=[pltpu.VMEM(cross, F32)] + exchange_scratch(group, cross),
        compiler_params=pltpu.CompilerParams(
            collective_id=collective_id, has_side_effects=True, vmem_limit_bytes=56 << 20
        ),
        name="gate_back",
    )(mix_all, weight_mix, ssm, lin, gain)


HIDDEN_TILE = 256


def feed_forward_kernel(second_ref, cot_ref, expand_ref, shrink_ref, act_ref, hidden_ref, out_ref, total):
    step = pl.program_id(0)
    expand = expand_ref[...]
    shrink = shrink_ref[...]
    for first in range(0, second_ref.shape[0], ROWS):
        rows = slice(first, first + ROWS)
        lin = mat(second_ref[rows, :], expand)
        gate, up = lin[:, :HIDDEN_TILE], lin[:, HIDDEN_TILE:]
        sig = sigmoid(gate)
        silu = gate * sig
        act = (silu * up).astype(BF16)
        act_ref[rows, :] = act
        grad = mat_nt(cot_ref[rows, :], shrink)
        hidden_ref[rows, :HIDDEN_TILE] = (grad * up * (sig * (1.0 + gate * (1.0 - sig)))).astype(BF16)
        hidden_ref[rows, HIDDEN_TILE:] = (grad * silu).astype(BF16)
        part = mat(act, shrink)

        @pl.when(step == 0)
        def _():
            total[rows, :] = part

        @pl.when(step > 0)
        def _():
            total[rows, :] += part

    @pl.when(step == pl.num_programs(0) - 1)
    def _():
        out_ref[...] = total[...].astype(BF16)


def feed_forward(second, cot, expand, shrink):
    total, model = second.shape
    hidden = shrink.shape[0]
    return pl.pallas_call(
        feed_forward_kernel,
        grid=(hidden // HIDDEN_TILE,),
        in_specs=[
            pl.BlockSpec(memory_space=pltpu.VMEM),
            pl.BlockSpec(memory_space=pltpu.VMEM),
            pl.BlockSpec((model, 2 * HIDDEN_TILE), lambda c: (0, c)),
            pl.BlockSpec((HIDDEN_TILE, model), lambda c: (c, 0)),
        ],
        out_specs=[
            pl.BlockSpec((total, HIDDEN_TILE), lambda c: (0, c)),
            pl.BlockSpec((total, 2 * HIDDEN_TILE), lambda c: (0, c)),
            pl.BlockSpec((total, model), lambda c: (0, 0)),
        ],
        out_shape=[
            jax.ShapeDtypeStruct((total, hidden), BF16),
            jax.ShapeDtypeStruct((total, 2 * hidden), BF16),
            jax.ShapeDtypeStruct((total, model), BF16),
        ],
        scratch_shapes=[pltpu.VMEM((total, model), F32)],
        compiler_params=pltpu.CompilerParams(vmem_limit_bytes=60 << 20),
        name="feed_forward",
    )(second, cot, expand, shrink)


def mix_finish(total, mine, own_refs, side_refs):
    tokens_ref, gain_ref = own_refs
    middle = tokens_ref[mine, :].astype(F32) + total
    side_refs[0][mine, :] = middle
    return (middle * rms_rows(middle) * gain_ref[...]).astype(BF16)


def second_finish(total, mine, own_refs, side_refs):
    cot_ref, middle_ref, gain_ref = own_refs
    middle = middle_ref[mine, :]
    grad = cot_ref[mine, :].astype(F32) + rms_back(middle, rms_rows(middle), gain_ref[...], total)
    side_refs[0][mine, :] = grad
    return grad.astype(BF16)


def first_finish(total, mine, own_refs, side_refs):
    tokens_ref, middle_ref, gain_ref = own_refs
    tokens = tokens_ref[mine, :].astype(F32)
    return middle_ref[mine, :] + rms_back(tokens, rms_rows(tokens), gain_ref[...], total)


def dot_columns(left, w_ref, cols):
    return mat(left, w_ref[:, cols])


def dot_rows(left, w_ref, cols):
    return mat_nt(left, w_ref[cols, :])


def gather(array, axis_name, axis):
    return lax.all_gather(array, axis_name, axis=axis, tiled=True)


def scatter(array, axis_name, axis):
    return lax.psum_scatter(array, axis_name, scatter_dimension=axis, tiled=True)


def per_device(
    tokens_in, segment_ids, cotangent, norm_first, query_weight, key_value_weight, output_weight,
    inner_weight, state_weight, step_weight, conv_inner, conv_state, head_params, gate_gain,
    mamba_weight, norm_second, expand_weight, shrink_weight,
):
    dp_size = lax.axis_size("dp")
    group = lax.axis_size("tensor")
    place = lax.axis_index("tensor")
    total = segment_ids.shape[0]
    own_rows, model = tokens_in.shape
    share = query_weight.shape[0]
    heads = step_weight.shape[1]
    channels = heads * PM
    query_cols = query_weight.shape[1]
    query_heads = query_cols // HEAD_SIZE
    pair_cols = key_value_weight.shape[1]
    hidden = shrink_weight.shape[0]
    state_cols = 2 * channels + 2 * NS
    mixer_cols = state_cols + LANES
    lead = -(-(mixer_cols + query_cols) // pair_cols) * pair_cols

    step_block = jnp.concatenate(
        [
            step_weight,
            jnp.zeros((share, LANES - 2 - heads), BF16),
            norm_first[:, None],
            norm_second[:, None],
        ],
        1,
    )
    spare = jnp.zeros((share, lead - mixer_cols - query_cols), BF16)
    weight_own = jnp.concatenate(
        [inner_weight.reshape(share, 2 * channels), state_weight, step_block, query_weight, spare, key_value_weight], 1
    )
    weight_mix = gather(jnp.concatenate([output_weight, mamba_weight], 0), "dp", 1)
    tokens_all, weight_in = entry_gather(tokens_in, weight_own, dp_size, group, 1)
    cot_mine, tokens_all, weight_in = lax.optimization_barrier((cotangent, tokens_all, weight_in))
    cot_all = gather(cot_mine, "tensor", 0)

    cosine, sine = angle_tables()
    key_head = (place * query_heads // (QUERY_HEADS // KEY_HEADS)).astype(jnp.int32).reshape(1)
    heads_map = (jnp.arange(channels)[None, :] // PM == jnp.arange(LANES)[:, None]).astype(BF16)
    conv_weight = jnp.concatenate(
        [conv_inner.reshape(KC + 1, channels), conv_state], 1
    ).astype(F32)
    conv_weight = jnp.pad(conv_weight, ((0, 8 - KC - 1), (0, 0)))
    heads_vec = jnp.pad(head_params, ((0, 5), (0, LANES - heads)))
    gate_row = gate_gain.astype(F32).reshape(1, channels)

    lin, first, gains = project(tokens_all, weight_in, mixer_cols // LANES - 1)
    gain_one, gain_two = gains[0:1], gains[1:2]
    query_block = mixer_cols // LANES
    ssm, mixed, square, states = mixer_forward(lin, segment_ids, conv_weight, heads_vec, heads_map, heads)
    attended = attend_forward(lin, query_block, lead, query_heads, key_head, segment_ids, cosine, sine)
    expand_own = jnp.moveaxis(expand_weight.reshape(share, 2, -1, HIDDEN_TILE), 1, 2).reshape(share, 2 * hidden)
    mix_in, inverse = gate_norm(square, ssm, lin, gate_row, attended, group, 4)
    second_all, middle, weight_expand, weight_shrink = line_sum(
        mix_in, weight_mix, [tokens_in, gain_two], False, mix_finish,
        [jax.ShapeDtypeStruct((own_rows, model), F32)], group, model, 2, "mix_sum", dp_size,
        gathers=[(expand_own, True), (shrink_weight, False)],
    )
    act, grad_hidden, ffn_part = feed_forward(second_all, cot_all, weight_expand, weight_shrink)
    lanes = jnp.concatenate(
        [
            (1.0 / norm_first.astype(F32))[:, None],
            (1.0 / norm_second.astype(F32))[:, None],
            jnp.zeros((share, LANES - 2), F32),
        ],
        1,
    )
    mix_all, grad_middle, ffn_sum, lanes = line_sum(
        grad_hidden, weight_expand, [cotangent, middle, gain_two], True, second_finish,
        [jax.ShapeDtypeStruct((own_rows, model), F32)], group, model, 3, "second_sum", dp_size,
        products=(second_all, cot_all, act), gains=(expand_own, lanes, 1),
    )
    ffn_part, mix_all = lax.optimization_barrier((ffn_part, mix_all))
    ffn_out = scatter(ffn_part, "tensor", 0)

    grad_attended, grad_normed, cross = gate_back(mix_all, weight_mix, ssm, lin, gate_row, query_cols, group, 5)
    grad_mix_weight = mat_tn(mix_all, mix_in).astype(BF16)
    grad_lin, small = mixer_backward(
        lin, segment_ids, conv_weight, heads_vec, heads_map, gate_row, grad_normed, inverse, cross,
        ssm, mixed, states, heads, lead, share,
    )
    grad_lin = attend_backward(
        lin, query_block, lead, query_heads, key_head, segment_ids, cosine, sine, grad_attended, grad_lin
    )
    grad_in = mat_tn(first, grad_lin).astype(BF16)
    grad_lin, ffn_out = lax.optimization_barrier((grad_lin, ffn_out))
    block_out = (middle + ffn_out.astype(F32)).astype(BF16)
    grad_tokens, in_sum, common, state, gain_sums = line_sum(
        grad_lin, weight_in, [tokens_in, grad_middle, gain_one], True, first_finish,
        [], group, model, 6, "first_sum", dp_size, spread=False,
        pieces=[grad_in, grad_mix_weight, small.astype(BF16)], gains=(weight_own, lanes, 0),
        ranges=((2 * channels, 2 * NS), (lead, pair_cols)),
        state_rows=(channels // LANES * 8, (channels + 2 * NS) // LANES * 8),
    )
    grads = unpack(
        in_sum, ffn_sum, common, state, gain_sums, heads, query_cols, mixer_cols, hidden, dp_size, group
    )
    return (block_out, grad_tokens, *grads)


def solution(mesh):
    return jax.shard_map(
        per_device,
        mesh=mesh,
        in_specs=(
            P(("dp", "tensor"), None),
            P("dp"),
            P(("dp", "tensor"), None),
            P("dp"),
            P("dp", "tensor"),
            P("dp", None),
            P("tensor", "dp"),
            P("dp", None, "tensor"),
            P("dp", None),
            P("dp", "tensor"),
            P(None, "tensor", None),
            P(),
            P(None, "tensor"),
            P("tensor", None),
            P("tensor", "dp"),
            P("dp"),
            P("dp", None, "tensor"),
            P("tensor", "dp"),
        ),
        out_specs=(
            P(("dp", "tensor"), None),
            P(("dp", "tensor"), None),
            P(("dp", "tensor")),
            P("dp", "tensor"),
            P(("dp", "tensor"), None),
            P("tensor", "dp"),
            P("dp", None, "tensor"),
            P(("dp", "tensor"), None),
            P("dp", "tensor"),
            P(None, "tensor", "dp"),
            P(None, ("dp", "tensor")),
            P(None, "tensor"),
            P("tensor", "dp"),
            P("tensor", "dp"),
            P(("dp", "tensor")),
            P("dp", None, "tensor"),
            P("tensor", "dp"),
        ),
        check_vma=False,
    )
```

```python
import functools
import math

import jax
import jax.numpy as jnp
from jax import lax
from jax.experimental import pallas as pl
from jax.experimental.pallas import tpu as pltpu
from jax.sharding import PartitionSpec as P

QUERY_HEADS = 8
KEY_HEADS = 2
HEAD_SIZE = 128
PM = 64
NS = 256
KC = 4
SEQ_LEN = 1024
DSSM = 3072
LANES = 128
CHUNK = 128
FAR = -1e30


EPS = 1e-05
THETA = 100000000000.0
HIGH = lax.Precision.HIGHEST
F32 = jnp.float32
BF16 = jnp.bfloat16


def mat(left_side, right_side):
    return jnp.dot(left_side, right_side, preferred_element_type=F32)


def mat_nt(left_side, right_side):
    return lax.dot_general(
        left_side, right_side, (((1,), (1,)), ((), ())), preferred_element_type=F32
    )


def mat_tn(left_side, right_side):
    return lax.dot_general(
        left_side, right_side, (((0,), (0,)), ((), ())), preferred_element_type=F32
    )


def iota(shape, dim):
    return lax.broadcasted_iota(jnp.int32, shape, dim)


def halves(value):
    high = value.astype(BF16)
    return high, (value - high.astype(F32)).astype(BF16)


def spread(value, heads_map):
    high, rest = halves(value)
    return mat(high, heads_map) + mat(rest, heads_map)


def gather_heads(value, heads_map):
    high, rest = halves(value)
    return mat_nt(high, heads_map) + mat_nt(rest, heads_map)


def sigmoid(value):
    return 0.5 + 0.5 * jnp.tanh(0.5 * value)


def softplus(value):
    return jnp.maximum(value, 0.0) + jnp.log(1.0 + jnp.exp(-jnp.abs(value)))


def conv_rows(inputs, before, seg, seg_before, weight):
    rows = inputs.shape[0]
    longer = jnp.concatenate([before, inputs], 0)
    seg_longer = jnp.concatenate([seg_before, seg], 0)
    result = weight[KC : KC + 1] + weight[KC - 1 : KC] * inputs
    moved_list = []
    for lag in range(1, KC):
        keep = seg_longer[8 - lag : 8 - lag + rows] == seg
        moved = jnp.where(keep, longer[8 - lag : 8 - lag + rows], 0.0)
        moved_list.append(moved)
        result = result + weight[KC - 1 - lag : KC - lag] * moved
    return result, moved_list


def chunk_decay(step_lin, heads_vec, heads, seg, seg_last_before):
    rows = step_lin.shape[0]
    head_lane = iota((1, LANES), 1) < heads
    shifted = step_lin + heads_vec[1:2]
    step = jnp.where(head_lane, softplus(shifted), 0.0)
    rate = jnp.exp(heads_vec[0:1])
    log_decay = -step * rate
    lower = (iota((rows, rows), 0) >= iota((rows, rows), 1)).astype(F32)
    running = jnp.dot(lower, log_decay, precision=HIGH, preferred_element_type=F32)
    last = running[rows - 1 : rows]
    seg_last = seg[rows - 1 : rows]
    into = jnp.where(seg == seg_last_before, jnp.exp(running), 0.0)
    out = jnp.where(seg == seg_last, jnp.exp(last - running), 0.0)
    across = jnp.where(seg_last == seg_last_before, jnp.exp(last), 0.0)
    return shifted, step, rate, log_decay, running, into, out, across


def two_heads(pair):
    front = iota(pair.shape, 1) < PM
    nothing = jnp.zeros_like(pair)
    return jnp.concatenate(
        [jnp.where(front, pair, nothing), jnp.where(front, nothing, pair)], 0
    )


def pair_decay(running, running_t, bias, index):
    parts = []
    for head in (2 * index, 2 * index + 1):
        gap = running[:, head : head + 1] - running_t[head : head + 1, :] + bias
        parts.append(jnp.exp(gap))
    return parts


def as_column(row):
    return jnp.broadcast_to(row, (8, row.shape[1])).T[:, 0:1]


def row_sums_as_row(values):
    return jnp.sum(values.T, 0, keepdims=True)


def chunk_bias(seg, seg_row):
    rows = seg.shape[0]
    allowed = (iota((rows, rows), 0) >= iota((rows, rows), 1)) & (seg == seg_row)
    return jnp.where(allowed, 0.0, FAR)


def mixer_forward_kernel(
    heads, lin_ref, seg_ref, segr_ref, conv_ref, hp_ref, map_ref,
    ssm_ref, mixed_ref, sums_ref, states_ref, state, tail, seg_tail,
):
    channels = heads * PM
    rows = lin_ref.shape[0]

    @pl.when(lax.rem(pl.program_id(0), SEQ_LEN // CHUNK) == 0)
    def _():
        state[...] = jnp.zeros_like(state)
        tail[...] = jnp.zeros_like(tail)
        seg_tail[...] = jnp.full_like(seg_tail, -1)

    heads_map = map_ref[...]
    seg = seg_ref[...]
    seg_before = seg_tail[...]
    inputs = lin_ref[:, channels : 2 * channels + 2 * NS]
    conv, _ = conv_rows(inputs, tail[...], seg, seg_before, conv_ref[...])
    mixed = (conv * sigmoid(conv)).astype(BF16)
    mixed_ref[...] = mixed
    tail[...] = inputs[rows - 8 :]
    seg_tail[...] = seg[rows - 8 :]

    step_lin = lin_ref[:, 2 * channels + 2 * NS :]
    _, step, _, _, running, into, out, across = chunk_decay(
        step_lin, hp_ref[...], heads, seg, seg_before[7:8]
    )
    inner = mixed[:, :channels].astype(F32)
    state_b = mixed[:, channels : channels + NS]
    state_c = mixed[:, channels + NS :]
    few = jnp.concatenate([across, hp_ref[2:3], jnp.zeros((6, LANES), F32)], 0)
    wide = spread(jnp.concatenate([step, into, out, few], 0), heads_map)
    stepped = (inner * wide[:rows]).astype(BF16)
    leaving = (stepped.astype(F32) * wide[2 * rows : 3 * rows]).astype(BF16)
    held = state[...]
    held_low = held.astype(BF16)
    states_ref[0] = held_low
    base = wide[rows : 2 * rows] * mat(state_c, held_low) + wide[3 * rows + 1 : 3 * rows + 2] * inner
    state[...] = wide[3 * rows : 3 * rows + 1] * held + mat_tn(state_b, leaving)

    gram = mat_nt(state_c, state_b)
    bias = chunk_bias(seg, segr_ref[...])
    running_t = running.T
    total = jnp.zeros((rows, LANES), F32)
    for index in range(heads // 2):
        cols = slice(index * LANES, (index + 1) * LANES)
        first, second = pair_decay(running, running_t, bias, index)
        mixing = jnp.concatenate([first * gram, second * gram], 1).astype(BF16)
        outcome = mat(mixing, two_heads(stepped[:, cols])) + base[:, cols]
        ssm_ref[:, cols] = outcome
        gate = lin_ref[:, cols]
        gated = outcome * gate * sigmoid(gate)
        total = total + gated * gated
    sums_ref[0] = row_sums_as_row(total)


def mixer_backward_kernel(
    heads, lin_ref, before_ref, seg_ref, segb_ref, segr_ref, conv_ref, hp_ref, map_ref, gain_ref,
    gn_ref, inv_ref, cross_ref, ssm_ref, mixed_ref, states_ref, mix_grad_ref, mix_in_ref,
    dlin_ref, small_ref, product_ref, dstate, dnext, seg_next, dconv_ref, dhp_ref, dgain_ref,
):
    channels = heads * PM
    rows = lin_ref.shape[0]
    chunks = SEQ_LEN // CHUNK
    chunk = pl.num_programs(0) - 1 - pl.program_id(0)
    place = lax.rem(chunk, chunks)

    @pl.when(pl.program_id(0) == 0)
    def _():
        dconv_ref[...] = jnp.zeros_like(dconv_ref)
        dhp_ref[...] = jnp.zeros_like(dhp_ref)
        dgain_ref[...] = jnp.zeros_like(dgain_ref)

    @pl.when(place == chunks - 1)
    def _():
        dstate[...] = jnp.zeros_like(dstate)
        dnext[...] = jnp.zeros_like(dnext)
        seg_next[...] = jnp.full_like(seg_next, -1)

    product_ref[...] = mat_tn(mix_grad_ref[...], mix_in_ref[...]).astype(BF16)

    heads_map = map_ref[...]
    seg = seg_ref[...]
    seg_before = jnp.where(place == 0, -1, segb_ref[...])

    gate = lin_ref[:, :channels]
    sig = sigmoid(gate)
    silu = gate * sig
    ssm = ssm_ref[...]
    gated = ssm * silu
    grad_normed = gn_ref[...]
    inverse = as_column(inv_ref[0])
    dgain_ref[0:1] += jnp.sum(gated * inverse * grad_normed, 0, keepdims=True)
    cube = inverse * inverse * inverse * (as_column(cross_ref[0]) * (1.0 / DSSM))
    grad_gated = inverse * (grad_normed * gain_ref[...]) - gated * cube
    grad_out = grad_gated * silu
    grad_gate = grad_gated * ssm * (sig * (1.0 + gate * (1.0 - sig)))
    dlin_ref[:, :channels] = grad_gate.astype(BF16)
    grad_low = grad_out.astype(BF16)

    step_lin = lin_ref[:, 2 * channels + 2 * NS :]
    shifted, step, rate, log_decay, running, into, out, across = chunk_decay(
        step_lin, hp_ref[...], heads, seg, seg_before[7:8]
    )
    mixed = mixed_ref[...]
    inner = mixed[:, :channels].astype(F32)
    state_b = mixed[:, channels : channels + NS]
    state_c = mixed[:, channels + NS :]
    few = jnp.concatenate([across, hp_ref[2:3], jnp.zeros((6, LANES), F32)], 0)
    wide = spread(jnp.concatenate([step, into, out, few], 0), heads_map)
    step_wide = wide[:rows]
    out_wide = wide[2 * rows : 3 * rows]
    skip_wide = wide[3 * rows + 1 : 3 * rows + 2]
    stepped = (inner * step_wide).astype(BF16)
    stepped_wide = stepped.astype(F32)
    leaving = (stepped_wide * out_wide).astype(BF16)

    held = states_ref[0]
    grad_state = dstate[...]
    grad_state_low = grad_state.astype(BF16)
    grad_leaving = mat(state_b, grad_state_low)
    grad_b = mat_nt(leaving, grad_state_low)
    entering = wide[rows : 2 * rows] * grad_out
    entering_low = entering.astype(BF16)
    grad_c = mat_nt(entering_low, held)
    carried = mat(state_c, held)
    dstate[...] = wide[3 * rows : 3 * rows + 1] * grad_state + mat_tn(state_c, entering_low)
    grad_across = jnp.sum(grad_state * held.astype(F32), 0, keepdims=True)

    gram = mat_nt(state_c, state_b)
    bias = chunk_bias(seg, segr_ref[...])
    running_t = running.T
    head_lane = iota((1, LANES), 1)
    head_row = iota((LANES, 1), 0)
    grad_gram = jnp.zeros((rows, rows), F32)
    row_sums = jnp.zeros((rows, LANES), F32)
    column_sums = jnp.zeros((LANES, rows), F32)
    grad_stepped = []
    for index in range(heads // 2):
        cols = slice(index * LANES, (index + 1) * LANES)
        grads = mat_nt(grad_low[:, cols], two_heads(stepped[:, cols]))
        mixings = []
        for side, decay in enumerate(pair_decay(running, running_t, bias, index)):
            part = grads[:, side * rows : (side + 1) * rows] * decay
            grad_gram = grad_gram + part
            part = part * gram
            head = 2 * index + side
            row_sums = jnp.where(head_lane == head, jnp.sum(part, 1, keepdims=True), row_sums)
            column_sums = jnp.where(head_row == head, jnp.sum(part, 0, keepdims=True), column_sums)
            mixings.append((decay * gram).astype(BF16))
        both = mat_tn(jnp.concatenate(mixings, 1), grad_low[:, cols])
        front = iota((rows, LANES), 1) < PM
        grad_stepped.append(jnp.where(front, both[:rows], both[rows:]))
    grad_gram_low = grad_gram.astype(BF16)
    grad_c = grad_c + mat(grad_gram_low, state_b)
    grad_b = grad_b + mat_tn(grad_gram_low, state_c)
    grad_stepped = jnp.concatenate(grad_stepped, 1) + out_wide * grad_leaving
    grad_inner = grad_stepped * step_wide + skip_wide * grad_out

    few = jnp.concatenate([grad_across, jnp.zeros((7, channels), F32)], 0)
    sums = gather_heads(
        jnp.concatenate(
            [stepped_wide * grad_leaving, entering * carried, grad_stepped * inner, grad_out * inner, few], 0
        ),
        heads_map,
    )
    leave = sums[:rows] * out
    grad_running = row_sums - column_sums.T + sums[rows : 2 * rows] - leave
    grad_last = jnp.sum(leave, 0, keepdims=True) + sums[4 * rows : 4 * rows + 1] * across
    grad_running = grad_running + jnp.where(iota((rows, 1), 0) == rows - 1, grad_last, 0.0)
    upper = (iota((rows, rows), 0) <= iota((rows, rows), 1)).astype(F32)
    grad_log = jnp.dot(upper, grad_running, precision=HIGH, preferred_element_type=F32)
    grad_step = sums[2 * rows : 3 * rows] - grad_log * rate
    grad_shifted = jnp.where(head_lane < heads, grad_step * sigmoid(shifted), 0.0)
    first_spare = 2 * channels + 2 * NS + LANES
    dlin_ref[:, first_spare - LANES : first_spare] = grad_shifted.astype(BF16)
    dlin_ref[:, first_spare:] = jnp.zeros((rows, dlin_ref.shape[1] - first_spare), BF16)
    dhp_ref[0:1] += jnp.sum(grad_log * log_decay, 0, keepdims=True)
    dhp_ref[1:2] += jnp.sum(grad_shifted, 0, keepdims=True)
    dhp_ref[2:3] += jnp.sum(sums[3 * rows : 4 * rows], 0, keepdims=True)

    grad_mixed = jnp.concatenate([grad_inner, grad_b, grad_c], 1)
    weight = conv_ref[...]
    inputs = lin_ref[:, channels : 2 * channels + 2 * NS]
    before = before_ref[:, channels : 2 * channels + 2 * NS]
    conv, moved_list = conv_rows(inputs, before, seg, seg_before, weight)
    sig = sigmoid(conv)
    grad_conv = grad_mixed * (sig * (1.0 + conv * (1.0 - sig)))
    dconv_ref[KC : KC + 1] += jnp.sum(grad_conv, 0, keepdims=True)
    dconv_ref[KC - 1 : KC] += jnp.sum(grad_conv * inputs, 0, keepdims=True)
    longer = jnp.concatenate([grad_conv, dnext[...]], 0)
    seg_longer = jnp.concatenate([seg, seg_next[...]], 0)
    grad_inputs = weight[KC - 1 : KC] * grad_conv
    for lag in range(1, KC):
        tap = slice(KC - 1 - lag, KC - lag)
        dconv_ref[tap] += jnp.sum(grad_conv * moved_list[lag - 1], 0, keepdims=True)
        keep = seg_longer[lag : lag + rows] == seg
        grad_inputs = grad_inputs + weight[tap] * jnp.where(keep, longer[lag : lag + rows], 0.0)
    dlin_ref[:, channels : 2 * channels + 2 * NS] = grad_inputs.astype(BF16)
    dnext[...] = grad_conv[:8]
    seg_next[...] = seg[:8]

    @pl.when(pl.program_id(0) == pl.num_programs(0) - 1)
    def _():
        small_ref[...] = jnp.zeros_like(small_ref)
        row = 0
        for array in (dconv_ref, dhp_ref, dgain_ref):
            for first in range(0, array.shape[1], LANES):
                small_ref[row : row + 8, :] = array[:, first : first + LANES]
                row += 8


def whole_block(array):
    return pl.BlockSpec(array.shape, lambda *_: (0,) * array.ndim)


def mixer_forward(lin, seg, conv_weight, heads_vec, heads_map, heads):
    total = lin.shape[0]
    channels = heads * PM
    width = 2 * channels + 2 * NS + LANES
    mixed_width = channels + 2 * NS
    steps = total // CHUNK
    by_rows = lambda cols: pl.BlockSpec((CHUNK, cols), lambda c: (c, 0))
    return pl.pallas_call(
        functools.partial(mixer_forward_kernel, heads),
        grid=(steps,),
        in_specs=[
            by_rows(width),
            by_rows(1),
            pl.BlockSpec((1, CHUNK), lambda c: (0, c)),
            whole_block(conv_weight),
            whole_block(heads_vec),
            whole_block(heads_map),
        ],
        out_specs=[
            by_rows(channels),
            by_rows(mixed_width),
            pl.BlockSpec((1, 1, CHUNK), lambda c: (c, 0, 0)),
            pl.BlockSpec((1, NS, channels), lambda c: (c, 0, 0)),
        ],
        out_shape=[
            jax.ShapeDtypeStruct((total, channels), F32),
            jax.ShapeDtypeStruct((total, mixed_width), BF16),
            jax.ShapeDtypeStruct((steps, 1, CHUNK), F32),
            jax.ShapeDtypeStruct((steps, NS, channels), BF16),
        ],
        scratch_shapes=[
            pltpu.VMEM((NS, channels), F32),
            pltpu.VMEM((8, mixed_width), F32),
            pltpu.VMEM((8, 1), jnp.int32),
        ],
        compiler_params=pltpu.CompilerParams(vmem_limit_bytes=48 << 20),
        name="mixer_forward",
    )(lin, seg.reshape(total, 1), seg.reshape(1, total), conv_weight, heads_vec, heads_map)


def mixer_backward(
    lin, seg, conv_weight, heads_vec, heads_map, gain, grad_normed, inverse, cross, ssm, mixed, states, heads, lead, share,
    grad_mix, mix_in,
):
    total = lin.shape[0]
    channels = heads * PM
    width = 2 * channels + 2 * NS + LANES
    mixed_width = channels + 2 * NS
    steps = total // CHUNK
    by_rows = lambda cols: pl.BlockSpec((CHUNK, cols), lambda c: (steps - 1 - c, 0))
    ahead = lambda cols: pl.BlockSpec(
        (8, cols), lambda c: (jnp.maximum((steps - 1 - c) * (CHUNK // 8) - 1, 0), 0)
    )
    seg_column = seg.reshape(total, 1)
    return pl.pallas_call(
        functools.partial(mixer_backward_kernel, heads),
        grid=(steps,),
        in_specs=[
            by_rows(width),
            ahead(width),
            by_rows(1),
            ahead(1),
            pl.BlockSpec((1, CHUNK), lambda c: (0, steps - 1 - c)),
            whole_block(conv_weight),
            whole_block(heads_vec),
            whole_block(heads_map),
            whole_block(gain),
            by_rows(channels),
            pl.BlockSpec((1, 1, CHUNK), lambda c: (steps - 1 - c, 0, 0)),
            pl.BlockSpec((1, 1, CHUNK), lambda c: (steps - 1 - c, 0, 0)),
            by_rows(channels),
            by_rows(mixed_width),
            pl.BlockSpec((1, NS, channels), lambda c: (steps - 1 - c, 0, 0)),
            pl.BlockSpec((total, grad_mix.shape[1] // steps), lambda c: (0, c)),
            whole_block(mix_in),
        ],
        out_specs=[
            by_rows(lead),
            pl.BlockSpec((share, LANES), lambda c: (0, 0)),
            pl.BlockSpec((grad_mix.shape[1] // steps, mix_in.shape[1]), lambda c: (c, 0)),
        ],
        out_shape=[
            jax.ShapeDtypeStruct((total, lin.shape[1]), BF16),
            jax.ShapeDtypeStruct((share, LANES), F32),
            jax.ShapeDtypeStruct((grad_mix.shape[1], mix_in.shape[1]), BF16),
        ],
        scratch_shapes=[
            pltpu.VMEM((NS, channels), F32),
            pltpu.VMEM((8, mixed_width), F32),
            pltpu.VMEM((8, 1), jnp.int32),
            pltpu.VMEM((8, mixed_width), F32),
            pltpu.VMEM((8, LANES), F32),
            pltpu.VMEM((8, channels), F32),
        ],
        compiler_params=pltpu.CompilerParams(vmem_limit_bytes=48 << 20),
        name="mixer_backward",
    )(
        lin, lin, seg_column, seg_column, seg.reshape(1, total), conv_weight, heads_vec, heads_map, gain,
        grad_normed, inverse, cross, ssm, mixed, states, grad_mix, mix_in,
    )


ROWS = 256


def turn(values, cosine, sine):
    return values * cosine + pltpu.roll(values, HEAD_SIZE // 2, 1) * sine


def attend_weights(query, keys, seg, seg_row, start):
    stop = start + ROWS
    scores = mat_nt(query, keys[:stop]) * (1.0 / math.sqrt(HEAD_SIZE))
    allowed = (iota((ROWS, stop), 0) + start >= iota((ROWS, stop), 1)) & (
        seg[start:stop] == seg_row[:, :stop]
    )
    scores = jnp.where(allowed, scores, FAR)
    shifted = jnp.exp(scores - jnp.max(scores, 1, keepdims=True))
    return shifted * (1.0 / jnp.sum(shifted, 1, keepdims=True))


def attend_forward_kernel(head_ref, q_ref, k_ref, v_ref, seg_ref, segr_ref, cos_ref, sin_ref, out_ref):
    cosine, sine = cos_ref[...], sin_ref[...]
    seg, seg_row = seg_ref[...], segr_ref[...]
    query = turn(q_ref[...], cosine, sine).astype(BF16)
    keys = turn(k_ref[...], cosine, sine).astype(BF16)
    values = v_ref[...].astype(BF16)
    for start in range(0, SEQ_LEN, ROWS):
        weights = attend_weights(query[start : start + ROWS], keys, seg, seg_row, start)
        out_ref[start : start + ROWS, :] = mat(
            weights.astype(BF16), values[: start + ROWS]
        ).astype(BF16)


def attend_backward_kernel(
    first_block, lead, head_ref, q_ref, k_ref, v_ref, seg_ref, segr_ref, cos_ref, sin_ref, do_ref, old_ref,
    dlin_ref, dkeys, dvalues, dq_ref, dkv_ref, sem,
):
    step = pl.program_id(1)
    here = pl.ds(pl.program_id(0) * SEQ_LEN, SEQ_LEN)
    cosine, sine = cos_ref[...], sin_ref[...]
    seg, seg_row = seg_ref[...], segr_ref[...]
    scale = 1.0 / math.sqrt(HEAD_SIZE)

    @pl.when(step == 0)
    def _():
        dkeys[...] = jnp.zeros_like(dkeys)
        dvalues[...] = jnp.zeros_like(dvalues)

    query = turn(q_ref[...], cosine, sine).astype(BF16)
    keys = turn(k_ref[...], cosine, sine).astype(BF16)
    values = v_ref[...].astype(BF16)
    for start in range(0, SEQ_LEN, ROWS):
        stop = start + ROWS
        rows = slice(start, stop)
        weights = attend_weights(query[rows], keys, seg, seg_row, start)
        grad_out = do_ref[rows, :]
        dvalues[:stop] += mat_tn(weights.astype(BF16), grad_out)
        grads = mat_nt(grad_out, values[:stop])
        inner = jnp.sum(grads * weights, 1, keepdims=True)
        scores = (weights * (grads - inner)).astype(BF16)
        dq = mat(scores, keys[:stop]) * scale
        dq_ref[step, rows, :] = turn(dq, cosine[rows], -sine[rows]).astype(BF16)
        dkeys[:stop] += mat_tn(scores, query[rows]) * scale

    def out_copy(head):
        place = pl.ds(pl.multiple_of((first_block + head) * HEAD_SIZE, HEAD_SIZE), HEAD_SIZE)
        return pltpu.make_async_copy(dq_ref.at[head], dlin_ref.at[here, place], sem.at[head])

    out_copy(step).start()

    @pl.when(step == pl.num_programs(1) - 1)
    def _():
        mine = head_ref[0]
        grad_keys = turn(dkeys[...], cosine, -sine)
        grad_values = dvalues[...]
        for head in range(KEY_HEADS):
            same = mine == head
            cols = slice(head * HEAD_SIZE, (head + 1) * HEAD_SIZE)
            dkv_ref[:, cols] = jnp.where(same, grad_keys, 0.0).astype(BF16)
            cols = slice((KEY_HEADS + head) * HEAD_SIZE, (KEY_HEADS + head + 1) * HEAD_SIZE)
            dkv_ref[:, cols] = jnp.where(same, grad_values, 0.0).astype(BF16)
        both = pltpu.make_async_copy(dkv_ref, dlin_ref.at[here, pl.ds(lead, dkv_ref.shape[1])], sem.at[dq_ref.shape[0]])
        both.start()
        for head in range(dq_ref.shape[0]):
            out_copy(head).wait()
        both.wait()


def attend_specs(first_block, lead):
    column = lambda first: pl.BlockSpec((SEQ_LEN, HEAD_SIZE), first)
    pair_block = lead // HEAD_SIZE
    return [
        column(lambda b, h, s: (b, first_block + h)),
        column(lambda b, h, s: (b, pair_block + s[0])),
        column(lambda b, h, s: (b, pair_block + KEY_HEADS + s[0])),
        pl.BlockSpec((SEQ_LEN, 1), lambda b, h, s: (b, 0)),
        pl.BlockSpec((1, SEQ_LEN), lambda b, h, s: (0, b)),
        pl.BlockSpec((SEQ_LEN, HEAD_SIZE), lambda b, h, s: (0, 0)),
        pl.BlockSpec((SEQ_LEN, HEAD_SIZE), lambda b, h, s: (0, 0)),
    ]


def attend_forward(lin, first_block, lead, heads, key_head, seg, cosine, sine):
    total = lin.shape[0]
    return pl.pallas_call(
        attend_forward_kernel,
        grid_spec=pltpu.PrefetchScalarGridSpec(
            num_scalar_prefetch=1,
            grid=(total // SEQ_LEN, heads),
            in_specs=attend_specs(first_block, lead),
            out_specs=pl.BlockSpec((SEQ_LEN, HEAD_SIZE), lambda b, h, s: (b, h)),
        ),
        out_shape=jax.ShapeDtypeStruct((total, heads * HEAD_SIZE), BF16),
        compiler_params=pltpu.CompilerParams(vmem_limit_bytes=48 << 20),
        name="attend_forward",
    )(key_head, lin, lin, lin, seg.reshape(total, 1), seg.reshape(1, total), cosine, sine)


def attend_backward(lin, first_block, lead, heads, key_head, seg, cosine, sine, grad_out, grad_lin):
    total = lin.shape[0]
    return pl.pallas_call(
        functools.partial(attend_backward_kernel, first_block, lead),
        grid_spec=pltpu.PrefetchScalarGridSpec(
            num_scalar_prefetch=1,
            grid=(total // SEQ_LEN, heads),
            in_specs=attend_specs(first_block, lead)
            + [
                pl.BlockSpec((SEQ_LEN, HEAD_SIZE), lambda b, h, s: (b, h)),
                pl.BlockSpec(memory_space=pl.ANY),
            ],
            out_specs=pl.BlockSpec(memory_space=pl.ANY),
            scratch_shapes=[
                pltpu.VMEM((SEQ_LEN, HEAD_SIZE), F32),
                pltpu.VMEM((SEQ_LEN, HEAD_SIZE), F32),
                pltpu.VMEM((heads, SEQ_LEN, HEAD_SIZE), BF16),
                pltpu.VMEM((SEQ_LEN, 2 * KEY_HEADS * HEAD_SIZE), BF16),
                pltpu.SemaphoreType.DMA((heads + 1,)),
            ],
        ),
        out_shape=jax.ShapeDtypeStruct(grad_lin.shape, BF16),
        input_output_aliases={9: 0},
        compiler_params=pltpu.CompilerParams(vmem_limit_bytes=48 << 20),
        name="attend_backward",
    )(key_head, lin, lin, lin, seg.reshape(total, 1), seg.reshape(1, total), cosine, sine, grad_out, grad_lin)


def rms_rows(values):
    return lax.rsqrt(jnp.mean(values * values, -1, keepdims=True) + EPS)


def rms_back(values, inverse, gain, grad):
    scaled = grad * gain
    inner = jnp.mean(scaled * values, -1, keepdims=True)
    return inverse * scaled - values * (inverse * inverse * inverse * inner)


def angle_tables():
    half = HEAD_SIZE // 2
    frequency = jnp.exp(jnp.arange(half).astype(F32) * (-2.0 * math.log(THETA) / HEAD_SIZE))
    turned = jnp.arange(SEQ_LEN).astype(F32)[:, None] * frequency[None, :]
    cosine, sine = jnp.cos(turned), jnp.sin(turned)
    return jnp.concatenate([cosine, cosine], 1), jnp.concatenate([-sine, sine], 1)


MESH = pl.DeviceIdType.MESH
LINE_CHUNKS = 4


CORE, ACROSS, ALONG, CORNER = 1, 2, 4, 6
PLANE_PARTS = 4


def partner(index, bits):
    for bit in (CORE, ACROSS, ALONG):
        if bits & bit:
            index = index + jnp.where(lax.rem(index // bit, 2) == 0, bit, -bit)
    return index


def greet(place, group, owner, plane, everyone=False):
    barrier = pltpu.get_barrier_semaphore()
    if everyone:
        for hop in range(1, group):
            pl.semaphore_signal(
                barrier, inc=1, device_id={"tensor": lax.rem(place + hop, group)}, device_id_type=MESH
            )
        count = group - 1
    else:

        @pl.when(place > 0)
        def _():
            pl.semaphore_signal(barrier, inc=1, device_id={"tensor": place - 1}, device_id_type=MESH)

        @pl.when(place < group - 1)
        def _():
            pl.semaphore_signal(barrier, inc=1, device_id={"tensor": place + 1}, device_id_type=MESH)

        count = jnp.where((place > 0) & (place < group - 1), 2, 1)
    if plane:
        for bits in (CORE, ACROSS, ALONG):
            pl.semaphore_signal(barrier, inc=1, device_id={"dp": partner(owner, bits)}, device_id_type=MESH)
        count = count + 3
    pl.semaphore_wait(barrier, count)


def plane_gather_steps(pieces, local_sem, send_sem, recv_sem):
    owner = lax.axis_index("dp")
    parts = PLANE_PARTS
    half = parts // 2

    def copies(slot, origin, to, part, own=False):
        result = []
        for index, (own_ref, full_ref, by_rows) in enumerate(pieces):
            share, cols = own_ref.shape
            rows = share // parts
            if by_rows:
                block = full_ref.at[pl.ds(origin * share + part * rows, rows)]
            else:
                block = full_ref.at[pl.ds(part * rows, rows), pl.ds(pl.multiple_of(origin * cols, cols), cols)]
            result.append(
                pltpu.make_async_remote_copy(
                    own_ref.at[pl.ds(part * rows, rows)] if own else block,
                    block,
                    send_sem.at[index, slot, part],
                    recv_sem.at[index, slot, part],
                    device_id={"dp": partner(owner, to)},
                    device_id_type=MESH,
                )
            )
        return result

    def start(*args):
        for item in copies(*args):
            item.start()

    def arrive(*args):
        for item in copies(*args):
            item.wait_recv()

    def keeps():
        result = []
        for index, (own_ref, full_ref, by_rows) in enumerate(pieces):
            share, cols = own_ref.shape
            if by_rows:
                block = full_ref.at[pl.ds(owner * share, share)]
            else:
                block = full_ref.at[:, pl.ds(pl.multiple_of(owner * cols, cols), cols)]
            result.append(pltpu.make_async_copy(own_ref, block, local_sem.at[index]))
        return result

    def begin():
        for part in range(parts):
            start(1, owner, ACROSS, part, True)
            start(2, owner, ALONG, (part + half) % parts, True)
            start(0, owner, CORE, part, True)
        for item in keeps():
            item.start()

    def neighbours(part):
        arrive(1, owner, ACROSS, part, True)

        @pl.when(part < half)
        def _():
            start(3, partner(owner, ACROSS), ALONG, part)

        start(4, partner(owner, ACROSS), CORE, part)
        other = (part + half) % parts
        arrive(2, owner, ALONG, other, True)

        @pl.when(part < half)
        def _():
            start(3, partner(owner, ALONG), ACROSS, other)

        start(5, partner(owner, ALONG), CORE, other)

    def corner(step):
        for part in (step, step + half):
            arrive(3, partner(owner, CORNER), ALONG, part)
            start(6, partner(owner, CORNER), CORE, part)

    def end():
        for part in range(parts):
            for slot in (0, 4, 5, 6):
                arrive(slot, owner, CORE, part)
            for slot in range(7):
                for item in copies(slot, owner, CORE, part):
                    item.wait_send()
        for item in keeps():
            item.wait()

    return begin, neighbours, corner, end


def plane_gather_scratch(count):
    return [
        pltpu.SemaphoreType.DMA((count,)),
        pltpu.SemaphoreType.DMA((count, 7, PLANE_PARTS)),
        pltpu.SemaphoreType.DMA((count, 7, PLANE_PARTS)),
    ]


def plane_gather_plain(array, by_rows):
    return gather(array, "dp", 0 if by_rows else 1)


def entry_gather_kernel(
    group, parts, own_ref, weight_ref, out_ref, full_ref,
    local_sem, send_sem, recv_sem, keep_sem, plane_send, plane_recv,
):
    place = lax.axis_index("tensor")
    rows = own_ref.shape[0] // parts
    greet(place, group, lax.axis_index("dp"), True)

    def copy(side, source, part, own=False):
        block = out_ref.at[source, pl.ds(part * rows, rows)]
        return pltpu.make_async_remote_copy(
            own_ref.at[pl.ds(part * rows, rows)] if own else block,
            block,
            send_sem.at[side, source, part],
            recv_sem.at[side, source, part],
            device_id={"tensor": place + 1 - 2 * side},
            device_id_type=MESH,
        )

    begin, neighbours, corner, end = plane_gather_steps(
        [(weight_ref, full_ref, True)], keep_sem, plane_send, plane_recv
    )
    more = (place < group - 1, place > 0)
    for part in range(parts):
        for side in (0, 1):

            @pl.when(more[side])
            def _():
                copy(side, place, part, True).start()

    begin()
    keep = pltpu.make_async_copy(own_ref, out_ref.at[place], local_sem)
    keep.start()
    plane_steps = [functools.partial(neighbours, part) for part in range(PLANE_PARTS)] + [
        functools.partial(corner, step) for step in range(PLANE_PARTS // 2)
    ]
    line_steps = (group - 1) * parts
    done = 0
    for hop in range(1, group):
        for part in range(parts):
            for side in (0, 1):
                source = place - hop if side == 0 else place + hop

                @pl.when((source >= 0) & (source < group))
                def _():
                    copy(side, source, part).wait_recv()

                    @pl.when(more[side])
                    def _():
                        copy(side, source, part).start()

            index = (hop - 1) * parts + part + 1
            while done < len(plane_steps) * index // line_steps:
                plane_steps[done]()
                done += 1

    end()
    keep.wait()
    for hop in range(group):
        for part in range(parts):
            for side in (0, 1):
                source = place - hop if side == 0 else place + hop

                @pl.when((source >= 0) & (source < group) & more[side])
                def _():
                    copy(side, source, part, hop == 0).wait_send()


def line_gather_kernel(group, parts, own_ref, out_ref, local_sem, send_sem, recv_sem):
    place = lax.axis_index("tensor")
    rows = own_ref.shape[0] // parts
    greet(place, group, None, False)

    def copy(side, source, part, own=False):
        block = out_ref.at[source, pl.ds(part * rows, rows)]
        return pltpu.make_async_remote_copy(
            own_ref.at[pl.ds(part * rows, rows)] if own else block,
            block,
            send_sem.at[side, source, part],
            recv_sem.at[side, source, part],
            device_id={"tensor": place + 1 - 2 * side},
            device_id_type=MESH,
        )

    keep = pltpu.make_async_copy(own_ref, out_ref.at[place], local_sem)
    keep.start()
    more = (place < group - 1, place > 0)
    for part in range(parts):
        for side in (0, 1):

            @pl.when(more[side])
            def _():
                copy(side, place, part, True).start()

    for hop in range(1, group):
        for part in range(parts):
            for side in (0, 1):
                source = place - hop if side == 0 else place + hop

                @pl.when((source >= 0) & (source < group))
                def _():
                    copy(side, source, part).wait_recv()

                    @pl.when(more[side])
                    def _():
                        copy(side, source, part).start()

    keep.wait()
    for hop in range(group):
        for part in range(parts):
            for side in (0, 1):
                source = place - hop if side == 0 else place + hop

                @pl.when((source >= 0) & (source < group) & more[side])
                def _():
                    copy(side, source, part, hop == 0).wait_send()


def entry_gather(own, weight, dp_size, group, collective_id):
    rows, cols = own.shape
    parts = 2
    anywhere = pl.BlockSpec(memory_space=pl.ANY)
    line_sems = pltpu.SemaphoreType.DMA((2, group, parts))
    if dp_size != 8:
        all_rows = pl.pallas_call(
            functools.partial(line_gather_kernel, group, parts),
            in_specs=[anywhere],
            out_specs=anywhere,
            out_shape=jax.ShapeDtypeStruct((group, rows, cols), own.dtype),
            scratch_shapes=[pltpu.SemaphoreType.DMA, line_sems, line_sems],
            compiler_params=pltpu.CompilerParams(collective_id=collective_id, has_side_effects=True),
            name="line_gather",
        )(own)
        return all_rows.reshape(group * rows, cols), plane_gather_plain(weight, True)
    all_rows, full = pl.pallas_call(
        functools.partial(entry_gather_kernel, group, parts),
        in_specs=[anywhere] * 2,
        out_specs=[anywhere] * 2,
        out_shape=[
            jax.ShapeDtypeStruct((group, rows, cols), own.dtype),
            jax.ShapeDtypeStruct((dp_size * weight.shape[0], weight.shape[1]), BF16),
        ],
        scratch_shapes=[pltpu.SemaphoreType.DMA, line_sems, line_sems] + plane_gather_scratch(1),
        compiler_params=pltpu.CompilerParams(collective_id=collective_id, has_side_effects=True),
        name="entry_gather",
    )(own, weight)
    return all_rows.reshape(group * rows, cols), full


def plane_scatter_steps(piece_refs, out_ref, got, staged, near_x, near_y, last, sems):
    owner = lax.axis_index("dp")
    share, width = out_ref.shape
    parts = LINE_CHUNKS
    half = share // 2
    rows = half // parts
    targets = (0, ACROSS, CORNER, ALONG)
    core_send, core_recv, stage_sem, x_send, x_recv, y_send, y_recv, last_send, last_recv = sems

    def block(piece_ref, target, side, part):
        first = 0 if piece_ref.shape[0] == share else target * share
        return piece_ref.at[pl.ds(first + side * half + part * rows, rows)]

    def whole_core(part):
        return pltpu.make_async_remote_copy(
            got.at[part], got.at[part], core_send.at[part], core_recv.at[part],
            device_id={"dp": partner(owner, CORE)}, device_id_type=MESH,
        )

    def to_x(part):
        return pltpu.make_async_remote_copy(
            got.at[part, 0, pl.ds(1, 2)], near_x.at[part], x_send.at[part], x_recv.at[part],
            device_id={"dp": partner(owner, ACROSS)}, device_id_type=MESH,
        )

    def to_y(part):
        return pltpu.make_async_remote_copy(
            got.at[part, 1, pl.ds(2, 2)], near_y.at[part], y_send.at[part], y_recv.at[part],
            device_id={"dp": partner(owner, ALONG)}, device_id_type=MESH,
        )

    def on_to_y(part):
        return pltpu.make_async_remote_copy(
            near_x.at[part, 1], last.at[part, 0], last_send.at[0, part], last_recv.at[0, part],
            device_id={"dp": partner(owner, ALONG)}, device_id_type=MESH,
        )

    def on_to_x(part):
        return pltpu.make_async_remote_copy(
            near_y.at[part, 0], last.at[part, 1], last_send.at[1, part], last_recv.at[1, part],
            device_id={"dp": partner(owner, ACROSS)}, device_id_type=MESH,
        )

    def begin():
        def send(part, carry):
            for side in (0, 1):
                for index, bits in enumerate(targets):
                    first = 0
                    for piece_ref in piece_refs:
                        cols = pl.ds(first, piece_ref.shape[1])
                        first += piece_ref.shape[1]
                        pltpu.make_async_remote_copy(
                            block(piece_ref, partner(owner, bits | CORE), side, part),
                            got.at[part, side, index, :, cols],
                            core_send.at[part],
                            core_recv.at[part],
                            device_id={"dp": partner(owner, CORE)},
                            device_id_type=MESH,
                        ).start()
            return carry

        lax.fori_loop(0, parts, send, 0)
        stage(0)

    def stage(part):
        for side in (0, 1):
            for index, bits in enumerate(targets):
                first = 0
                for piece_ref in piece_refs:
                    cols = pl.ds(first, piece_ref.shape[1])
                    first += piece_ref.shape[1]
                    pltpu.make_async_copy(
                        block(piece_ref, partner(owner, bits), side, part), staged.at[side, index, :, cols], stage_sem
                    ).start()

    def add_core(part):
        whole_core(part).wait_recv()
        pltpu.make_async_copy(staged, staged, stage_sem).wait()

        def add(step, carry):
            side, index = step // 4, lax.rem(step, 4)
            total = got[part, side, index].astype(F32) + staged[side, index].astype(F32)
            got[part, side, index] = total.astype(BF16)
            return carry

        lax.fori_loop(0, 8, add, 0)
        to_x(part).start()
        to_y(part).start()

        @pl.when(part + 1 < parts)
        def _():
            stage(part + 1)

    def add_near(part):
        to_x(part).wait_recv()
        near_x[part, 1] = (near_x[part, 1].astype(F32) + got[part, 0, 3].astype(F32)).astype(BF16)
        on_to_y(part).start()
        to_y(part).wait_recv()
        near_y[part, 0] = (near_y[part, 0].astype(F32) + got[part, 1, 1].astype(F32)).astype(BF16)
        on_to_x(part).start()

    def add_last(part):
        for side, near, step in ((0, near_x.at[part, 0], on_to_y), (1, near_y.at[part, 1], on_to_x)):
            step(part).wait_recv()
            total = got[part, side, 0].astype(F32) + near[...].astype(F32)
            out_ref[pl.ds(side * half + part * rows, rows), :] = total + last[part, side].astype(F32)

    def end(part):
        whole_core(part).wait_send()
        to_x(part).wait_send()
        to_y(part).wait_send()
        on_to_y(part).wait_send()
        on_to_x(part).wait_send()

    return begin, add_core, add_near, add_last, end


def plane_scatter_scratch(share, width):
    rows = share // 2 // LINE_CHUNKS
    by_part = pltpu.SemaphoreType.DMA((LINE_CHUNKS,))
    by_side = pltpu.SemaphoreType.DMA((2, LINE_CHUNKS))
    return [
        pltpu.VMEM((LINE_CHUNKS, 2, 4, rows, width), BF16),
        pltpu.VMEM((2, 4, rows, width), BF16),
        pltpu.VMEM((LINE_CHUNKS, 2, rows, width), BF16),
        pltpu.VMEM((LINE_CHUNKS, 2, rows, width), BF16),
        pltpu.VMEM((LINE_CHUNKS, 2, rows, width), BF16),
        by_part, by_part, pltpu.SemaphoreType.DMA, by_part, by_part, by_part, by_part, by_side, by_side,
    ]


def gain_lanes(lanes, weight, summed, index):
    own = jnp.sum(weight.astype(F32) * summed, 1, keepdims=True)
    return jnp.where(iota(lanes.shape, 1) == index, own * lanes, lanes)


def common_sum(group, place, ranges, state_rows, piece_out, lanes, refs):
    common_ref, state_ref, gains_ref, outbox, inbox, send_sem, recv_sem = refs
    rows, width = common_ref.shape
    start, stop = state_rows
    first = 0
    for column, count in ranges:
        outbox[:, first : first + count] = piece_out[:, column : column + count].astype(BF16)
        first += count
    state = piece_out[start:stop, piece_out.shape[1] - LANES :]
    for peer in range(group):
        outbox[peer * rows : peer * rows + stop - start, width : width + LANES] = state.astype(BF16)
    outbox[:, width + LANES :] = lanes.astype(BF16)
    copies = []
    for hop in range(1, group):
        peer = lax.rem(place + hop, group)
        copies.append(
            pltpu.make_async_remote_copy(
                outbox.at[pl.ds(peer * rows, rows)], inbox.at[hop - 1], send_sem.at[hop - 1], recv_sem.at[hop - 1],
                device_id={"tensor": peer}, device_id_type=MESH,
            )
        )
    for copy in copies:
        copy.start()
    total = outbox[pl.ds(place * rows, rows), :].astype(F32)
    for hop, copy in enumerate(copies):
        copy.wait_recv()
        total = total + inbox[hop].astype(F32)
    common_ref[...] = total[:, :width]
    state_ref[...] = total[: stop - start, width : width + LANES]
    gains_ref[...] = total[:, width + LANES :]
    for copy in copies:
        copy.wait_send()


PRODUCT_TURNS = (
    (0, 2, 0, 0), (0, 2, 1, 1), (1, 2, 2, 0), (0, 2, 3, 2), (1, 3, 0, 1), (2, 3, 0, 0), (0, 3, 1, 3), (1, 3, 2, 2),
    (2, 3, 2, 1), (1, 4, 0, 3), (2, 4, 0, 2), (2, 4, 3, 3), (3, 2, 0, 0), (3, 2, 1, 1), (3, 2, 2, 2), (3, 2, 3, 3),
    (3, 3, 0, 4), (3, 3, 1, 5), (3, 3, 2, 6), (3, 3, 3, 7),
)


GATHER_TURNS = (
    (0, 0, 1, 0), (0, 0, 3, 1), (0, 1, 1, 2), (0, 1, 3, 3), (1, 2, 1, 0), (1, 2, 2, 1), (2, 2, 3, 0),
    (3, 3, 0, 0), (3, 3, 1, 1), (3, 3, 2, 2), (3, 3, 3, 3), (3, 4, 1, 4), (3, 4, 2, 5),
)


def product_steps(left_refs, x_held, right_ref, piece_refs, left_held, made, left_sem, made_sem):
    total, share = left_held.shape[2:]
    owners = piece_refs[0].shape[0] // share
    widths = [ref.shape[1] for ref in piece_refs]

    def left_copy(tile, which):
        cols = pl.ds(pl.multiple_of(tile * share, share), share)
        slot = lax.rem(tile, 2)
        return pltpu.make_async_copy(left_refs[which].at[:, cols], left_held.at[slot, which], left_sem.at[slot, which])

    def made_copy(tile, which):
        slot = lax.rem(tile, 2)
        first = sum(widths[:which])
        return pltpu.make_async_copy(
            made.at[slot, :, pl.ds(first, widths[which])],
            piece_refs[which].at[pl.ds(tile * share, share)],
            made_sem.at[slot, which],
        )

    def load_left(tile):
        left_copy(tile, 0).start()
        left_copy(tile, 1).start()

    def product(tile):
        slot = lax.rem(tile, 2)

        @pl.when(tile + 1 < owners)
        def _():
            load_left(tile + 1)

        @pl.when(tile >= 2)
        def _():
            made_copy(tile - 2, 0).wait()
            made_copy(tile - 2, 1).wait()

        step = 512
        for which in (0, 1):
            left_copy(tile, which).wait()
            left = left_held[slot, which]
            first = sum(widths[:which])
            for col in range(0, widths[which], step):
                if which == 0:
                    right = x_held[:, :, col : col + step].reshape(total, step)
                else:
                    right = right_ref[:, col : col + step]
                made[slot, :, first + col : first + col + step] = mat_tn(left, right).astype(BF16)
            made_copy(tile, which).start()

    def end():
        for tile in (owners - 2, owners - 1):
            made_copy(tile, 0).wait()
            made_copy(tile, 1).wait()

    return load_left, product, end


def line_sum_kernel(
    group, spread, by_rows, finish, own_count, side_count, piece_count, products, gather_rows, gain_index, ranges,
    state_rows, *refs,
):
    def take(count):
        nonlocal refs
        taken, refs = refs[:count], refs[count:]
        return taken

    x_ref, w_ref = take(2)
    own_refs = take(own_count)
    if products:
        left_refs, (right_ref, extra_ref) = take(2), take(2)
    else:
        piece_refs = take(piece_count)
    gather_refs = take(len(gather_rows))
    if piece_count:
        weight_ref, lanes_ref = take(2)
    (out_ref,) = take(1)
    side_refs = take(side_count)
    if products:
        piece_refs = take(piece_count)
        (extra_out,) = take(1)
    if piece_count:
        (piece_out,) = take(1)
        common_refs = take(3 if ranges else 1)
    full_refs = take(len(gather_rows))
    if gather_rows:
        (next_ref,) = take(1)
    x_held, w_held, load_sem, held, part, sum_send, sum_recv, out_send, out_recv = take(9)
    place = lax.axis_index("tensor")
    away = group - 1 - place
    chunks = LINE_CHUNKS
    rows = x_ref.shape[1] // chunks
    few = rows // 2
    model = out_ref.shape[-1]
    tile = model // group
    more = (place < group - 1, place > 0)
    ahead = (place > 0, place < group - 1)

    def load_x():
        return pltpu.make_async_copy(x_ref, x_held, load_sem.at[group])

    def load_w(index):
        cols = pl.ds(index * tile, tile)
        if by_rows:
            return pltpu.make_async_copy(w_ref.at[cols], w_held.at[cols], load_sem.at[index])
        return pltpu.make_async_copy(w_ref.at[:, cols], w_held.at[:, cols], load_sem.at[index])

    load_x().start()
    for index in range(group):
        load_w(index).start()
    greet(place, group, lax.axis_index("dp"), piece_count + len(gather_rows) > 0, bool(ranges))
    if piece_count:
        begin, add_core, add_near, add_last, end = plane_scatter_steps(piece_refs, piece_out, *take(5), take(9))
        if products:
            load_left, product, product_end = product_steps(left_refs, x_held, right_ref, piece_refs, *take(4))
            load_left(0)
            extra_held, extra_made, extra_sem = take(3)
            extra_load = pltpu.make_async_copy(extra_ref, extra_held, extra_sem.at[2])
            extra_load.start()

            def extra_copy(index):
                slot = lax.rem(index, 2)
                return pltpu.make_async_copy(
                    extra_made.at[slot], extra_out.at[pl.ds(index * CHUNK, CHUNK)], extra_sem.at[slot]
                )

            def extra_product(index):
                if index == 0:
                    extra_load.wait()
                if index >= 2:
                    extra_copy(index - 2).wait()
                left = right_ref[index * CHUNK : (index + 1) * CHUNK, :]
                for col in range(0, model, tile):
                    extra_made[index % 2, :, col : col + tile] = mat(left, extra_held[:, col : col + tile]).astype(BF16)
                extra_copy(index).start()

        else:
            begin()
    if gather_rows:
        pieces = list(zip(gather_refs, full_refs, gather_rows))
        begin, neighbours, corner, end = plane_gather_steps(pieces, *take(3))
        begin()
        next_w, next_held, next_sem = take(3)

        def load_next():
            return pltpu.make_async_copy(full_refs[0], next_w, next_sem.at[2])

        def next_copy(chunk):
            slot = lax.rem(chunk, 2)
            return pltpu.make_async_copy(
                next_held.at[slot], next_ref.at[:, pl.ds(chunk * rows, rows)], next_sem.at[slot]
            )

        def multiply_next(chunk, half):
            width = next_w.shape[1] // 2

            @pl.when((chunk >= 2) & (half == 0))
            def _():
                next_copy(chunk - 2).wait()

            left = out_ref[:, pl.ds(chunk * rows, rows), :].reshape(group * rows, model)
            for first in range(half * width, (half + 1) * width, tile):
                product = mat(left, next_w[:, first : first + tile])
                next_held[lax.rem(chunk, 2), :, :, first : first + tile] = product.reshape(group, rows, tile)
            if half == 1:
                next_copy(chunk).start()

    def multiply(chunk, index):
        left = x_held[:, pl.ds(chunk * rows, rows), :].reshape(group * rows, x_ref.shape[2])
        cols = pl.ds(index * tile, tile)
        product = mat_nt(left, w_held[cols, :]) if by_rows else mat(left, w_held[:, cols])
        part[lax.rem(chunk, 2), :, :, cols] = product.reshape(group, rows, tile)

    def sum_copy(side, chunk, share, half):
        block = held.at[chunk, share + 1 - side, pl.ds(half * few, few)]
        index = 2 * chunk + half
        return pltpu.make_async_remote_copy(
            block, block, sum_send.at[side, index, share], sum_recv.at[side, index, share],
            device_id={"tensor": place + 1 - 2 * side}, device_id_type=MESH,
        )

    def out_copy(side, chunk, source, half):
        block = out_ref.at[source, pl.ds(chunk * rows + half * few, few)]
        index = 2 * chunk + half
        return pltpu.make_async_remote_copy(
            block, block, out_send.at[side, index, source], out_recv.at[side, index, source],
            device_id={"tensor": place + 1 - 2 * side}, device_id_type=MESH,
        )

    load_x().wait()
    for index in range(group):
        load_w(index).wait()
        multiply(0, index)

    def pass_out(chunk, slot, half):
        for side in (0, 1):
            source = place - (slot + 1) if side == 0 else place + (slot + 1)

            @pl.when((chunk > 0) & (source >= 0) & (source < group))
            def _():
                out_copy(side, chunk - 1, source, half).wait_recv()

                @pl.when(more[side])
                def _():
                    out_copy(side, chunk - 1, source, half).start()

    def add_on(chunk, slot, half):
        local = pl.ds(half * few, few)
        for side in (0, 1):
            depth = place if side == 0 else away
            share = group - 1 - slot + place if side == 0 else slot - away

            @pl.when((chunk < chunks) & (depth <= slot))
            def _():
                mine = part[lax.rem(chunk, 2), share, local]
                spot = share + 1 - side

                @pl.when(ahead[side])
                def _():
                    sum_copy(side, chunk, share, half).wait_recv()
                    held[chunk, spot, local] = (held[chunk, spot, local].astype(F32) + mine).astype(BF16)

                @pl.when(jnp.logical_not(ahead[side]))
                def _():
                    held[chunk, spot, local] = mine.astype(BF16)

                sum_copy(side, chunk, share, half).start()

    def complete(chunk, half):
        local = pl.ds(half * few, few)

        @pl.when(chunk < chunks)
        def _():
            total = part.at[lax.rem(chunk, 2), place, local]
            for side in (0, 1):

                @pl.when(ahead[side])
                def _():
                    sum_copy(side, chunk, place, half).wait_recv()
                    total[...] += held[chunk, place + 1 - side, local].astype(F32)

            mine = pl.ds(chunk * rows + half * few, few)
            result = finish(total[...], mine, own_refs, side_refs)
            if spread:
                out_ref[place, mine, :] = result
                for side in (0, 1):

                    @pl.when(more[side])
                    def _():
                        out_copy(side, chunk, place, half).start()
            else:
                out_ref[mine, :] = result

    def one_chunk(chunk, carry):
        for slot in range(group):
            for half in (0, 1):
                if slot + 1 < group and spread:
                    pass_out(chunk, slot, half)
                if slot < group - 1:
                    add_on(chunk, slot, half)
                else:
                    complete(chunk, half)

            @pl.when(chunk + 1 < chunks)
            def _():
                multiply(chunk + 1, slot)

            if products:

                @pl.when(chunk < 2)
                def _():
                    product(chunk * group + slot)

                if slot == group - 1:

                    @pl.when(chunk == 1)
                    def _():
                        product_end()
                        begin()

                for step, turn_chunk, turn_slot, index in PRODUCT_TURNS:
                    if turn_slot == slot:

                        @pl.when(chunk == turn_chunk)
                        def _():
                            (add_core, add_near, add_last, extra_product)[step](index)

            if piece_count and not products and slot == 0:

                @pl.when(chunk < chunks)
                def _():
                    add_core(chunk)

            if piece_count and not products and slot == group // 2:

                @pl.when(chunk < chunks)
                def _():
                    add_near(chunk)

            if piece_count and not products and slot == 1:

                @pl.when(chunk > 0)
                def _():
                    add_last(chunk - 1)

            if gather_rows:
                for step, turn_chunk, turn_slot, index in GATHER_TURNS:
                    if turn_slot == slot:

                        @pl.when(chunk == turn_chunk)
                        def _():
                            if step == 0:
                                neighbours(index)
                            elif step == 1:
                                corner(index)
                            elif step == 2:
                                end()
                                load_next().start()
                            else:
                                if index == 0:
                                    load_next().wait()
                                multiply_next(index // 2, index % 2)

        return carry

    lax.fori_loop(0, chunks + 1 if spread or piece_count else chunks, one_chunk, 0)
    if piece_count:
        lanes = gain_lanes(lanes_ref[...], weight_ref[...], piece_out[:, : weight_ref.shape[1]], gain_index)
        if ranges:
            common_sum(group, place, ranges, state_rows, piece_out, lanes, common_refs + take(4))
        else:
            common_refs[0][...] = lanes

    def finish_sends(chunk, carry):
        for half in (0, 1):
            for slot in range(group):
                for side in (0, 1):
                    depth = place if side == 0 else away
                    share = group - 1 - slot + place if side == 0 else slot - away
                    if slot < group - 1:

                        @pl.when(depth <= slot)
                        def _():
                            sum_copy(side, chunk, share, half).wait_send()

                    source = place - slot if side == 0 else place + slot
                    if spread:

                        @pl.when((source >= 0) & (source < group) & more[side])
                        def _():
                            out_copy(side, chunk, source, half).wait_send()

        if piece_count:
            end(chunk)
        return carry

    if gather_rows:
        multiply_next(chunks - 1, 0)
        multiply_next(chunks - 1, 1)
    lax.fori_loop(0, chunks, finish_sends, 0)
    if products:
        extra_copy(6).wait()
        extra_copy(7).wait()
    if gather_rows:
        next_copy(chunks - 2).wait()
        next_copy(chunks - 1).wait()


def line_sum(
    x, w, own, by_rows, finish, side_shapes, group, model, collective_id, name, dp_size,
    spread=True, pieces=(), products=(), gains=None, ranges=(), state_rows=None, gathers=(),
):
    total = x.shape[0]
    rows = total // group
    vmem = pl.BlockSpec(memory_space=pltpu.VMEM)
    anywhere = pl.BlockSpec(memory_space=pl.ANY)
    piece_rows = rows // LINE_CHUNKS
    sems = pltpu.SemaphoreType.DMA((2, 2 * LINE_CHUNKS, group))
    out_shape = [jax.ShapeDtypeStruct((group, rows, model), BF16) if spread else jax.ShapeDtypeStruct((rows, model), F32)]
    out_shape += side_shapes
    scratch = [
        pltpu.VMEM((group, rows, x.shape[1]), BF16),
        pltpu.VMEM(w.shape, BF16),
        pltpu.SemaphoreType.DMA((group + 1,)),
        pltpu.VMEM((LINE_CHUNKS, group + 1, piece_rows, model), BF16),
        pltpu.VMEM((2, group, piece_rows, model), F32),
        sems, sems, sems, sems,
    ]
    late = []
    if products and (dp_size != 8 or group != 4):
        lefts, right = products[:2], products[2]
        pieces = [mat_tn(lefts[0], x).astype(BF16), mat_tn(lefts[1], right).astype(BF16)]
        late = [mat(right, products[3]).astype(BF16)]
        products = ()
    if dp_size != 8:
        if pieces:
            share = pieces[0].shape[0] // dp_size
            parts = [scatter(piece, "dp", 0) if piece.shape[0] > share else lax.psum(piece, "dp") for piece in pieces]
            total_sum = jnp.concatenate(parts, 1).astype(F32)
            late += [total_sum]
            weight, lanes, gain_index = gains
            lanes = gain_lanes(lanes, weight, total_sum[:, : weight.shape[1]], gain_index)
            if ranges:
                columns = [total_sum[:, start : start + count] for start, count in ranges]
                late += [
                    scatter(jnp.concatenate(columns, 1).astype(BF16), "tensor", 0).astype(F32),
                    lax.psum(total_sum[state_rows[0] : state_rows[1], total_sum.shape[1] - LANES :], "tensor"),
                    scatter(lanes, "tensor", 0),
                ]
            else:
                late += [lanes]
        late += [plane_gather_plain(array, kind) for array, kind in gathers]
        multiplied, pieces, ranges, gathers = bool(gathers), (), (), ()
    outs = [vmem] * len(out_shape)
    last, gain_index = [], 0
    piece_inputs, piece_specs = list(pieces), [anywhere] * len(pieces)
    if products:
        pieces = [jax.ShapeDtypeStruct((model, x.shape[1]), BF16), jax.ShapeDtypeStruct((model, products[2].shape[1]), BF16)]
        piece_inputs, piece_specs = list(products), [anywhere, anywhere, vmem, anywhere]
        out_shape += pieces + [jax.ShapeDtypeStruct((total, model), BF16)]
        outs += [anywhere] * 3
    if pieces:
        share, width = pieces[0].shape[0] // dp_size, sum(piece.shape[1] for piece in pieces)
        last, gain_index = list(gains[:2]), gains[2]
        out_shape += [jax.ShapeDtypeStruct((share, width), F32)]
        scratch += plane_scatter_scratch(share, width)
        if products:
            scratch += [
                pltpu.VMEM((2, 2, total, share), BF16),
                pltpu.VMEM((2, share, width), BF16),
                pltpu.SemaphoreType.DMA((2, 2)),
                pltpu.SemaphoreType.DMA((2, 2)),
                pltpu.VMEM(products[3].shape, BF16),
                pltpu.VMEM((2, CHUNK, model), BF16),
                pltpu.SemaphoreType.DMA((3,)),
            ]
        if ranges:
            common_width = sum(count for _, count in ranges)
            out_shape += [
                jax.ShapeDtypeStruct((share // group, common_width), F32),
                jax.ShapeDtypeStruct((state_rows[1] - state_rows[0], LANES), F32),
                jax.ShapeDtypeStruct((share // group, LANES), F32),
            ]
            scratch += [
                pltpu.VMEM((share, common_width + 2 * LANES), BF16),
                pltpu.VMEM((group - 1, share // group, common_width + 2 * LANES), BF16),
                pltpu.SemaphoreType.DMA((group - 1,)),
                pltpu.SemaphoreType.DMA((group - 1,)),
            ]
        else:
            out_shape += [jax.ShapeDtypeStruct((share, LANES), F32)]
        outs += [vmem] * (len(out_shape) - len(outs))
    if gathers:
        for array, kind in gathers:
            shape = (dp_size * array.shape[0], array.shape[1]) if kind else (array.shape[0], dp_size * array.shape[1])
            out_shape += [jax.ShapeDtypeStruct(shape, BF16)]
            outs += [anywhere]
        next_width = gathers[0][0].shape[1]
        out_shape += [jax.ShapeDtypeStruct((group, rows, next_width), F32)]
        outs += [anywhere]
        scratch += plane_gather_scratch(len(gathers)) + [
            pltpu.VMEM((model, next_width), BF16),
            pltpu.VMEM((2, group, piece_rows, next_width), F32),
            pltpu.SemaphoreType.DMA((3,)),
        ]
    results = pl.pallas_call(
        functools.partial(
            line_sum_kernel, group, spread, by_rows, finish, len(own), len(side_shapes), len(pieces), bool(products),
            tuple(kind for _, kind in gathers), gain_index, ranges, state_rows,
        ),
        in_specs=[anywhere] * 2 + [vmem] * len(own) + piece_specs + [anywhere] * len(gathers) + [vmem] * len(last),
        out_specs=outs,
        out_shape=out_shape,
        scratch_shapes=scratch,
        compiler_params=pltpu.CompilerParams(
            collective_id=collective_id, has_side_effects=True, vmem_limit_bytes=62 << 20
        ),
        name=name,
    )(x.reshape(group, rows, x.shape[1]), w, *own, *piece_inputs, *[array for array, _ in gathers], *last)
    results = list(results)
    if spread:
        results[0] = results[0].reshape(total, model)
    if gathers:
        results[-1] = results[-1].reshape(total, next_width)
    elif dp_size != 8 and multiplied:
        late += [mat(results[0], late[0])]
    if products:
        del results[1 + len(side_shapes) : 3 + len(side_shapes)]
    return results + late


def unpack_kernel(
    heads, query_cols, first_query, dp_size, group, in_ref, ffn_ref, common_ref, state_ref, gains_ref,
    gain_one, query, pair, output, inner, state, step, conv_inner, conv_state, head, gate_gain, mamba, gain_two,
    expand, shrink,
):
    owner, place = lax.axis_index("dp"), lax.axis_index("tensor")
    channels = heads * PM
    hidden = shrink.shape[0]
    state_cols = 2 * channels + 2 * NS
    inner[:, 0, :] = in_ref[:, :channels]
    inner[:, 1, :] = in_ref[:, channels : 2 * channels]
    step[...] = in_ref[:, state_cols : state_cols + heads]
    query[...] = in_ref[:, first_query : first_query + query_cols]
    first = in_ref.shape[1] - LANES - query_cols - channels
    for row in range(0, query_cols, LANES):
        output[row : row + LANES, :] = in_ref[:, first + row : first + row + LANES].T
    first += query_cols
    for row in range(0, channels, LANES):
        mamba[row : row + LANES, :] = in_ref[:, first + row : first + row + LANES].T
    for tile in range(hidden // HIDDEN_TILE):
        cols = slice(tile * HIDDEN_TILE, (tile + 1) * HIDDEN_TILE)
        for kind in (0, 1):
            start = (2 * tile + kind) * HIDDEN_TILE
            expand[:, kind, cols] = ffn_ref[:, start : start + HIDDEN_TILE]
    for row in range(0, hidden, LANES):
        shrink[row : row + LANES, :] = ffn_ref[:, 2 * hidden + row : 2 * hidden + row + LANES].T
    state[...] = common_ref[:, : 2 * NS]
    pair[...] = common_ref[:, 2 * NS :]
    for lane, gain in ((0, gain_one), (1, gain_two)):
        column = gains_ref[:, lane : lane + 1]
        rows = column.shape[0]
        gain[...] = jnp.sum(jnp.where(iota((rows, rows), 0) == iota((rows, rows), 1), column, 0.0), 0, keepdims=True)
    piece = PM // dp_size
    last = in_ref.shape[1] - LANES
    gate_first = (channels + 2 * NS) // LANES * 8 + 8
    head[...] = in_ref[gate_first - 8 : gate_first - 5, last : last + heads]
    for index in range(heads // 2):
        for start, rows, target in ((0, KC + 1, conv_inner), (gate_first, 1, gate_gain)):
            block = in_ref[start + 8 * index : start + 8 * index + 8, last:]
            block = pltpu.roll(block, lax.rem(LANES - owner * piece, LANES), 1)
            for side in (0, 1):
                values = block[:rows, side * PM : side * PM + piece]
                if rows == 1:
                    target[2 * index + side : 2 * index + side + 1, :] = values
                else:
                    target[:, 2 * index + side, :] = values
    width = conv_state.shape[1]
    column = (owner * group + place) * width
    block = state_ref[pl.ds(pl.multiple_of(column // LANES * 8, 8), 8), :]
    block = pltpu.roll(block, lax.rem(LANES - lax.rem(column, LANES), LANES), 1)
    conv_state[...] = block[: KC + 1, :width]


def unpack(in_sum, ffn_sum, common, state, gains, heads, query_cols, first_query, hidden, dp_size, group):
    share, rows, channels, own_cols = in_sum.shape[0], common.shape[0], heads * PM, in_sum.shape[0]
    vmem = pl.BlockSpec(memory_space=pltpu.VMEM)
    shapes = [
        (1, rows), (share, query_cols), (rows, common.shape[1] - 2 * NS), (query_cols, own_cols), (share, 2, channels),
        (rows, 2 * NS), (share, heads), (KC + 1, heads, PM // dp_size), (KC + 1, 2 * NS // (dp_size * group)),
        (3, heads), (heads, PM // dp_size), (channels, own_cols), (1, rows), (share, 2, hidden), (hidden, own_cols),
    ]
    results = list(
        pl.pallas_call(
            functools.partial(unpack_kernel, heads, query_cols, first_query, dp_size, group),
            in_specs=[vmem] * 5,
            out_specs=[vmem] * len(shapes),
            out_shape=[jax.ShapeDtypeStruct(shape, F32) for shape in shapes],
            compiler_params=pltpu.CompilerParams(vmem_limit_bytes=48 << 20),
            name="unpack",
        )(in_sum, ffn_sum, common, state, gains)
    )
    results[0], results[12] = results[0].reshape(rows), results[12].reshape(rows)
    return results


def project_kernel(tokens_ref, gains_ref, w_ref, lin_ref, first_ref, gain_rows_ref):
    @pl.when(pl.program_id(0) == 0)
    def _():
        picks = (iota((8, LANES), 0) + LANES - 2 == iota((8, LANES), 1)).astype(BF16)
        gain_rows_ref[...] = mat_nt(picks, gains_ref[...])
        gain = gain_rows_ref[0:1]

        def normalise(step, carry):
            rows = pl.ds(step * CHUNK, CHUNK)
            values = tokens_ref[rows, :].astype(F32)
            first_ref[rows, :] = (values * rms_rows(values) * gain).astype(BF16)
            return carry

        lax.fori_loop(0, tokens_ref.shape[0] // CHUNK, normalise, 0)

    lin_ref[...] = mat(first_ref[...], w_ref[...])


def project(tokens, weight, gain_block):
    total, model = tokens.shape
    cols = weight.shape[1]
    tile = 512
    return pl.pallas_call(
        project_kernel,
        grid=(cols // tile,),
        in_specs=[
            whole_block(tokens),
            pl.BlockSpec((model, LANES), lambda c: (0, gain_block)),
            pl.BlockSpec((model, tile), lambda c: (0, c)),
        ],
        out_specs=[
            pl.BlockSpec((total, tile), lambda c: (0, c)),
            pl.BlockSpec((total, model), lambda c: (0, 0)),
            pl.BlockSpec((8, model), lambda c: (0, 0)),
        ],
        out_shape=[
            jax.ShapeDtypeStruct((total, cols), F32),
            jax.ShapeDtypeStruct((total, model), BF16),
            jax.ShapeDtypeStruct((8, model), F32),
        ],
        compiler_params=pltpu.CompilerParams(vmem_limit_bytes=56 << 20),
        name="project",
    )(tokens, weight, weight)


def exchange_copies(group, own_ref, slots, send_sem, recv_sem):
    place = lax.axis_index("tensor")
    return [
        pltpu.make_async_remote_copy(
            own_ref, slots.at[hop - 1], send_sem.at[hop - 1], recv_sem.at[hop - 1],
            device_id={"tensor": lax.rem(place + hop, group)}, device_id_type=MESH,
        )
        for hop in range(1, group)
    ]


def exchange_scratch(group, shape):
    return [
        pltpu.VMEM((group - 1,) + shape, F32),
        pltpu.SemaphoreType.DMA((group - 1,)),
        pltpu.SemaphoreType.DMA((group - 1,)),
    ]


def gate_norm_kernel(
    group, square_ref, ssm_ref, gate_ref, gain_ref, attended_ref, mix_ref, inverse_ref, slots, send_sem, recv_sem
):
    greet(lax.axis_index("tensor"), group, None, False, True)
    copies = exchange_copies(group, square_ref, slots, send_sem, recv_sem)
    for copy in copies:
        copy.start()
    total = square_ref[...]
    for hop, copy in enumerate(copies):
        copy.wait_recv()
        total = total + slots[hop]
    inverse_ref[...] = lax.rsqrt(total * (1.0 / DSSM) + EPS)
    query_cols = attended_ref.shape[1]
    mix_ref[:, :query_cols] = attended_ref[...]

    def norm(step, carry):
        rows = pl.ds(step * CHUNK, CHUNK)
        gate = gate_ref[rows, :]
        gated = ssm_ref[rows, :] * gate * sigmoid(gate)
        mix_ref[rows, query_cols:] = (gated * as_column(inverse_ref[step]) * gain_ref[...]).astype(BF16)
        return carry

    lax.fori_loop(0, square_ref.shape[0], norm, 0)
    for copy in copies:
        copy.wait_send()


def gate_norm(square, ssm, lin, gain, attended, group, collective_id):
    total, channels = ssm.shape
    width = attended.shape[1] + channels
    return pl.pallas_call(
        functools.partial(gate_norm_kernel, group),
        grid=(1,),
        in_specs=[
            whole_block(square),
            whole_block(ssm),
            pl.BlockSpec((total, channels), lambda c: (0, 0)),
            whole_block(gain),
            whole_block(attended),
        ],
        out_specs=[pl.BlockSpec((total, width), lambda c: (0, 0)), whole_block(square)],
        out_shape=[jax.ShapeDtypeStruct((total, width), BF16), jax.ShapeDtypeStruct(square.shape, F32)],
        scratch_shapes=exchange_scratch(group, square.shape),
        compiler_params=pltpu.CompilerParams(
            collective_id=collective_id, has_side_effects=True, vmem_limit_bytes=56 << 20
        ),
        name="gate_norm",
    )(square, ssm, lin, gain, attended)


def gate_back_kernel(
    group, query_cols, mix_ref, w_ref, ssm_ref, gate_ref, gain_ref, attended_ref, normed_ref, cross_ref,
    own, slots, send_sem, recv_sem,
):
    step = pl.program_id(0)

    @pl.when(step == 0)
    def _():
        greet(lax.axis_index("tensor"), group, None, False, True)

    grads = mat_nt(mix_ref[...], w_ref[...])
    attended_ref[...] = grads[:, :query_cols].astype(BF16)
    grads = grads[:, query_cols:]
    normed_ref[...] = grads
    gate = gate_ref[...]
    products = ssm_ref[...] * gate * sigmoid(gate) * (grads * gain_ref[...])
    total = products[:, :LANES]
    for index in range(1, products.shape[1] // LANES):
        total = total + products[:, index * LANES : (index + 1) * LANES]
    per_step = ROWS // CHUNK
    for index in range(per_step):
        own[step * per_step + index] = row_sums_as_row(total[index * CHUNK : (index + 1) * CHUNK])

    @pl.when(step == pl.num_programs(0) - 1)
    def _():
        copies = exchange_copies(group, own, slots, send_sem, recv_sem)
        for copy in copies:
            copy.start()
        result = own[...]
        for hop, copy in enumerate(copies):
            copy.wait_recv()
            result = result + slots[hop]
        cross_ref[...] = result
        for copy in copies:
            copy.wait_send()


def gate_back(mix_all, weight_mix, ssm, lin, gain, query_cols, group, collective_id):
    total, channels = ssm.shape
    model = mix_all.shape[1]
    cross = (total // CHUNK, 1, CHUNK)
    by_rows = lambda cols: pl.BlockSpec((ROWS, cols), lambda c: (c, 0))
    return pl.pallas_call(
        functools.partial(gate_back_kernel, group, query_cols),
        grid=(total // ROWS,),
        in_specs=[by_rows(model), whole_block(weight_mix), by_rows(channels), by_rows(channels), whole_block(gain)],
        out_specs=[by_rows(query_cols), by_rows(channels), pl.BlockSpec(cross, lambda c: (0, 0, 0))],
        out_shape=[
            jax.ShapeDtypeStruct((total, query_cols), BF16),
            jax.ShapeDtypeStruct((total, channels), F32),
            jax.ShapeDtypeStruct(cross, F32),
        ],
        scratch_shapes=[pltpu.VMEM(cross, F32)] + exchange_scratch(group, cross),
        compiler_params=pltpu.CompilerParams(
            collective_id=collective_id, has_side_effects=True, vmem_limit_bytes=56 << 20
        ),
        name="gate_back",
    )(mix_all, weight_mix, ssm, lin, gain)


HIDDEN_TILE = 256


def feed_forward_kernel(cot_ref, lin_ref, shrink_ref, act_ref, hidden_ref):
    shrink = shrink_ref[...]
    for first in range(0, cot_ref.shape[0], ROWS):
        rows = slice(first, first + ROWS)
        gate, up = lin_ref[rows, :HIDDEN_TILE], lin_ref[rows, HIDDEN_TILE:]
        sig = sigmoid(gate)
        silu = gate * sig
        act = (silu * up).astype(BF16)
        act_ref[rows, :] = act
        grad = mat_nt(cot_ref[rows, :], shrink)
        hidden_ref[rows, :HIDDEN_TILE] = (grad * up * (sig * (1.0 + gate * (1.0 - sig)))).astype(BF16)
        hidden_ref[rows, HIDDEN_TILE:] = (grad * silu).astype(BF16)


def feed_forward(cot, hidden_lin, shrink):
    total, model = cot.shape
    hidden = shrink.shape[0]
    return pl.pallas_call(
        feed_forward_kernel,
        grid=(hidden // HIDDEN_TILE,),
        in_specs=[
            pl.BlockSpec(memory_space=pltpu.VMEM),
            pl.BlockSpec((total, 2 * HIDDEN_TILE), lambda c: (0, c)),
            pl.BlockSpec((HIDDEN_TILE, model), lambda c: (c, 0)),
        ],
        out_specs=[
            pl.BlockSpec((total, HIDDEN_TILE), lambda c: (0, c)),
            pl.BlockSpec((total, 2 * HIDDEN_TILE), lambda c: (0, c)),
        ],
        out_shape=[
            jax.ShapeDtypeStruct((total, hidden), BF16),
            jax.ShapeDtypeStruct((total, 2 * hidden), BF16),
        ],
        compiler_params=pltpu.CompilerParams(vmem_limit_bytes=60 << 20),
        name="feed_forward",
    )(cot, hidden_lin, shrink)


def mix_finish(total, mine, own_refs, side_refs):
    tokens_ref, gain_ref = own_refs
    middle = tokens_ref[mine, :].astype(F32) + total
    side_refs[0][mine, :] = middle
    return (middle * rms_rows(middle) * gain_ref[...]).astype(BF16)


def second_finish(total, mine, own_refs, side_refs):
    cot_ref, middle_ref, gain_ref = own_refs
    middle = middle_ref[mine, :]
    grad = cot_ref[mine, :].astype(F32) + rms_back(middle, rms_rows(middle), gain_ref[...], total)
    side_refs[0][mine, :] = grad
    return grad.astype(BF16)


def first_finish(total, mine, own_refs, side_refs):
    tokens_ref, middle_ref, gain_ref = own_refs
    tokens = tokens_ref[mine, :].astype(F32)
    return middle_ref[mine, :] + rms_back(tokens, rms_rows(tokens), gain_ref[...], total)


def dot_columns(left, w_ref, cols):
    return mat(left, w_ref[:, cols])


def dot_rows(left, w_ref, cols):
    return mat_nt(left, w_ref[cols, :])


def gather(array, axis_name, axis):
    return lax.all_gather(array, axis_name, axis=axis, tiled=True)


def scatter(array, axis_name, axis):
    return lax.psum_scatter(array, axis_name, scatter_dimension=axis, tiled=True)


def per_device(
    tokens_in, segment_ids, cotangent, norm_first, query_weight, key_value_weight, output_weight,
    inner_weight, state_weight, step_weight, conv_inner, conv_state, head_params, gate_gain,
    mamba_weight, norm_second, expand_weight, shrink_weight,
):
    dp_size = lax.axis_size("dp")
    group = lax.axis_size("tensor")
    place = lax.axis_index("tensor")
    total = segment_ids.shape[0]
    own_rows, model = tokens_in.shape
    share = query_weight.shape[0]
    heads = step_weight.shape[1]
    channels = heads * PM
    query_cols = query_weight.shape[1]
    query_heads = query_cols // HEAD_SIZE
    pair_cols = key_value_weight.shape[1]
    hidden = shrink_weight.shape[0]
    state_cols = 2 * channels + 2 * NS
    mixer_cols = state_cols + LANES
    lead = -(-(mixer_cols + query_cols) // pair_cols) * pair_cols

    step_block = jnp.concatenate(
        [
            step_weight,
            jnp.zeros((share, LANES - 2 - heads), BF16),
            norm_first[:, None],
            norm_second[:, None],
        ],
        1,
    )
    spare = jnp.zeros((share, lead - mixer_cols - query_cols), BF16)
    weight_own = jnp.concatenate(
        [inner_weight.reshape(share, 2 * channels), state_weight, step_block, query_weight, spare, key_value_weight], 1
    )
    weight_mix = gather(jnp.concatenate([output_weight, mamba_weight], 0), "dp", 1)
    tokens_all, weight_in = entry_gather(tokens_in, weight_own, dp_size, group, 1)
    cot_mine, tokens_all, weight_in = lax.optimization_barrier((cotangent, tokens_all, weight_in))
    cot_all = gather(cot_mine, "tensor", 0)

    cosine, sine = angle_tables()
    key_head = (place * query_heads // (QUERY_HEADS // KEY_HEADS)).astype(jnp.int32).reshape(1)
    heads_map = (jnp.arange(channels)[None, :] // PM == jnp.arange(LANES)[:, None]).astype(BF16)
    conv_weight = jnp.concatenate(
        [conv_inner.reshape(KC + 1, channels), conv_state], 1
    ).astype(F32)
    conv_weight = jnp.pad(conv_weight, ((0, 8 - KC - 1), (0, 0)))
    heads_vec = jnp.pad(head_params, ((0, 5), (0, LANES - heads)))
    gate_row = gate_gain.astype(F32).reshape(1, channels)

    lin, first, gains = project(tokens_all, weight_in, mixer_cols // LANES - 1)
    gain_one, gain_two = gains[0:1], gains[1:2]
    query_block = mixer_cols // LANES
    ssm, mixed, square, states = mixer_forward(lin, segment_ids, conv_weight, heads_vec, heads_map, heads)
    attended = attend_forward(lin, query_block, lead, query_heads, key_head, segment_ids, cosine, sine)
    expand_own = jnp.moveaxis(expand_weight.reshape(share, 2, -1, HIDDEN_TILE), 1, 2).reshape(share, 2 * hidden)
    mix_in, inverse = gate_norm(square, ssm, lin, gate_row, attended, group, 4)
    second_all, middle, weight_expand, weight_shrink, hidden_lin = line_sum(
        mix_in, weight_mix, [tokens_in, gain_two], False, mix_finish,
        [jax.ShapeDtypeStruct((own_rows, model), F32)], group, model, 2, "mix_sum", dp_size,
        gathers=[(expand_own, True), (shrink_weight, False)],
    )
    act, grad_hidden = feed_forward(cot_all, hidden_lin, weight_shrink)
    lanes = jnp.concatenate(
        [
            (1.0 / norm_first.astype(F32))[:, None],
            (1.0 / norm_second.astype(F32))[:, None],
            jnp.zeros((share, LANES - 2), F32),
        ],
        1,
    )
    mix_all, grad_middle, ffn_part, ffn_sum, lanes = line_sum(
        grad_hidden, weight_expand, [cotangent, middle, gain_two], True, second_finish,
        [jax.ShapeDtypeStruct((own_rows, model), F32)], group, model, 3, "second_sum", dp_size,
        products=(second_all, cot_all, act, weight_shrink), gains=(expand_own, lanes, 1),
    )
    ffn_part, mix_all = lax.optimization_barrier((ffn_part, mix_all))
    ffn_out = scatter(ffn_part, "tensor", 0)

    grad_attended, grad_normed, cross = gate_back(mix_all, weight_mix, ssm, lin, gate_row, query_cols, group, 5)
    grad_lin, small, grad_mix_weight = mixer_backward(
        lin, segment_ids, conv_weight, heads_vec, heads_map, gate_row, grad_normed, inverse, cross,
        ssm, mixed, states, heads, lead, share, mix_all, mix_in,
    )
    grad_lin = attend_backward(
        lin, query_block, lead, query_heads, key_head, segment_ids, cosine, sine, grad_attended, grad_lin
    )
    grad_in = mat_tn(first, grad_lin).astype(BF16)
    grad_lin, ffn_out = lax.optimization_barrier((grad_lin, ffn_out))
    block_out = (middle + ffn_out.astype(F32)).astype(BF16)
    grad_tokens, in_sum, common, state, gain_sums = line_sum(
        grad_lin, weight_in, [tokens_in, grad_middle, gain_one], True, first_finish,
        [], group, model, 6, "first_sum", dp_size, spread=False,
        pieces=[grad_in, grad_mix_weight, small.astype(BF16)], gains=(weight_own, lanes, 0),
        ranges=((2 * channels, 2 * NS), (lead, pair_cols)),
        state_rows=(channels // LANES * 8, (channels + 2 * NS) // LANES * 8),
    )
    grads = unpack(
        in_sum, ffn_sum, common, state, gain_sums, heads, query_cols, mixer_cols, hidden, dp_size, group
    )
    return (block_out, grad_tokens, *grads)


def solution(mesh):
    return jax.shard_map(
        per_device,
        mesh=mesh,
        in_specs=(
            P(("dp", "tensor"), None),
            P("dp"),
            P(("dp", "tensor"), None),
            P("dp"),
            P("dp", "tensor"),
            P("dp", None),
            P("tensor", "dp"),
            P("dp", None, "tensor"),
            P("dp", None),
            P("dp", "tensor"),
            P(None, "tensor", None),
            P(),
            P(None, "tensor"),
            P("tensor", None),
            P("tensor", "dp"),
            P("dp"),
            P("dp", None, "tensor"),
            P("tensor", "dp"),
        ),
        out_specs=(
            P(("dp", "tensor"), None),
            P(("dp", "tensor"), None),
            P(("dp", "tensor")),
            P("dp", "tensor"),
            P(("dp", "tensor"), None),
            P("tensor", "dp"),
            P("dp", None, "tensor"),
            P(("dp", "tensor"), None),
            P("dp", "tensor"),
            P(None, "tensor", "dp"),
            P(None, ("dp", "tensor")),
            P(None, "tensor"),
            P("tensor", "dp"),
            P("tensor", "dp"),
            P(("dp", "tensor")),
            P("dp", None, "tensor"),
            P("tensor", "dp"),
        ),
        check_vma=False,
    )
```

```python
import functools
import math

import jax
import jax.numpy as jnp
from jax import lax
from jax.experimental import pallas as pl
from jax.experimental.pallas import tpu as pltpu
from jax.sharding import PartitionSpec as P

QUERY_HEADS = 8
KEY_HEADS = 2
HEAD_SIZE = 128
PM = 64
NS = 256
KC = 4
SEQ_LEN = 1024
DSSM = 3072
LANES = 128
CHUNK = 128
FAR = -1e30


EPS = 1e-05
THETA = 100000000000.0
HIGH = lax.Precision.HIGHEST
F32 = jnp.float32
BF16 = jnp.bfloat16


def mat(left_side, right_side):
    return jnp.dot(left_side, right_side, preferred_element_type=F32)


def mat_nt(left_side, right_side):
    return lax.dot_general(
        left_side, right_side, (((1,), (1,)), ((), ())), preferred_element_type=F32
    )


def mat_tn(left_side, right_side):
    return lax.dot_general(
        left_side, right_side, (((0,), (0,)), ((), ())), preferred_element_type=F32
    )


def iota(shape, dim):
    return lax.broadcasted_iota(jnp.int32, shape, dim)


def halves(value):
    high = value.astype(BF16)
    return high, (value - high.astype(F32)).astype(BF16)


def spread(value, heads_map):
    high, rest = halves(value)
    return mat(high, heads_map) + mat(rest, heads_map)


def gather_heads(value, heads_map):
    high, rest = halves(value)
    return mat_nt(high, heads_map) + mat_nt(rest, heads_map)


def sigmoid(value):
    return 0.5 + 0.5 * jnp.tanh(0.5 * value)


def softplus(value):
    return jnp.maximum(value, 0.0) + jnp.log(1.0 + jnp.exp(-jnp.abs(value)))


def conv_rows(inputs, before, seg, seg_before, weight):
    rows = inputs.shape[0]
    longer = jnp.concatenate([before, inputs], 0)
    seg_longer = jnp.concatenate([seg_before, seg], 0)
    result = weight[KC : KC + 1] + weight[KC - 1 : KC] * inputs
    moved_list = []
    for lag in range(1, KC):
        keep = seg_longer[8 - lag : 8 - lag + rows] == seg
        moved = jnp.where(keep, longer[8 - lag : 8 - lag + rows], 0.0)
        moved_list.append(moved)
        result = result + weight[KC - 1 - lag : KC - lag] * moved
    return result, moved_list


def chunk_decay(step_lin, heads_vec, heads, seg, seg_last_before):
    rows = step_lin.shape[0]
    head_lane = iota((1, LANES), 1) < heads
    shifted = step_lin + heads_vec[1:2]
    step = jnp.where(head_lane, softplus(shifted), 0.0)
    rate = jnp.exp(heads_vec[0:1])
    log_decay = -step * rate
    lower = (iota((rows, rows), 0) >= iota((rows, rows), 1)).astype(F32)
    running = jnp.dot(lower, log_decay, precision=HIGH, preferred_element_type=F32)
    last = running[rows - 1 : rows]
    seg_last = seg[rows - 1 : rows]
    into = jnp.where(seg == seg_last_before, jnp.exp(running), 0.0)
    out = jnp.where(seg == seg_last, jnp.exp(last - running), 0.0)
    across = jnp.where(seg_last == seg_last_before, jnp.exp(last), 0.0)
    return shifted, step, rate, log_decay, running, into, out, across


def two_heads(pair):
    front = iota(pair.shape, 1) < PM
    nothing = jnp.zeros_like(pair)
    return jnp.concatenate(
        [jnp.where(front, pair, nothing), jnp.where(front, nothing, pair)], 0
    )


def pair_decay(running, running_t, bias, index):
    parts = []
    for head in (2 * index, 2 * index + 1):
        gap = running[:, head : head + 1] - running_t[head : head + 1, :] + bias
        parts.append(jnp.exp(gap))
    return parts


def as_column(row):
    return jnp.broadcast_to(row, (8, row.shape[1])).T[:, 0:1]


def row_sums_as_row(values):
    return jnp.sum(values.T, 0, keepdims=True)


def chunk_bias(seg, seg_row):
    rows = seg.shape[0]
    allowed = (iota((rows, rows), 0) >= iota((rows, rows), 1)) & (seg == seg_row)
    return jnp.where(allowed, 0.0, FAR)


def mixer_forward_kernel(
    heads, lin_ref, seg_ref, segr_ref, conv_ref, hp_ref, map_ref,
    ssm_ref, mixed_ref, sums_ref, states_ref, state, tail, seg_tail,
):
    channels = heads * PM
    rows = lin_ref.shape[0]

    @pl.when(lax.rem(pl.program_id(0), SEQ_LEN // CHUNK) == 0)
    def _():
        state[...] = jnp.zeros_like(state)
        tail[...] = jnp.zeros_like(tail)
        seg_tail[...] = jnp.full_like(seg_tail, -1)

    heads_map = map_ref[...]
    seg = seg_ref[...]
    seg_before = seg_tail[...]
    inputs = lin_ref[:, channels : 2 * channels + 2 * NS]
    conv, _ = conv_rows(inputs, tail[...], seg, seg_before, conv_ref[...])
    mixed = (conv * sigmoid(conv)).astype(BF16)
    mixed_ref[...] = mixed
    tail[...] = inputs[rows - 8 :]
    seg_tail[...] = seg[rows - 8 :]

    step_lin = lin_ref[:, 2 * channels + 2 * NS :]
    _, step, _, _, running, into, out, across = chunk_decay(
        step_lin, hp_ref[...], heads, seg, seg_before[7:8]
    )
    inner = mixed[:, :channels].astype(F32)
    state_b = mixed[:, channels : channels + NS]
    state_c = mixed[:, channels + NS :]
    few = jnp.concatenate([across, hp_ref[2:3], jnp.zeros((6, LANES), F32)], 0)
    wide = spread(jnp.concatenate([step, into, out, few], 0), heads_map)
    stepped = (inner * wide[:rows]).astype(BF16)
    leaving = (stepped.astype(F32) * wide[2 * rows : 3 * rows]).astype(BF16)
    held = state[...]
    held_low = held.astype(BF16)
    states_ref[0] = held_low
    base = wide[rows : 2 * rows] * mat(state_c, held_low) + wide[3 * rows + 1 : 3 * rows + 2] * inner
    state[...] = wide[3 * rows : 3 * rows + 1] * held + mat_tn(state_b, leaving)

    gram = mat_nt(state_c, state_b)
    bias = chunk_bias(seg, segr_ref[...])
    running_t = running.T
    total = jnp.zeros((rows, LANES), F32)
    for index in range(heads // 2):
        cols = slice(index * LANES, (index + 1) * LANES)
        first, second = pair_decay(running, running_t, bias, index)
        mixing = jnp.concatenate([first * gram, second * gram], 1).astype(BF16)
        outcome = mat(mixing, two_heads(stepped[:, cols])) + base[:, cols]
        ssm_ref[:, cols] = outcome
        gate = lin_ref[:, cols]
        gated = outcome * gate * sigmoid(gate)
        total = total + gated * gated
    sums_ref[0] = row_sums_as_row(total)


def mixer_backward_kernel(
    heads, lin_ref, before_ref, seg_ref, segb_ref, segr_ref, conv_ref, hp_ref, map_ref, gain_ref,
    gn_ref, inv_ref, cross_ref, ssm_ref, mixed_ref, states_ref, mix_grad_ref, mix_in_ref,
    dlin_ref, small_ref, product_ref, dstate, dnext, seg_next, dconv_ref, dhp_ref, dgain_ref,
):
    channels = heads * PM
    rows = lin_ref.shape[0]
    chunks = SEQ_LEN // CHUNK
    chunk = pl.num_programs(0) - 1 - pl.program_id(0)
    place = lax.rem(chunk, chunks)

    @pl.when(pl.program_id(0) == 0)
    def _():
        dconv_ref[...] = jnp.zeros_like(dconv_ref)
        dhp_ref[...] = jnp.zeros_like(dhp_ref)
        dgain_ref[...] = jnp.zeros_like(dgain_ref)

    @pl.when(place == chunks - 1)
    def _():
        dstate[...] = jnp.zeros_like(dstate)
        dnext[...] = jnp.zeros_like(dnext)
        seg_next[...] = jnp.full_like(seg_next, -1)

    product_ref[...] = mat_tn(mix_grad_ref[...], mix_in_ref[...]).astype(BF16)

    heads_map = map_ref[...]
    seg = seg_ref[...]
    seg_before = jnp.where(place == 0, -1, segb_ref[...])

    gate = lin_ref[:, :channels]
    sig = sigmoid(gate)
    silu = gate * sig
    ssm = ssm_ref[...]
    gated = ssm * silu
    grad_normed = gn_ref[...]
    inverse = as_column(inv_ref[0])
    dgain_ref[0:1] += jnp.sum(gated * inverse * grad_normed, 0, keepdims=True)
    cube = inverse * inverse * inverse * (as_column(cross_ref[0]) * (1.0 / DSSM))
    grad_gated = inverse * (grad_normed * gain_ref[...]) - gated * cube
    grad_out = grad_gated * silu
    grad_gate = grad_gated * ssm * (sig * (1.0 + gate * (1.0 - sig)))
    dlin_ref[:, :channels] = grad_gate.astype(BF16)
    grad_low = grad_out.astype(BF16)

    step_lin = lin_ref[:, 2 * channels + 2 * NS :]
    shifted, step, rate, log_decay, running, into, out, across = chunk_decay(
        step_lin, hp_ref[...], heads, seg, seg_before[7:8]
    )
    mixed = mixed_ref[...]
    inner = mixed[:, :channels].astype(F32)
    state_b = mixed[:, channels : channels + NS]
    state_c = mixed[:, channels + NS :]
    few = jnp.concatenate([across, hp_ref[2:3], jnp.zeros((6, LANES), F32)], 0)
    wide = spread(jnp.concatenate([step, into, out, few], 0), heads_map)
    step_wide = wide[:rows]
    out_wide = wide[2 * rows : 3 * rows]
    skip_wide = wide[3 * rows + 1 : 3 * rows + 2]
    stepped = (inner * step_wide).astype(BF16)
    stepped_wide = stepped.astype(F32)
    leaving = (stepped_wide * out_wide).astype(BF16)

    held = states_ref[0]
    grad_state = dstate[...]
    grad_state_low = grad_state.astype(BF16)
    grad_leaving = mat(state_b, grad_state_low)
    grad_b = mat_nt(leaving, grad_state_low)
    entering = wide[rows : 2 * rows] * grad_out
    entering_low = entering.astype(BF16)
    grad_c = mat_nt(entering_low, held)
    carried = mat(state_c, held)
    dstate[...] = wide[3 * rows : 3 * rows + 1] * grad_state + mat_tn(state_c, entering_low)
    grad_across = jnp.sum(grad_state * held.astype(F32), 0, keepdims=True)

    gram = mat_nt(state_c, state_b)
    bias = chunk_bias(seg, segr_ref[...])
    running_t = running.T
    head_lane = iota((1, LANES), 1)
    head_row = iota((LANES, 1), 0)
    grad_gram = jnp.zeros((rows, rows), F32)
    row_sums = jnp.zeros((rows, LANES), F32)
    column_sums = jnp.zeros((LANES, rows), F32)
    grad_stepped = []
    for index in range(heads // 2):
        cols = slice(index * LANES, (index + 1) * LANES)
        grads = mat_nt(grad_low[:, cols], two_heads(stepped[:, cols]))
        mixings = []
        for side, decay in enumerate(pair_decay(running, running_t, bias, index)):
            part = grads[:, side * rows : (side + 1) * rows] * decay
            grad_gram = grad_gram + part
            part = part * gram
            head = 2 * index + side
            row_sums = jnp.where(head_lane == head, jnp.sum(part, 1, keepdims=True), row_sums)
            column_sums = jnp.where(head_row == head, jnp.sum(part, 0, keepdims=True), column_sums)
            mixings.append((decay * gram).astype(BF16))
        both = mat_tn(jnp.concatenate(mixings, 1), grad_low[:, cols])
        front = iota((rows, LANES), 1) < PM
        grad_stepped.append(jnp.where(front, both[:rows], both[rows:]))
    grad_gram_low = grad_gram.astype(BF16)
    grad_c = grad_c + mat(grad_gram_low, state_b)
    grad_b = grad_b + mat_tn(grad_gram_low, state_c)
    grad_stepped = jnp.concatenate(grad_stepped, 1) + out_wide * grad_leaving
    grad_inner = grad_stepped * step_wide + skip_wide * grad_out

    few = jnp.concatenate([grad_across, jnp.zeros((7, channels), F32)], 0)
    sums = gather_heads(
        jnp.concatenate(
            [stepped_wide * grad_leaving, entering * carried, grad_stepped * inner, grad_out * inner, few], 0
        ),
        heads_map,
    )
    leave = sums[:rows] * out
    grad_running = row_sums - column_sums.T + sums[rows : 2 * rows] - leave
    grad_last = jnp.sum(leave, 0, keepdims=True) + sums[4 * rows : 4 * rows + 1] * across
    grad_running = grad_running + jnp.where(iota((rows, 1), 0) == rows - 1, grad_last, 0.0)
    upper = (iota((rows, rows), 0) <= iota((rows, rows), 1)).astype(F32)
    grad_log = jnp.dot(upper, grad_running, precision=HIGH, preferred_element_type=F32)
    grad_step = sums[2 * rows : 3 * rows] - grad_log * rate
    grad_shifted = jnp.where(head_lane < heads, grad_step * sigmoid(shifted), 0.0)
    first_spare = 2 * channels + 2 * NS + LANES
    dlin_ref[:, first_spare - LANES : first_spare] = grad_shifted.astype(BF16)
    dlin_ref[:, first_spare:] = jnp.zeros((rows, dlin_ref.shape[1] - first_spare), BF16)
    dhp_ref[0:1] += jnp.sum(grad_log * log_decay, 0, keepdims=True)
    dhp_ref[1:2] += jnp.sum(grad_shifted, 0, keepdims=True)
    dhp_ref[2:3] += jnp.sum(sums[3 * rows : 4 * rows], 0, keepdims=True)

    grad_mixed = jnp.concatenate([grad_inner, grad_b, grad_c], 1)
    weight = conv_ref[...]
    inputs = lin_ref[:, channels : 2 * channels + 2 * NS]
    before = before_ref[:, channels : 2 * channels + 2 * NS]
    conv, moved_list = conv_rows(inputs, before, seg, seg_before, weight)
    sig = sigmoid(conv)
    grad_conv = grad_mixed * (sig * (1.0 + conv * (1.0 - sig)))
    dconv_ref[KC : KC + 1] += jnp.sum(grad_conv, 0, keepdims=True)
    dconv_ref[KC - 1 : KC] += jnp.sum(grad_conv * inputs, 0, keepdims=True)
    longer = jnp.concatenate([grad_conv, dnext[...]], 0)
    seg_longer = jnp.concatenate([seg, seg_next[...]], 0)
    grad_inputs = weight[KC - 1 : KC] * grad_conv
    for lag in range(1, KC):
        tap = slice(KC - 1 - lag, KC - lag)
        dconv_ref[tap] += jnp.sum(grad_conv * moved_list[lag - 1], 0, keepdims=True)
        keep = seg_longer[lag : lag + rows] == seg
        grad_inputs = grad_inputs + weight[tap] * jnp.where(keep, longer[lag : lag + rows], 0.0)
    dlin_ref[:, channels : 2 * channels + 2 * NS] = grad_inputs.astype(BF16)
    dnext[...] = grad_conv[:8]
    seg_next[...] = seg[:8]

    @pl.when(pl.program_id(0) == pl.num_programs(0) - 1)
    def _():
        small_ref[...] = jnp.zeros_like(small_ref)
        row = 0
        state_first = list(range(channels, dconv_ref.shape[1], LANES)) + list(range(0, channels, LANES))
        for array, columns in ((dconv_ref, state_first), (dhp_ref, [0]), (dgain_ref, range(0, channels, LANES))):
            for first in columns:
                small_ref[row : row + 8, :] = array[:, first : first + LANES]
                row += 8


def whole_block(array):
    return pl.BlockSpec(array.shape, lambda *_: (0,) * array.ndim)


def mixer_forward(lin, seg, conv_weight, heads_vec, heads_map, heads):
    total = lin.shape[0]
    channels = heads * PM
    width = 2 * channels + 2 * NS + LANES
    mixed_width = channels + 2 * NS
    steps = total // CHUNK
    by_rows = lambda cols: pl.BlockSpec((CHUNK, cols), lambda c: (c, 0))
    return pl.pallas_call(
        functools.partial(mixer_forward_kernel, heads),
        grid=(steps,),
        in_specs=[
            by_rows(width),
            by_rows(1),
            pl.BlockSpec((1, CHUNK), lambda c: (0, c)),
            whole_block(conv_weight),
            whole_block(heads_vec),
            whole_block(heads_map),
        ],
        out_specs=[
            by_rows(channels),
            by_rows(mixed_width),
            pl.BlockSpec((1, 1, CHUNK), lambda c: (c, 0, 0)),
            pl.BlockSpec((1, NS, channels), lambda c: (c, 0, 0)),
        ],
        out_shape=[
            jax.ShapeDtypeStruct((total, channels), F32),
            jax.ShapeDtypeStruct((total, mixed_width), BF16),
            jax.ShapeDtypeStruct((steps, 1, CHUNK), F32),
            jax.ShapeDtypeStruct((steps, NS, channels), BF16),
        ],
        scratch_shapes=[
            pltpu.VMEM((NS, channels), F32),
            pltpu.VMEM((8, mixed_width), F32),
            pltpu.VMEM((8, 1), jnp.int32),
        ],
        compiler_params=pltpu.CompilerParams(vmem_limit_bytes=48 << 20),
        name="mixer_forward",
    )(lin, seg.reshape(total, 1), seg.reshape(1, total), conv_weight, heads_vec, heads_map)


def mixer_backward(
    lin, seg, conv_weight, heads_vec, heads_map, gain, grad_normed, inverse, cross, ssm, mixed, states, heads, lead, share,
    grad_mix, mix_in,
):
    total = lin.shape[0]
    channels = heads * PM
    width = 2 * channels + 2 * NS + LANES
    mixed_width = channels + 2 * NS
    steps = total // CHUNK
    by_rows = lambda cols: pl.BlockSpec((CHUNK, cols), lambda c: (steps - 1 - c, 0))
    ahead = lambda cols: pl.BlockSpec(
        (8, cols), lambda c: (jnp.maximum((steps - 1 - c) * (CHUNK // 8) - 1, 0), 0)
    )
    seg_column = seg.reshape(total, 1)
    return pl.pallas_call(
        functools.partial(mixer_backward_kernel, heads),
        grid=(steps,),
        in_specs=[
            by_rows(width),
            ahead(width),
            by_rows(1),
            ahead(1),
            pl.BlockSpec((1, CHUNK), lambda c: (0, steps - 1 - c)),
            whole_block(conv_weight),
            whole_block(heads_vec),
            whole_block(heads_map),
            whole_block(gain),
            by_rows(channels),
            pl.BlockSpec((1, 1, CHUNK), lambda c: (steps - 1 - c, 0, 0)),
            pl.BlockSpec((1, 1, CHUNK), lambda c: (steps - 1 - c, 0, 0)),
            by_rows(channels),
            by_rows(mixed_width),
            pl.BlockSpec((1, NS, channels), lambda c: (steps - 1 - c, 0, 0)),
            pl.BlockSpec((total, grad_mix.shape[1] // steps), lambda c: (0, c)),
            whole_block(mix_in),
        ],
        out_specs=[
            by_rows(lead),
            pl.BlockSpec((share, LANES), lambda c: (0, 0)),
            pl.BlockSpec((grad_mix.shape[1] // steps, mix_in.shape[1]), lambda c: (c, 0)),
        ],
        out_shape=[
            jax.ShapeDtypeStruct((total, lin.shape[1]), BF16),
            jax.ShapeDtypeStruct((share, LANES), F32),
            jax.ShapeDtypeStruct((grad_mix.shape[1], mix_in.shape[1]), BF16),
        ],
        scratch_shapes=[
            pltpu.VMEM((NS, channels), F32),
            pltpu.VMEM((8, mixed_width), F32),
            pltpu.VMEM((8, 1), jnp.int32),
            pltpu.VMEM((8, mixed_width), F32),
            pltpu.VMEM((8, LANES), F32),
            pltpu.VMEM((8, channels), F32),
        ],
        compiler_params=pltpu.CompilerParams(vmem_limit_bytes=48 << 20),
        name="mixer_backward",
    )(
        lin, lin, seg_column, seg_column, seg.reshape(1, total), conv_weight, heads_vec, heads_map, gain,
        grad_normed, inverse, cross, ssm, mixed, states, grad_mix, mix_in,
    )


ROWS = 256


def turn(values, cosine, sine):
    return values * cosine + pltpu.roll(values, HEAD_SIZE // 2, 1) * sine


def attend_weights(query, keys, seg, seg_row, start):
    stop = start + ROWS
    scores = mat_nt(query, keys[:stop]) * (1.0 / math.sqrt(HEAD_SIZE))
    allowed = (iota((ROWS, stop), 0) + start >= iota((ROWS, stop), 1)) & (
        seg[start:stop] == seg_row[:, :stop]
    )
    scores = jnp.where(allowed, scores, FAR)
    shifted = jnp.exp(scores - jnp.max(scores, 1, keepdims=True))
    return shifted * (1.0 / jnp.sum(shifted, 1, keepdims=True))


def attend_forward_kernel(head_ref, q_ref, k_ref, v_ref, seg_ref, segr_ref, cos_ref, sin_ref, out_ref):
    cosine, sine = cos_ref[...], sin_ref[...]
    seg, seg_row = seg_ref[...], segr_ref[...]
    query = turn(q_ref[...], cosine, sine).astype(BF16)
    keys = turn(k_ref[...], cosine, sine).astype(BF16)
    values = v_ref[...].astype(BF16)
    for start in range(0, SEQ_LEN, ROWS):
        weights = attend_weights(query[start : start + ROWS], keys, seg, seg_row, start)
        out_ref[start : start + ROWS, :] = mat(
            weights.astype(BF16), values[: start + ROWS]
        ).astype(BF16)


def attend_backward_kernel(
    first_block, lead, head_ref, q_ref, k_ref, v_ref, seg_ref, segr_ref, cos_ref, sin_ref, do_ref, old_ref,
    dlin_ref, dkeys, dvalues, dq_ref, dkv_ref, sem,
):
    step = pl.program_id(1)
    here = pl.ds(pl.program_id(0) * SEQ_LEN, SEQ_LEN)
    cosine, sine = cos_ref[...], sin_ref[...]
    seg, seg_row = seg_ref[...], segr_ref[...]
    scale = 1.0 / math.sqrt(HEAD_SIZE)

    @pl.when(step == 0)
    def _():
        dkeys[...] = jnp.zeros_like(dkeys)
        dvalues[...] = jnp.zeros_like(dvalues)

    query = turn(q_ref[...], cosine, sine).astype(BF16)
    keys = turn(k_ref[...], cosine, sine).astype(BF16)
    values = v_ref[...].astype(BF16)
    for start in range(0, SEQ_LEN, ROWS):
        stop = start + ROWS
        rows = slice(start, stop)
        weights = attend_weights(query[rows], keys, seg, seg_row, start)
        grad_out = do_ref[rows, :]
        dvalues[:stop] += mat_tn(weights.astype(BF16), grad_out)
        grads = mat_nt(grad_out, values[:stop])
        inner = jnp.sum(grads * weights, 1, keepdims=True)
        scores = (weights * (grads - inner)).astype(BF16)
        dq = mat(scores, keys[:stop]) * scale
        dq_ref[step, rows, :] = turn(dq, cosine[rows], -sine[rows]).astype(BF16)
        dkeys[:stop] += mat_tn(scores, query[rows]) * scale

    def out_copy(head):
        place = pl.ds(pl.multiple_of((first_block + head) * HEAD_SIZE, HEAD_SIZE), HEAD_SIZE)
        return pltpu.make_async_copy(dq_ref.at[head], dlin_ref.at[here, place], sem.at[head])

    out_copy(step).start()

    @pl.when(step == pl.num_programs(1) - 1)
    def _():
        mine = head_ref[0]
        grad_keys = turn(dkeys[...], cosine, -sine)
        grad_values = dvalues[...]
        for head in range(KEY_HEADS):
            same = mine == head
            cols = slice(head * HEAD_SIZE, (head + 1) * HEAD_SIZE)
            dkv_ref[:, cols] = jnp.where(same, grad_keys, 0.0).astype(BF16)
            cols = slice((KEY_HEADS + head) * HEAD_SIZE, (KEY_HEADS + head + 1) * HEAD_SIZE)
            dkv_ref[:, cols] = jnp.where(same, grad_values, 0.0).astype(BF16)
        both = pltpu.make_async_copy(dkv_ref, dlin_ref.at[here, pl.ds(lead, dkv_ref.shape[1])], sem.at[dq_ref.shape[0]])
        both.start()
        for head in range(dq_ref.shape[0]):
            out_copy(head).wait()
        both.wait()


def attend_specs(first_block, lead):
    column = lambda first: pl.BlockSpec((SEQ_LEN, HEAD_SIZE), first)
    pair_block = lead // HEAD_SIZE
    return [
        column(lambda b, h, s: (b, first_block + h)),
        column(lambda b, h, s: (b, pair_block + s[0])),
        column(lambda b, h, s: (b, pair_block + KEY_HEADS + s[0])),
        pl.BlockSpec((SEQ_LEN, 1), lambda b, h, s: (b, 0)),
        pl.BlockSpec((1, SEQ_LEN), lambda b, h, s: (0, b)),
        pl.BlockSpec((SEQ_LEN, HEAD_SIZE), lambda b, h, s: (0, 0)),
        pl.BlockSpec((SEQ_LEN, HEAD_SIZE), lambda b, h, s: (0, 0)),
    ]


def attend_forward(lin, first_block, lead, heads, key_head, seg, cosine, sine):
    total = lin.shape[0]
    return pl.pallas_call(
        attend_forward_kernel,
        grid_spec=pltpu.PrefetchScalarGridSpec(
            num_scalar_prefetch=1,
            grid=(total // SEQ_LEN, heads),
            in_specs=attend_specs(first_block, lead),
            out_specs=pl.BlockSpec((SEQ_LEN, HEAD_SIZE), lambda b, h, s: (b, h)),
        ),
        out_shape=jax.ShapeDtypeStruct((total, heads * HEAD_SIZE), BF16),
        compiler_params=pltpu.CompilerParams(vmem_limit_bytes=48 << 20),
        name="attend_forward",
    )(key_head, lin, lin, lin, seg.reshape(total, 1), seg.reshape(1, total), cosine, sine)


def attend_backward(lin, first_block, lead, heads, key_head, seg, cosine, sine, grad_out, grad_lin):
    total = lin.shape[0]
    return pl.pallas_call(
        functools.partial(attend_backward_kernel, first_block, lead),
        grid_spec=pltpu.PrefetchScalarGridSpec(
            num_scalar_prefetch=1,
            grid=(total // SEQ_LEN, heads),
            in_specs=attend_specs(first_block, lead)
            + [
                pl.BlockSpec((SEQ_LEN, HEAD_SIZE), lambda b, h, s: (b, h)),
                pl.BlockSpec(memory_space=pl.ANY),
            ],
            out_specs=pl.BlockSpec(memory_space=pl.ANY),
            scratch_shapes=[
                pltpu.VMEM((SEQ_LEN, HEAD_SIZE), F32),
                pltpu.VMEM((SEQ_LEN, HEAD_SIZE), F32),
                pltpu.VMEM((heads, SEQ_LEN, HEAD_SIZE), BF16),
                pltpu.VMEM((SEQ_LEN, 2 * KEY_HEADS * HEAD_SIZE), BF16),
                pltpu.SemaphoreType.DMA((heads + 1,)),
            ],
        ),
        out_shape=jax.ShapeDtypeStruct(grad_lin.shape, BF16),
        input_output_aliases={9: 0},
        compiler_params=pltpu.CompilerParams(vmem_limit_bytes=48 << 20),
        name="attend_backward",
    )(key_head, lin, lin, lin, seg.reshape(total, 1), seg.reshape(1, total), cosine, sine, grad_out, grad_lin)


def rms_rows(values):
    return lax.rsqrt(jnp.mean(values * values, -1, keepdims=True) + EPS)


def rms_back(values, inverse, gain, grad):
    scaled = grad * gain
    inner = jnp.mean(scaled * values, -1, keepdims=True)
    return inverse * scaled - values * (inverse * inverse * inverse * inner)


def angle_tables():
    half = HEAD_SIZE // 2
    frequency = jnp.exp(jnp.arange(half).astype(F32) * (-2.0 * math.log(THETA) / HEAD_SIZE))
    turned = jnp.arange(SEQ_LEN).astype(F32)[:, None] * frequency[None, :]
    cosine, sine = jnp.cos(turned), jnp.sin(turned)
    return jnp.concatenate([cosine, cosine], 1), jnp.concatenate([-sine, sine], 1)


MESH = pl.DeviceIdType.MESH
LINE_CHUNKS = 4


CORE, ACROSS, ALONG, CORNER = 1, 2, 4, 6
PLANE_PARTS = 4


def partner(index, bits):
    for bit in (CORE, ACROSS, ALONG):
        if bits & bit:
            index = index + jnp.where(lax.rem(index // bit, 2) == 0, bit, -bit)
    return index


def greet(place, group, owner, plane, everyone=False):
    barrier = pltpu.get_barrier_semaphore()
    if everyone:
        for hop in range(1, group):
            pl.semaphore_signal(
                barrier, inc=1, device_id={"tensor": lax.rem(place + hop, group)}, device_id_type=MESH
            )
        count = group - 1
    else:

        @pl.when(place > 0)
        def _():
            pl.semaphore_signal(barrier, inc=1, device_id={"tensor": place - 1}, device_id_type=MESH)

        @pl.when(place < group - 1)
        def _():
            pl.semaphore_signal(barrier, inc=1, device_id={"tensor": place + 1}, device_id_type=MESH)

        count = jnp.where((place > 0) & (place < group - 1), 2, 1)
    if plane:
        for bits in (CORE, ACROSS, ALONG):
            pl.semaphore_signal(barrier, inc=1, device_id={"dp": partner(owner, bits)}, device_id_type=MESH)
        count = count + 3
    pl.semaphore_wait(barrier, count)


def plane_gather_steps(pieces, local_sem, send_sem, recv_sem):
    owner = lax.axis_index("dp")
    parts = PLANE_PARTS
    half = parts // 2

    def copies(slot, origin, to, part, own=False):
        result = []
        for index, (own_ref, full_ref, by_rows) in enumerate(pieces):
            share, cols = own_ref.shape
            rows = share // parts
            if by_rows:
                block = full_ref.at[pl.ds(origin * share + part * rows, rows)]
            else:
                block = full_ref.at[pl.ds(part * rows, rows), pl.ds(pl.multiple_of(origin * cols, cols), cols)]
            result.append(
                pltpu.make_async_remote_copy(
                    own_ref.at[pl.ds(part * rows, rows)] if own else block,
                    block,
                    send_sem.at[index, slot, part],
                    recv_sem.at[index, slot, part],
                    device_id={"dp": partner(owner, to)},
                    device_id_type=MESH,
                )
            )
        return result

    def start(*args):
        for item in copies(*args):
            item.start()

    def arrive(*args):
        for item in copies(*args):
            item.wait_recv()

    def keeps():
        result = []
        for index, (own_ref, full_ref, by_rows) in enumerate(pieces):
            share, cols = own_ref.shape
            if by_rows:
                block = full_ref.at[pl.ds(owner * share, share)]
            else:
                block = full_ref.at[:, pl.ds(pl.multiple_of(owner * cols, cols), cols)]
            result.append(pltpu.make_async_copy(own_ref, block, local_sem.at[index]))
        return result

    def begin():
        for part in range(parts):
            start(1, owner, ACROSS, part, True)
            start(2, owner, ALONG, (part + half) % parts, True)
            start(0, owner, CORE, part, True)
        for item in keeps():
            item.start()

    def neighbours(part):
        arrive(1, owner, ACROSS, part, True)

        @pl.when(part < half)
        def _():
            start(3, partner(owner, ACROSS), ALONG, part)

        start(4, partner(owner, ACROSS), CORE, part)
        other = (part + half) % parts
        arrive(2, owner, ALONG, other, True)

        @pl.when(part < half)
        def _():
            start(3, partner(owner, ALONG), ACROSS, other)

        start(5, partner(owner, ALONG), CORE, other)

    def corner(step):
        for part in (step, step + half):
            arrive(3, partner(owner, CORNER), ALONG, part)
            start(6, partner(owner, CORNER), CORE, part)

    def end():
        for part in range(parts):
            for slot in (0, 4, 5, 6):
                arrive(slot, owner, CORE, part)
            for slot in range(7):
                for item in copies(slot, owner, CORE, part):
                    item.wait_send()
        for item in keeps():
            item.wait()

    return begin, neighbours, corner, end


def plane_gather_scratch(count):
    return [
        pltpu.SemaphoreType.DMA((count,)),
        pltpu.SemaphoreType.DMA((count, 7, PLANE_PARTS)),
        pltpu.SemaphoreType.DMA((count, 7, PLANE_PARTS)),
    ]


def plane_gather_plain(array, by_rows):
    return gather(array, "dp", 0 if by_rows else 1)


def entry_gather_kernel(
    group, parts, own_ref, weight_ref, out_ref, full_ref,
    local_sem, send_sem, recv_sem, keep_sem, plane_send, plane_recv,
):
    place = lax.axis_index("tensor")
    rows = own_ref.shape[0] // parts
    greet(place, group, lax.axis_index("dp"), True)

    def copy(side, source, part, own=False):
        block = out_ref.at[source, pl.ds(part * rows, rows)]
        return pltpu.make_async_remote_copy(
            own_ref.at[pl.ds(part * rows, rows)] if own else block,
            block,
            send_sem.at[side, source, part],
            recv_sem.at[side, source, part],
            device_id={"tensor": place + 1 - 2 * side},
            device_id_type=MESH,
        )

    begin, neighbours, corner, end = plane_gather_steps(
        [(weight_ref, full_ref, True)], keep_sem, plane_send, plane_recv
    )
    more = (place < group - 1, place > 0)
    for part in range(parts):
        for side in (0, 1):

            @pl.when(more[side])
            def _():
                copy(side, place, part, True).start()

    begin()
    keep = pltpu.make_async_copy(own_ref, out_ref.at[place], local_sem)
    keep.start()
    plane_steps = [functools.partial(neighbours, part) for part in range(PLANE_PARTS)] + [
        functools.partial(corner, step) for step in range(PLANE_PARTS // 2)
    ]
    line_steps = (group - 1) * parts
    done = 0
    for hop in range(1, group):
        for part in range(parts):
            for side in (0, 1):
                source = place - hop if side == 0 else place + hop

                @pl.when((source >= 0) & (source < group))
                def _():
                    copy(side, source, part).wait_recv()

                    @pl.when(more[side])
                    def _():
                        copy(side, source, part).start()

            index = (hop - 1) * parts + part + 1
            while done < len(plane_steps) * index // line_steps:
                plane_steps[done]()
                done += 1

    end()
    keep.wait()
    for hop in range(group):
        for part in range(parts):
            for side in (0, 1):
                source = place - hop if side == 0 else place + hop

                @pl.when((source >= 0) & (source < group) & more[side])
                def _():
                    copy(side, source, part, hop == 0).wait_send()


def line_gather_kernel(group, parts, own_ref, out_ref, local_sem, send_sem, recv_sem):
    place = lax.axis_index("tensor")
    rows = own_ref.shape[0] // parts
    greet(place, group, None, False)

    def copy(side, source, part, own=False):
        block = out_ref.at[source, pl.ds(part * rows, rows)]
        return pltpu.make_async_remote_copy(
            own_ref.at[pl.ds(part * rows, rows)] if own else block,
            block,
            send_sem.at[side, source, part],
            recv_sem.at[side, source, part],
            device_id={"tensor": place + 1 - 2 * side},
            device_id_type=MESH,
        )

    keep = pltpu.make_async_copy(own_ref, out_ref.at[place], local_sem)
    keep.start()
    more = (place < group - 1, place > 0)
    for part in range(parts):
        for side in (0, 1):

            @pl.when(more[side])
            def _():
                copy(side, place, part, True).start()

    for hop in range(1, group):
        for part in range(parts):
            for side in (0, 1):
                source = place - hop if side == 0 else place + hop

                @pl.when((source >= 0) & (source < group))
                def _():
                    copy(side, source, part).wait_recv()

                    @pl.when(more[side])
                    def _():
                        copy(side, source, part).start()

    keep.wait()
    for hop in range(group):
        for part in range(parts):
            for side in (0, 1):
                source = place - hop if side == 0 else place + hop

                @pl.when((source >= 0) & (source < group) & more[side])
                def _():
                    copy(side, source, part, hop == 0).wait_send()


def entry_gather(own, weight, dp_size, group, collective_id):
    rows, cols = own.shape
    parts = 2
    anywhere = pl.BlockSpec(memory_space=pl.ANY)
    line_sems = pltpu.SemaphoreType.DMA((2, group, parts))
    if dp_size != 8:
        all_rows = pl.pallas_call(
            functools.partial(line_gather_kernel, group, parts),
            in_specs=[anywhere],
            out_specs=anywhere,
            out_shape=jax.ShapeDtypeStruct((group, rows, cols), own.dtype),
            scratch_shapes=[pltpu.SemaphoreType.DMA, line_sems, line_sems],
            compiler_params=pltpu.CompilerParams(collective_id=collective_id, has_side_effects=True),
            name="line_gather",
        )(own)
        return all_rows.reshape(group * rows, cols), plane_gather_plain(weight, True)
    all_rows, full = pl.pallas_call(
        functools.partial(entry_gather_kernel, group, parts),
        in_specs=[anywhere] * 2,
        out_specs=[anywhere] * 2,
        out_shape=[
            jax.ShapeDtypeStruct((group, rows, cols), own.dtype),
            jax.ShapeDtypeStruct((dp_size * weight.shape[0], weight.shape[1]), BF16),
        ],
        scratch_shapes=[pltpu.SemaphoreType.DMA, line_sems, line_sems] + plane_gather_scratch(1),
        compiler_params=pltpu.CompilerParams(collective_id=collective_id, has_side_effects=True),
        name="entry_gather",
    )(own, weight)
    return all_rows.reshape(group * rows, cols), full


def plane_scatter_steps(piece_refs, out_ref, got, staged, near_x, near_y, last, sems):
    owner = lax.axis_index("dp")
    share, width = out_ref.shape
    parts = LINE_CHUNKS
    half = share // 2
    rows = half // parts
    targets = (0, ACROSS, CORNER, ALONG)
    core_send, core_recv, stage_sem, x_send, x_recv, y_send, y_recv, last_send, last_recv = sems

    def block(piece_ref, target, side, part):
        first = 0 if piece_ref.shape[0] == share else target * share
        return piece_ref.at[pl.ds(first + side * half + part * rows, rows)]

    def whole_core(part):
        return pltpu.make_async_remote_copy(
            got.at[part], got.at[part], core_send.at[part], core_recv.at[part],
            device_id={"dp": partner(owner, CORE)}, device_id_type=MESH,
        )

    def to_x(part):
        return pltpu.make_async_remote_copy(
            got.at[part, 0, pl.ds(1, 2)], near_x.at[part], x_send.at[part], x_recv.at[part],
            device_id={"dp": partner(owner, ACROSS)}, device_id_type=MESH,
        )

    def to_y(part):
        return pltpu.make_async_remote_copy(
            got.at[part, 1, pl.ds(2, 2)], near_y.at[part], y_send.at[part], y_recv.at[part],
            device_id={"dp": partner(owner, ALONG)}, device_id_type=MESH,
        )

    def on_to_y(part):
        return pltpu.make_async_remote_copy(
            near_x.at[part, 1], last.at[part, 0], last_send.at[0, part], last_recv.at[0, part],
            device_id={"dp": partner(owner, ALONG)}, device_id_type=MESH,
        )

    def on_to_x(part):
        return pltpu.make_async_remote_copy(
            near_y.at[part, 0], last.at[part, 1], last_send.at[1, part], last_recv.at[1, part],
            device_id={"dp": partner(owner, ACROSS)}, device_id_type=MESH,
        )

    def begin():
        def send(part, carry):
            for side in (0, 1):
                for index, bits in enumerate(targets):
                    first = 0
                    for piece_ref in piece_refs:
                        cols = pl.ds(first, piece_ref.shape[1])
                        first += piece_ref.shape[1]
                        pltpu.make_async_remote_copy(
                            block(piece_ref, partner(owner, bits | CORE), side, part),
                            got.at[part, side, index, :, cols],
                            core_send.at[part],
                            core_recv.at[part],
                            device_id={"dp": partner(owner, CORE)},
                            device_id_type=MESH,
                        ).start()
            return carry

        lax.fori_loop(0, parts, send, 0)
        stage(0)

    def stage(part):
        for side in (0, 1):
            for index, bits in enumerate(targets):
                first = 0
                for piece_ref in piece_refs:
                    cols = pl.ds(first, piece_ref.shape[1])
                    first += piece_ref.shape[1]
                    pltpu.make_async_copy(
                        block(piece_ref, partner(owner, bits), side, part), staged.at[side, index, :, cols], stage_sem
                    ).start()

    def add_core(part):
        whole_core(part).wait_recv()
        pltpu.make_async_copy(staged, staged, stage_sem).wait()

        def add(step, carry):
            side, index = step // 4, lax.rem(step, 4)
            total = got[part, side, index].astype(F32) + staged[side, index].astype(F32)
            got[part, side, index] = total.astype(BF16)
            return carry

        lax.fori_loop(0, 8, add, 0)
        to_x(part).start()
        to_y(part).start()

        @pl.when(part + 1 < parts)
        def _():
            stage(part + 1)

    def add_near(part):
        to_x(part).wait_recv()
        near_x[part, 1] = (near_x[part, 1].astype(F32) + got[part, 0, 3].astype(F32)).astype(BF16)
        on_to_y(part).start()
        to_y(part).wait_recv()
        near_y[part, 0] = (near_y[part, 0].astype(F32) + got[part, 1, 1].astype(F32)).astype(BF16)
        on_to_x(part).start()

    def add_last(part):
        for side, near, step in ((0, near_x.at[part, 0], on_to_y), (1, near_y.at[part, 1], on_to_x)):
            step(part).wait_recv()
            total = got[part, side, 0].astype(F32) + near[...].astype(F32)
            out_ref[pl.ds(side * half + part * rows, rows), :] = total + last[part, side].astype(F32)

    def end(part):
        whole_core(part).wait_send()
        to_x(part).wait_send()
        to_y(part).wait_send()
        on_to_y(part).wait_send()
        on_to_x(part).wait_send()

    return begin, add_core, add_near, add_last, end


def plane_scatter_scratch(share, width):
    rows = share // 2 // LINE_CHUNKS
    by_part = pltpu.SemaphoreType.DMA((LINE_CHUNKS,))
    by_side = pltpu.SemaphoreType.DMA((2, LINE_CHUNKS))
    return [
        pltpu.VMEM((LINE_CHUNKS, 2, 4, rows, width), BF16),
        pltpu.VMEM((2, 4, rows, width), BF16),
        pltpu.VMEM((LINE_CHUNKS, 2, rows, width), BF16),
        pltpu.VMEM((LINE_CHUNKS, 2, rows, width), BF16),
        pltpu.VMEM((LINE_CHUNKS, 2, rows, width), BF16),
        by_part, by_part, pltpu.SemaphoreType.DMA, by_part, by_part, by_part, by_part, by_side, by_side,
    ]


def gain_lanes(lanes, weight, summed, index):
    own = jnp.sum(weight.astype(F32) * summed, 1, keepdims=True)
    return jnp.where(iota(lanes.shape, 1) == index, own * lanes, lanes)


def common_sum(group, place, ranges, state_rows, piece_out, make_lanes, refs):
    common_ref, state_ref, gains_ref, outbox, inbox, send_sem, recv_sem = refs
    rows, width = common_ref.shape
    start, stop = state_rows

    def copy(hop):
        peer = lax.rem(place + hop, group)
        return peer, pltpu.make_async_remote_copy(
            outbox.at[pl.ds(peer * rows, rows)], inbox.at[hop - 1], send_sem.at[hop - 1], recv_sem.at[hop - 1],
            device_id={"tensor": peer}, device_id_type=MESH,
        )

    def send(odd):
        state = piece_out[start:stop, piece_out.shape[1] - LANES :].astype(BF16)
        for peer in range(odd, group, 2):
            here = slice(peer * rows, (peer + 1) * rows)
            first = 0
            for column, count in ranges:
                outbox[here, first : first + count] = piece_out[here, column : column + count].astype(BF16)
                first += count
            outbox[peer * rows : peer * rows + stop - start, width : width + LANES] = state
            outbox[here, width + LANES :] = make_lanes(here).astype(BF16)
        for hop in range(1, group):
            peer, item = copy(hop)

            @pl.when(lax.rem(peer, 2) == odd)
            def _():
                item.start()

    def finish():
        total = outbox[pl.ds(place * rows, rows), :].astype(F32)
        for hop in range(1, group):
            copy(hop)[1].wait_recv()
            total = total + inbox[hop - 1].astype(F32)
        common_ref[...] = total[:, :width]
        state_ref[...] = total[: stop - start, width : width + LANES]
        gains_ref[...] = total[:, width + LANES :]
        for hop in range(1, group):
            copy(hop)[1].wait_send()

    return send, finish


PRODUCT_TURNS = (
    (0, 2, 0, 0), (0, 2, 1, 1), (1, 2, 2, 0), (0, 2, 3, 2), (1, 3, 0, 1), (2, 3, 0, 0), (0, 3, 1, 3), (1, 3, 2, 2),
    (2, 3, 2, 1), (1, 4, 0, 3), (2, 4, 0, 2), (2, 4, 3, 3), (3, 2, 0, 0), (3, 2, 1, 1), (3, 2, 2, 2), (3, 2, 3, 3),
    (3, 3, 0, 4), (3, 3, 1, 5), (3, 3, 2, 6), (3, 3, 3, 7),
)


GATHER_TURNS = (
    (0, 0, 1, 0), (0, 0, 3, 1), (0, 1, 1, 2), (0, 1, 3, 3), (1, 2, 1, 0), (1, 2, 2, 1), (2, 2, 3, 0),
    (3, 3, 0, 0), (3, 3, 1, 1), (3, 3, 2, 2), (3, 3, 3, 3), (3, 4, 1, 4), (3, 4, 2, 5),
)


def product_steps(left_refs, x_held, right_ref, piece_refs, left_held, made, left_sem, made_sem):
    total, share = left_held.shape[2:]
    owners = piece_refs[0].shape[0] // share
    widths = [ref.shape[1] for ref in piece_refs]

    def left_copy(tile, which):
        cols = pl.ds(pl.multiple_of(tile * share, share), share)
        slot = lax.rem(tile, 2)
        return pltpu.make_async_copy(left_refs[which].at[:, cols], left_held.at[slot, which], left_sem.at[slot, which])

    def made_copy(tile, which):
        slot = lax.rem(tile, 2)
        first = sum(widths[:which])
        return pltpu.make_async_copy(
            made.at[slot, :, pl.ds(first, widths[which])],
            piece_refs[which].at[pl.ds(tile * share, share)],
            made_sem.at[slot, which],
        )

    def load_left(tile):
        left_copy(tile, 0).start()
        left_copy(tile, 1).start()

    def product(tile):
        slot = lax.rem(tile, 2)

        @pl.when(tile + 1 < owners)
        def _():
            load_left(tile + 1)

        @pl.when(tile >= 2)
        def _():
            made_copy(tile - 2, 0).wait()
            made_copy(tile - 2, 1).wait()

        step = 512
        for which in (0, 1):
            left_copy(tile, which).wait()
            left = left_held[slot, which]
            first = sum(widths[:which])
            for col in range(0, widths[which], step):
                if which == 0:
                    right = x_held[:, :, col : col + step].reshape(total, step)
                else:
                    right = right_ref[:, col : col + step]
                made[slot, :, first + col : first + col + step] = mat_tn(left, right).astype(BF16)
            made_copy(tile, which).start()

    def end():
        for tile in (owners - 2, owners - 1):
            made_copy(tile, 0).wait()
            made_copy(tile, 1).wait()

    return load_left, product, end


def line_sum_kernel(
    group, spread, by_rows, finish, own_count, side_count, piece_count, products, gather_rows, gain_index, ranges,
    state_rows, *refs,
):
    def take(count):
        nonlocal refs
        taken, refs = refs[:count], refs[count:]
        return taken

    x_ref, w_ref = take(2)
    own_refs = take(own_count)
    if products:
        left_refs, (right_ref, extra_ref) = take(2), take(2)
    else:
        piece_refs = take(piece_count)
    gather_refs = take(len(gather_rows))
    if piece_count:
        weight_ref, lanes_ref = take(2)
    (out_ref,) = take(1)
    side_refs = take(side_count)
    if products:
        piece_refs = take(piece_count)
        (extra_out,) = take(1)
    if piece_count:
        (piece_out,) = take(1)
        common_refs = take(3 if ranges else 1)
    full_refs = take(len(gather_rows))
    if gather_rows:
        (next_ref,) = take(1)
    x_held, w_held, load_sem, held, part, sum_send, sum_recv, out_send, out_recv = take(9)
    place = lax.axis_index("tensor")
    away = group - 1 - place
    chunks = LINE_CHUNKS
    rows = x_ref.shape[1] // chunks
    few = rows // 2
    model = out_ref.shape[-1]
    tile = model // group
    more = (place < group - 1, place > 0)
    ahead = (place > 0, place < group - 1)

    def load_x():
        return pltpu.make_async_copy(x_ref, x_held, load_sem.at[group])

    def load_w(index):
        cols = pl.ds(index * tile, tile)
        if by_rows:
            return pltpu.make_async_copy(w_ref.at[cols], w_held.at[cols], load_sem.at[index])
        return pltpu.make_async_copy(w_ref.at[:, cols], w_held.at[:, cols], load_sem.at[index])

    load_x().start()
    for index in range(group):
        load_w(index).start()
    greet(place, group, lax.axis_index("dp"), piece_count + len(gather_rows) > 0, bool(ranges))
    if piece_count:
        begin, add_core, add_near, add_last, end = plane_scatter_steps(piece_refs, piece_out, *take(5), take(9))
        if products:
            load_left, product, product_end = product_steps(left_refs, x_held, right_ref, piece_refs, *take(4))
            load_left(0)
            extra_held, extra_made, extra_sem = take(3)
            extra_load = pltpu.make_async_copy(extra_ref, extra_held, extra_sem.at[2])
            extra_load.start()

            def extra_copy(index):
                slot = lax.rem(index, 2)
                return pltpu.make_async_copy(
                    extra_made.at[slot], extra_out.at[pl.ds(index * CHUNK, CHUNK)], extra_sem.at[slot]
                )

            def extra_product(index):
                if index == 0:
                    extra_load.wait()
                if index >= 2:
                    extra_copy(index - 2).wait()
                left = right_ref[index * CHUNK : (index + 1) * CHUNK, :]
                for col in range(0, model, tile):
                    extra_made[index % 2, :, col : col + tile] = mat(left, extra_held[:, col : col + tile]).astype(BF16)
                extra_copy(index).start()

        else:
            begin()
    if gather_rows:
        pieces = list(zip(gather_refs, full_refs, gather_rows))
        begin, neighbours, corner, end = plane_gather_steps(pieces, *take(3))
        begin()
        next_w, next_held, next_sem = take(3)

        def load_next():
            return pltpu.make_async_copy(full_refs[0], next_w, next_sem.at[2])

        def next_copy(chunk):
            slot = lax.rem(chunk, 2)
            return pltpu.make_async_copy(
                next_held.at[slot], next_ref.at[:, pl.ds(chunk * rows, rows)], next_sem.at[slot]
            )

        def multiply_next(chunk, half):
            width = next_w.shape[1] // 2

            @pl.when((chunk >= 2) & (half == 0))
            def _():
                next_copy(chunk - 2).wait()

            left = out_ref[:, pl.ds(chunk * rows, rows), :].reshape(group * rows, model)
            for first in range(half * width, (half + 1) * width, tile):
                product = mat(left, next_w[:, first : first + tile])
                next_held[lax.rem(chunk, 2), :, :, first : first + tile] = product.reshape(group, rows, tile)
            if half == 1:
                next_copy(chunk).start()

    def multiply(chunk, index):
        left = x_held[:, pl.ds(chunk * rows, rows), :].reshape(group * rows, x_ref.shape[2])
        cols = pl.ds(index * tile, tile)
        product = mat_nt(left, w_held[cols, :]) if by_rows else mat(left, w_held[:, cols])
        part[lax.rem(chunk, 2), :, :, cols] = product.reshape(group, rows, tile)

    def sum_copy(side, chunk, share, half):
        block = held.at[chunk, share + 1 - side, pl.ds(half * few, few)]
        index = 2 * chunk + half
        return pltpu.make_async_remote_copy(
            block, block, sum_send.at[side, index, share], sum_recv.at[side, index, share],
            device_id={"tensor": place + 1 - 2 * side}, device_id_type=MESH,
        )

    def out_copy(side, chunk, source, half):
        block = out_ref.at[source, pl.ds(chunk * rows + half * few, few)]
        index = 2 * chunk + half
        return pltpu.make_async_remote_copy(
            block, block, out_send.at[side, index, source], out_recv.at[side, index, source],
            device_id={"tensor": place + 1 - 2 * side}, device_id_type=MESH,
        )

    if ranges:
        make_lanes = lambda here: gain_lanes(
            lanes_ref[here, :], weight_ref[here, :], piece_out[here, : weight_ref.shape[1]], gain_index
        )
        common_send, common_finish = common_sum(
            group, place, ranges, state_rows, piece_out, make_lanes, common_refs + take(4)
        )

    load_x().wait()
    for index in range(group):
        load_w(index).wait()
        multiply(0, index)

    def pass_out(chunk, slot, half):
        for side in (0, 1):
            source = place - (slot + 1) if side == 0 else place + (slot + 1)

            @pl.when((chunk > 0) & (source >= 0) & (source < group))
            def _():
                out_copy(side, chunk - 1, source, half).wait_recv()

                @pl.when(more[side])
                def _():
                    out_copy(side, chunk - 1, source, half).start()

    def add_on(chunk, slot, half):
        local = pl.ds(half * few, few)
        for side in (0, 1):
            depth = place if side == 0 else away
            share = group - 1 - slot + place if side == 0 else slot - away

            @pl.when((chunk < chunks) & (depth <= slot))
            def _():
                mine = part[lax.rem(chunk, 2), share, local]
                spot = share + 1 - side

                @pl.when(ahead[side])
                def _():
                    sum_copy(side, chunk, share, half).wait_recv()
                    held[chunk, spot, local] = (held[chunk, spot, local].astype(F32) + mine).astype(BF16)

                @pl.when(jnp.logical_not(ahead[side]))
                def _():
                    held[chunk, spot, local] = mine.astype(BF16)

                sum_copy(side, chunk, share, half).start()

    def complete(chunk, half):
        local = pl.ds(half * few, few)

        @pl.when(chunk < chunks)
        def _():
            total = part.at[lax.rem(chunk, 2), place, local]
            for side in (0, 1):

                @pl.when(ahead[side])
                def _():
                    sum_copy(side, chunk, place, half).wait_recv()
                    total[...] += held[chunk, place + 1 - side, local].astype(F32)

            mine = pl.ds(chunk * rows + half * few, few)
            result = finish(total[...], mine, own_refs, side_refs)
            if spread:
                out_ref[place, mine, :] = result
                for side in (0, 1):

                    @pl.when(more[side])
                    def _():
                        out_copy(side, chunk, place, half).start()
            else:
                out_ref[mine, :] = result

    def one_chunk(chunk, carry):
        for slot in range(group):
            for half in (0, 1):
                if slot + 1 < group and spread:
                    pass_out(chunk, slot, half)
                if slot < group - 1:
                    add_on(chunk, slot, half)
                else:
                    complete(chunk, half)

            @pl.when(chunk + 1 < chunks)
            def _():
                multiply(chunk + 1, slot)

            if products:

                @pl.when(chunk < 2)
                def _():
                    product(chunk * group + slot)

                if slot == group - 1:

                    @pl.when(chunk == 1)
                    def _():
                        product_end()
                        begin()

                for step, turn_chunk, turn_slot, index in PRODUCT_TURNS:
                    if turn_slot == slot:

                        @pl.when(chunk == turn_chunk)
                        def _():
                            (add_core, add_near, add_last, extra_product)[step](index)

            if piece_count and not products and slot == 0:

                @pl.when(chunk < chunks)
                def _():
                    add_core(chunk)

            if piece_count and not products and slot == group // 2:

                @pl.when(chunk < chunks)
                def _():
                    add_near(chunk)

            if piece_count and not products and slot == 1:

                @pl.when(chunk > 0)
                def _():
                    add_last(chunk - 1)

            if ranges and slot == 1:

                @pl.when(chunk == chunks // 2)
                def _():
                    common_send(0)

            if gather_rows:
                for step, turn_chunk, turn_slot, index in GATHER_TURNS:
                    if turn_slot == slot:

                        @pl.when(chunk == turn_chunk)
                        def _():
                            if step == 0:
                                neighbours(index)
                            elif step == 1:
                                corner(index)
                            elif step == 2:
                                end()
                                load_next().start()
                            else:
                                if index == 0:
                                    load_next().wait()
                                multiply_next(index // 2, index % 2)

        return carry

    lax.fori_loop(0, chunks + 1 if spread or piece_count else chunks, one_chunk, 0)
    if piece_count:
        if ranges:
            common_send(1)
            common_finish()
        else:
            common_refs[0][...] = gain_lanes(
                lanes_ref[...], weight_ref[...], piece_out[:, : weight_ref.shape[1]], gain_index
            )

    def finish_sends(chunk, carry):
        for half in (0, 1):
            for slot in range(group):
                for side in (0, 1):
                    depth = place if side == 0 else away
                    share = group - 1 - slot + place if side == 0 else slot - away
                    if slot < group - 1:

                        @pl.when(depth <= slot)
                        def _():
                            sum_copy(side, chunk, share, half).wait_send()

                    source = place - slot if side == 0 else place + slot
                    if spread:

                        @pl.when((source >= 0) & (source < group) & more[side])
                        def _():
                            out_copy(side, chunk, source, half).wait_send()

        if piece_count:
            end(chunk)
        return carry

    if gather_rows:
        multiply_next(chunks - 1, 0)
        multiply_next(chunks - 1, 1)
    lax.fori_loop(0, chunks, finish_sends, 0)
    if products:
        extra_copy(6).wait()
        extra_copy(7).wait()
    if gather_rows:
        next_copy(chunks - 2).wait()
        next_copy(chunks - 1).wait()


def line_sum(
    x, w, own, by_rows, finish, side_shapes, group, model, collective_id, name, dp_size,
    spread=True, pieces=(), products=(), gains=None, ranges=(), state_rows=None, gathers=(),
):
    total = x.shape[0]
    rows = total // group
    vmem = pl.BlockSpec(memory_space=pltpu.VMEM)
    anywhere = pl.BlockSpec(memory_space=pl.ANY)
    piece_rows = rows // LINE_CHUNKS
    sems = pltpu.SemaphoreType.DMA((2, 2 * LINE_CHUNKS, group))
    out_shape = [jax.ShapeDtypeStruct((group, rows, model), BF16) if spread else jax.ShapeDtypeStruct((rows, model), F32)]
    out_shape += side_shapes
    scratch = [
        pltpu.VMEM((group, rows, x.shape[1]), BF16),
        pltpu.VMEM(w.shape, BF16),
        pltpu.SemaphoreType.DMA((group + 1,)),
        pltpu.VMEM((LINE_CHUNKS, group + 1, piece_rows, model), BF16),
        pltpu.VMEM((2, group, piece_rows, model), F32),
        sems, sems, sems, sems,
    ]
    late = []
    if products and (dp_size != 8 or group != 4):
        lefts, right = products[:2], products[2]
        pieces = [mat_tn(lefts[0], x).astype(BF16), mat_tn(lefts[1], right).astype(BF16)]
        late = [mat(right, products[3]).astype(BF16)]
        products = ()
    if dp_size != 8:
        if pieces:
            share = pieces[0].shape[0] // dp_size
            parts = [scatter(piece, "dp", 0) if piece.shape[0] > share else lax.psum(piece, "dp") for piece in pieces]
            total_sum = jnp.concatenate(parts, 1).astype(F32)
            late += [total_sum]
            weight, lanes, gain_index = gains
            lanes = gain_lanes(lanes, weight, total_sum[:, : weight.shape[1]], gain_index)
            if ranges:
                columns = [total_sum[:, start : start + count] for start, count in ranges]
                late += [
                    scatter(jnp.concatenate(columns, 1).astype(BF16), "tensor", 0).astype(F32),
                    lax.psum(total_sum[state_rows[0] : state_rows[1], total_sum.shape[1] - LANES :], "tensor"),
                    scatter(lanes, "tensor", 0),
                ]
            else:
                late += [lanes]
        late += [plane_gather_plain(array, kind) for array, kind in gathers]
        multiplied, pieces, ranges, gathers = bool(gathers), (), (), ()
    outs = [vmem] * len(out_shape)
    last, gain_index = [], 0
    piece_inputs, piece_specs = list(pieces), [anywhere] * len(pieces)
    if products:
        pieces = [jax.ShapeDtypeStruct((model, x.shape[1]), BF16), jax.ShapeDtypeStruct((model, products[2].shape[1]), BF16)]
        piece_inputs, piece_specs = list(products), [anywhere, anywhere, vmem, anywhere]
        out_shape += pieces + [jax.ShapeDtypeStruct((total, model), BF16)]
        outs += [anywhere] * 3
    if pieces:
        share, width = pieces[0].shape[0] // dp_size, sum(piece.shape[1] for piece in pieces)
        last, gain_index = list(gains[:2]), gains[2]
        out_shape += [jax.ShapeDtypeStruct((share, width), F32)]
        scratch += plane_scatter_scratch(share, width)
        if products:
            scratch += [
                pltpu.VMEM((2, 2, total, share), BF16),
                pltpu.VMEM((2, share, width), BF16),
                pltpu.SemaphoreType.DMA((2, 2)),
                pltpu.SemaphoreType.DMA((2, 2)),
                pltpu.VMEM(products[3].shape, BF16),
                pltpu.VMEM((2, CHUNK, model), BF16),
                pltpu.SemaphoreType.DMA((3,)),
            ]
        if ranges:
            common_width = sum(count for _, count in ranges)
            out_shape += [
                jax.ShapeDtypeStruct((share // group, common_width), F32),
                jax.ShapeDtypeStruct((state_rows[1] - state_rows[0], LANES), F32),
                jax.ShapeDtypeStruct((share // group, LANES), F32),
            ]
            scratch += [
                pltpu.VMEM((share, common_width + 2 * LANES), BF16),
                pltpu.VMEM((group - 1, share // group, common_width + 2 * LANES), BF16),
                pltpu.SemaphoreType.DMA((group - 1,)),
                pltpu.SemaphoreType.DMA((group - 1,)),
            ]
        else:
            out_shape += [jax.ShapeDtypeStruct((share, LANES), F32)]
        outs += [vmem] * (len(out_shape) - len(outs))
    if gathers:
        for array, kind in gathers:
            shape = (dp_size * array.shape[0], array.shape[1]) if kind else (array.shape[0], dp_size * array.shape[1])
            out_shape += [jax.ShapeDtypeStruct(shape, BF16)]
            outs += [anywhere]
        next_width = gathers[0][0].shape[1]
        out_shape += [jax.ShapeDtypeStruct((group, rows, next_width), F32)]
        outs += [anywhere]
        scratch += plane_gather_scratch(len(gathers)) + [
            pltpu.VMEM((model, next_width), BF16),
            pltpu.VMEM((2, group, piece_rows, next_width), F32),
            pltpu.SemaphoreType.DMA((3,)),
        ]
    results = pl.pallas_call(
        functools.partial(
            line_sum_kernel, group, spread, by_rows, finish, len(own), len(side_shapes), len(pieces), bool(products),
            tuple(kind for _, kind in gathers), gain_index, ranges, state_rows,
        ),
        in_specs=[anywhere] * 2 + [vmem] * len(own) + piece_specs + [anywhere] * len(gathers) + [vmem] * len(last),
        out_specs=outs,
        out_shape=out_shape,
        scratch_shapes=scratch,
        compiler_params=pltpu.CompilerParams(
            collective_id=collective_id, has_side_effects=True, vmem_limit_bytes=62 << 20
        ),
        name=name,
    )(x.reshape(group, rows, x.shape[1]), w, *own, *piece_inputs, *[array for array, _ in gathers], *last)
    results = list(results)
    if spread:
        results[0] = results[0].reshape(total, model)
    if gathers:
        results[-1] = results[-1].reshape(total, next_width)
    elif dp_size != 8 and multiplied:
        late += [mat(results[0], late[0])]
    if products:
        del results[1 + len(side_shapes) : 3 + len(side_shapes)]
    return results + late


def unpack_kernel(
    heads, query_cols, first_query, dp_size, group, in_ref, ffn_ref, common_ref, state_ref, gains_ref,
    gain_one, query, pair, output, inner, state, step, conv_inner, conv_state, head, gate_gain, mamba, gain_two,
    expand, shrink,
):
    owner, place = lax.axis_index("dp"), lax.axis_index("tensor")
    channels = heads * PM
    hidden = shrink.shape[0]
    state_cols = 2 * channels + 2 * NS
    inner[:, 0, :] = in_ref[:, :channels]
    inner[:, 1, :] = in_ref[:, channels : 2 * channels]
    step[...] = in_ref[:, state_cols : state_cols + heads]
    query[...] = in_ref[:, first_query : first_query + query_cols]
    first = in_ref.shape[1] - LANES - query_cols - channels
    for row in range(0, query_cols, LANES):
        output[row : row + LANES, :] = in_ref[:, first + row : first + row + LANES].T
    first += query_cols
    for row in range(0, channels, LANES):
        mamba[row : row + LANES, :] = in_ref[:, first + row : first + row + LANES].T
    for tile in range(hidden // HIDDEN_TILE):
        cols = slice(tile * HIDDEN_TILE, (tile + 1) * HIDDEN_TILE)
        for kind in (0, 1):
            start = (2 * tile + kind) * HIDDEN_TILE
            expand[:, kind, cols] = ffn_ref[:, start : start + HIDDEN_TILE]
    for row in range(0, hidden, LANES):
        shrink[row : row + LANES, :] = ffn_ref[:, 2 * hidden + row : 2 * hidden + row + LANES].T
    state[...] = common_ref[:, : 2 * NS]
    pair[...] = common_ref[:, 2 * NS :]
    for lane, gain in ((0, gain_one), (1, gain_two)):
        column = gains_ref[:, lane : lane + 1]
        rows = column.shape[0]
        gain[...] = jnp.sum(jnp.where(iota((rows, rows), 0) == iota((rows, rows), 1), column, 0.0), 0, keepdims=True)
    piece = PM // dp_size
    last = in_ref.shape[1] - LANES
    gate_first = (channels + 2 * NS) // LANES * 8 + 8
    head[...] = in_ref[gate_first - 8 : gate_first - 5, last : last + heads]
    for index in range(heads // 2):
        for start, rows, target in ((2 * NS // LANES * 8, KC + 1, conv_inner), (gate_first, 1, gate_gain)):
            block = in_ref[start + 8 * index : start + 8 * index + 8, last:]
            block = pltpu.roll(block, lax.rem(LANES - owner * piece, LANES), 1)
            for side in (0, 1):
                values = block[:rows, side * PM : side * PM + piece]
                if rows == 1:
                    target[2 * index + side : 2 * index + side + 1, :] = values
                else:
                    target[:, 2 * index + side, :] = values
    width = conv_state.shape[1]
    column = (owner * group + place) * width
    block = state_ref[pl.ds(pl.multiple_of(column // LANES * 8, 8), 8), :]
    block = pltpu.roll(block, lax.rem(LANES - lax.rem(column, LANES), LANES), 1)
    conv_state[...] = block[: KC + 1, :width]


def unpack(in_sum, ffn_sum, common, state, gains, heads, query_cols, first_query, hidden, dp_size, group):
    share, rows, channels, own_cols = in_sum.shape[0], common.shape[0], heads * PM, in_sum.shape[0]
    vmem = pl.BlockSpec(memory_space=pltpu.VMEM)
    shapes = [
        (1, rows), (share, query_cols), (rows, common.shape[1] - 2 * NS), (query_cols, own_cols), (share, 2, channels),
        (rows, 2 * NS), (share, heads), (KC + 1, heads, PM // dp_size), (KC + 1, 2 * NS // (dp_size * group)),
        (3, heads), (heads, PM // dp_size), (channels, own_cols), (1, rows), (share, 2, hidden), (hidden, own_cols),
    ]
    results = list(
        pl.pallas_call(
            functools.partial(unpack_kernel, heads, query_cols, first_query, dp_size, group),
            in_specs=[vmem] * 5,
            out_specs=[vmem] * len(shapes),
            out_shape=[jax.ShapeDtypeStruct(shape, F32) for shape in shapes],
            compiler_params=pltpu.CompilerParams(vmem_limit_bytes=48 << 20),
            name="unpack",
        )(in_sum, ffn_sum, common, state, gains)
    )
    results[0], results[12] = results[0].reshape(rows), results[12].reshape(rows)
    return results


def project_kernel(tokens_ref, gains_ref, w_ref, lin_ref, first_ref, gain_rows_ref):
    @pl.when(pl.program_id(0) == 0)
    def _():
        picks = (iota((8, LANES), 0) + LANES - 2 == iota((8, LANES), 1)).astype(BF16)
        gain_rows_ref[...] = mat_nt(picks, gains_ref[...])
        gain = gain_rows_ref[0:1]

        def normalise(step, carry):
            rows = pl.ds(step * CHUNK, CHUNK)
            values = tokens_ref[rows, :].astype(F32)
            first_ref[rows, :] = (values * rms_rows(values) * gain).astype(BF16)
            return carry

        lax.fori_loop(0, tokens_ref.shape[0] // CHUNK, normalise, 0)

    lin_ref[...] = mat(first_ref[...], w_ref[...])


def project(tokens, weight, gain_block):
    total, model = tokens.shape
    cols = weight.shape[1]
    tile = 512
    return pl.pallas_call(
        project_kernel,
        grid=(cols // tile,),
        in_specs=[
            whole_block(tokens),
            pl.BlockSpec((model, LANES), lambda c: (0, gain_block)),
            pl.BlockSpec((model, tile), lambda c: (0, c)),
        ],
        out_specs=[
            pl.BlockSpec((total, tile), lambda c: (0, c)),
            pl.BlockSpec((total, model), lambda c: (0, 0)),
            pl.BlockSpec((8, model), lambda c: (0, 0)),
        ],
        out_shape=[
            jax.ShapeDtypeStruct((total, cols), F32),
            jax.ShapeDtypeStruct((total, model), BF16),
            jax.ShapeDtypeStruct((8, model), F32),
        ],
        compiler_params=pltpu.CompilerParams(vmem_limit_bytes=56 << 20),
        name="project",
    )(tokens, weight, weight)


def exchange_copies(group, own_ref, slots, send_sem, recv_sem):
    place = lax.axis_index("tensor")
    return [
        pltpu.make_async_remote_copy(
            own_ref, slots.at[hop - 1], send_sem.at[hop - 1], recv_sem.at[hop - 1],
            device_id={"tensor": lax.rem(place + hop, group)}, device_id_type=MESH,
        )
        for hop in range(1, group)
    ]


def exchange_scratch(group, shape):
    return [
        pltpu.VMEM((group - 1,) + shape, F32),
        pltpu.SemaphoreType.DMA((group - 1,)),
        pltpu.SemaphoreType.DMA((group - 1,)),
    ]


def gate_norm_kernel(
    group, square_ref, ssm_ref, gate_ref, gain_ref, attended_ref, mix_ref, inverse_ref, slots, send_sem, recv_sem
):
    greet(lax.axis_index("tensor"), group, None, False, True)
    copies = exchange_copies(group, square_ref, slots, send_sem, recv_sem)
    for copy in copies:
        copy.start()
    total = square_ref[...]
    for hop, copy in enumerate(copies):
        copy.wait_recv()
        total = total + slots[hop]
    inverse_ref[...] = lax.rsqrt(total * (1.0 / DSSM) + EPS)
    query_cols = attended_ref.shape[1]
    mix_ref[:, :query_cols] = attended_ref[...]

    def norm(step, carry):
        rows = pl.ds(step * CHUNK, CHUNK)
        gate = gate_ref[rows, :]
        gated = ssm_ref[rows, :] * gate * sigmoid(gate)
        mix_ref[rows, query_cols:] = (gated * as_column(inverse_ref[step]) * gain_ref[...]).astype(BF16)
        return carry

    lax.fori_loop(0, square_ref.shape[0], norm, 0)
    for copy in copies:
        copy.wait_send()


def gate_norm(square, ssm, lin, gain, attended, group, collective_id):
    total, channels = ssm.shape
    width = attended.shape[1] + channels
    return pl.pallas_call(
        functools.partial(gate_norm_kernel, group),
        grid=(1,),
        in_specs=[
            whole_block(square),
            whole_block(ssm),
            pl.BlockSpec((total, channels), lambda c: (0, 0)),
            whole_block(gain),
            whole_block(attended),
        ],
        out_specs=[pl.BlockSpec((total, width), lambda c: (0, 0)), whole_block(square)],
        out_shape=[jax.ShapeDtypeStruct((total, width), BF16), jax.ShapeDtypeStruct(square.shape, F32)],
        scratch_shapes=exchange_scratch(group, square.shape),
        compiler_params=pltpu.CompilerParams(
            collective_id=collective_id, has_side_effects=True, vmem_limit_bytes=56 << 20
        ),
        name="gate_norm",
    )(square, ssm, lin, gain, attended)


def gate_back_kernel(
    group, query_cols, mix_ref, w_ref, ssm_ref, gate_ref, gain_ref, attended_ref, normed_ref, cross_ref,
    own, slots, send_sem, recv_sem,
):
    step = pl.program_id(0)

    @pl.when(step == 0)
    def _():
        greet(lax.axis_index("tensor"), group, None, False, True)

    grads = mat_nt(mix_ref[...], w_ref[...])
    attended_ref[...] = grads[:, :query_cols].astype(BF16)
    grads = grads[:, query_cols:]
    normed_ref[...] = grads
    gate = gate_ref[...]
    products = ssm_ref[...] * gate * sigmoid(gate) * (grads * gain_ref[...])
    total = products[:, :LANES]
    for index in range(1, products.shape[1] // LANES):
        total = total + products[:, index * LANES : (index + 1) * LANES]
    per_step = ROWS // CHUNK
    for index in range(per_step):
        own[step * per_step + index] = row_sums_as_row(total[index * CHUNK : (index + 1) * CHUNK])

    @pl.when(step == pl.num_programs(0) - 1)
    def _():
        copies = exchange_copies(group, own, slots, send_sem, recv_sem)
        for copy in copies:
            copy.start()
        result = own[...]
        for hop, copy in enumerate(copies):
            copy.wait_recv()
            result = result + slots[hop]
        cross_ref[...] = result
        for copy in copies:
            copy.wait_send()


def gate_back(mix_all, weight_mix, ssm, lin, gain, query_cols, group, collective_id):
    total, channels = ssm.shape
    model = mix_all.shape[1]
    cross = (total // CHUNK, 1, CHUNK)
    by_rows = lambda cols: pl.BlockSpec((ROWS, cols), lambda c: (c, 0))
    return pl.pallas_call(
        functools.partial(gate_back_kernel, group, query_cols),
        grid=(total // ROWS,),
        in_specs=[by_rows(model), whole_block(weight_mix), by_rows(channels), by_rows(channels), whole_block(gain)],
        out_specs=[by_rows(query_cols), by_rows(channels), pl.BlockSpec(cross, lambda c: (0, 0, 0))],
        out_shape=[
            jax.ShapeDtypeStruct((total, query_cols), BF16),
            jax.ShapeDtypeStruct((total, channels), F32),
            jax.ShapeDtypeStruct(cross, F32),
        ],
        scratch_shapes=[pltpu.VMEM(cross, F32)] + exchange_scratch(group, cross),
        compiler_params=pltpu.CompilerParams(
            collective_id=collective_id, has_side_effects=True, vmem_limit_bytes=56 << 20
        ),
        name="gate_back",
    )(mix_all, weight_mix, ssm, lin, gain)


HIDDEN_TILE = 256


def feed_forward_kernel(cot_ref, lin_ref, shrink_ref, act_ref, hidden_ref):
    shrink = shrink_ref[...]
    for first in range(0, cot_ref.shape[0], ROWS):
        rows = slice(first, first + ROWS)
        gate, up = lin_ref[rows, :HIDDEN_TILE], lin_ref[rows, HIDDEN_TILE:]
        sig = sigmoid(gate)
        silu = gate * sig
        act = (silu * up).astype(BF16)
        act_ref[rows, :] = act
        grad = mat_nt(cot_ref[rows, :], shrink)
        hidden_ref[rows, :HIDDEN_TILE] = (grad * up * (sig * (1.0 + gate * (1.0 - sig)))).astype(BF16)
        hidden_ref[rows, HIDDEN_TILE:] = (grad * silu).astype(BF16)


def feed_forward(cot, hidden_lin, shrink):
    total, model = cot.shape
    hidden = shrink.shape[0]
    return pl.pallas_call(
        feed_forward_kernel,
        grid=(hidden // HIDDEN_TILE,),
        in_specs=[
            pl.BlockSpec(memory_space=pltpu.VMEM),
            pl.BlockSpec((total, 2 * HIDDEN_TILE), lambda c: (0, c)),
            pl.BlockSpec((HIDDEN_TILE, model), lambda c: (c, 0)),
        ],
        out_specs=[
            pl.BlockSpec((total, HIDDEN_TILE), lambda c: (0, c)),
            pl.BlockSpec((total, 2 * HIDDEN_TILE), lambda c: (0, c)),
        ],
        out_shape=[
            jax.ShapeDtypeStruct((total, hidden), BF16),
            jax.ShapeDtypeStruct((total, 2 * hidden), BF16),
        ],
        compiler_params=pltpu.CompilerParams(vmem_limit_bytes=60 << 20),
        name="feed_forward",
    )(cot, hidden_lin, shrink)


def mix_finish(total, mine, own_refs, side_refs):
    tokens_ref, gain_ref = own_refs
    middle = tokens_ref[mine, :].astype(F32) + total
    side_refs[0][mine, :] = middle
    return (middle * rms_rows(middle) * gain_ref[...]).astype(BF16)


def second_finish(total, mine, own_refs, side_refs):
    cot_ref, middle_ref, gain_ref = own_refs
    middle = middle_ref[mine, :]
    grad = cot_ref[mine, :].astype(F32) + rms_back(middle, rms_rows(middle), gain_ref[...], total)
    side_refs[0][mine, :] = grad
    return grad.astype(BF16)


def first_finish(total, mine, own_refs, side_refs):
    tokens_ref, middle_ref, gain_ref = own_refs
    tokens = tokens_ref[mine, :].astype(F32)
    return middle_ref[mine, :] + rms_back(tokens, rms_rows(tokens), gain_ref[...], total)


def dot_columns(left, w_ref, cols):
    return mat(left, w_ref[:, cols])


def dot_rows(left, w_ref, cols):
    return mat_nt(left, w_ref[cols, :])


def gather(array, axis_name, axis):
    return lax.all_gather(array, axis_name, axis=axis, tiled=True)


def scatter(array, axis_name, axis):
    return lax.psum_scatter(array, axis_name, scatter_dimension=axis, tiled=True)


def per_device(
    tokens_in, segment_ids, cotangent, norm_first, query_weight, key_value_weight, output_weight,
    inner_weight, state_weight, step_weight, conv_inner, conv_state, head_params, gate_gain,
    mamba_weight, norm_second, expand_weight, shrink_weight,
):
    dp_size = lax.axis_size("dp")
    group = lax.axis_size("tensor")
    place = lax.axis_index("tensor")
    total = segment_ids.shape[0]
    own_rows, model = tokens_in.shape
    share = query_weight.shape[0]
    heads = step_weight.shape[1]
    channels = heads * PM
    query_cols = query_weight.shape[1]
    query_heads = query_cols // HEAD_SIZE
    pair_cols = key_value_weight.shape[1]
    hidden = shrink_weight.shape[0]
    state_cols = 2 * channels + 2 * NS
    mixer_cols = state_cols + LANES
    lead = -(-(mixer_cols + query_cols) // pair_cols) * pair_cols

    step_block = jnp.concatenate(
        [
            step_weight,
            jnp.zeros((share, LANES - 2 - heads), BF16),
            norm_first[:, None],
            norm_second[:, None],
        ],
        1,
    )
    spare = jnp.zeros((share, lead - mixer_cols - query_cols), BF16)
    weight_own = jnp.concatenate(
        [inner_weight.reshape(share, 2 * channels), state_weight, step_block, query_weight, spare, key_value_weight], 1
    )
    weight_mix = gather(jnp.concatenate([output_weight, mamba_weight], 0), "dp", 1)
    tokens_all, weight_in = entry_gather(tokens_in, weight_own, dp_size, group, 1)
    cot_mine, tokens_all, weight_in = lax.optimization_barrier((cotangent, tokens_all, weight_in))
    cot_all = gather(cot_mine, "tensor", 0)

    cosine, sine = angle_tables()
    key_head = (place * query_heads // (QUERY_HEADS // KEY_HEADS)).astype(jnp.int32).reshape(1)
    heads_map = (jnp.arange(channels)[None, :] // PM == jnp.arange(LANES)[:, None]).astype(BF16)
    conv_weight = jnp.concatenate(
        [conv_inner.reshape(KC + 1, channels), conv_state], 1
    ).astype(F32)
    conv_weight = jnp.pad(conv_weight, ((0, 8 - KC - 1), (0, 0)))
    heads_vec = jnp.pad(head_params, ((0, 5), (0, LANES - heads)))
    gate_row = gate_gain.astype(F32).reshape(1, channels)

    lin, first, gains = project(tokens_all, weight_in, mixer_cols // LANES - 1)
    gain_one, gain_two = gains[0:1], gains[1:2]
    query_block = mixer_cols // LANES
    ssm, mixed, square, states = mixer_forward(lin, segment_ids, conv_weight, heads_vec, heads_map, heads)
    attended = attend_forward(lin, query_block, lead, query_heads, key_head, segment_ids, cosine, sine)
    expand_own = jnp.moveaxis(expand_weight.reshape(share, 2, -1, HIDDEN_TILE), 1, 2).reshape(share, 2 * hidden)
    mix_in, inverse = gate_norm(square, ssm, lin, gate_row, attended, group, 4)
    second_all, middle, weight_expand, weight_shrink, hidden_lin = line_sum(
        mix_in, weight_mix, [tokens_in, gain_two], False, mix_finish,
        [jax.ShapeDtypeStruct((own_rows, model), F32)], group, model, 2, "mix_sum", dp_size,
        gathers=[(expand_own, True), (shrink_weight, False)],
    )
    act, grad_hidden = feed_forward(cot_all, hidden_lin, weight_shrink)
    lanes = jnp.concatenate(
        [
            (1.0 / norm_first.astype(F32))[:, None],
            (1.0 / norm_second.astype(F32))[:, None],
            jnp.zeros((share, LANES - 2), F32),
        ],
        1,
    )
    mix_all, grad_middle, ffn_part, ffn_sum, lanes = line_sum(
        grad_hidden, weight_expand, [cotangent, middle, gain_two], True, second_finish,
        [jax.ShapeDtypeStruct((own_rows, model), F32)], group, model, 3, "second_sum", dp_size,
        products=(second_all, cot_all, act, weight_shrink), gains=(expand_own, lanes, 1),
    )
    ffn_part, mix_all = lax.optimization_barrier((ffn_part, mix_all))
    ffn_out = scatter(ffn_part, "tensor", 0)

    grad_attended, grad_normed, cross = gate_back(mix_all, weight_mix, ssm, lin, gate_row, query_cols, group, 5)
    grad_lin, small, grad_mix_weight = mixer_backward(
        lin, segment_ids, conv_weight, heads_vec, heads_map, gate_row, grad_normed, inverse, cross,
        ssm, mixed, states, heads, lead, share, mix_all, mix_in,
    )
    grad_lin = attend_backward(
        lin, query_block, lead, query_heads, key_head, segment_ids, cosine, sine, grad_attended, grad_lin
    )
    grad_in = mat_tn(first, grad_lin).astype(BF16)
    grad_lin, ffn_out = lax.optimization_barrier((grad_lin, ffn_out))
    block_out = (middle + ffn_out.astype(F32)).astype(BF16)
    grad_tokens, in_sum, common, state, gain_sums = line_sum(
        grad_lin, weight_in, [tokens_in, grad_middle, gain_one], True, first_finish,
        [], group, model, 6, "first_sum", dp_size, spread=False,
        pieces=[grad_in, grad_mix_weight, small.astype(BF16)], gains=(weight_own, lanes, 0),
        ranges=((2 * channels, 2 * NS), (lead, pair_cols)),
        state_rows=(0, 2 * NS // LANES * 8),
    )
    grads = unpack(
        in_sum, ffn_sum, common, state, gain_sums, heads, query_cols, mixer_cols, hidden, dp_size, group
    )
    return (block_out, grad_tokens, *grads)


def solution(mesh):
    return jax.shard_map(
        per_device,
        mesh=mesh,
        in_specs=(
            P(("dp", "tensor"), None),
            P("dp"),
            P(("dp", "tensor"), None),
            P("dp"),
            P("dp", "tensor"),
            P("dp", None),
            P("tensor", "dp"),
            P("dp", None, "tensor"),
            P("dp", None),
            P("dp", "tensor"),
            P(None, "tensor", None),
            P(),
            P(None, "tensor"),
            P("tensor", None),
            P("tensor", "dp"),
            P("dp"),
            P("dp", None, "tensor"),
            P("tensor", "dp"),
        ),
        out_specs=(
            P(("dp", "tensor"), None),
            P(("dp", "tensor"), None),
            P(("dp", "tensor")),
            P("dp", "tensor"),
            P(("dp", "tensor"), None),
            P("tensor", "dp"),
            P("dp", None, "tensor"),
            P(("dp", "tensor"), None),
            P("dp", "tensor"),
            P(None, "tensor", "dp"),
            P(None, ("dp", "tensor")),
            P(None, "tensor"),
            P("tensor", "dp"),
            P("tensor", "dp"),
            P(("dp", "tensor")),
            P("dp", None, "tensor"),
            P("tensor", "dp"),
        ),
        check_vma=False,
    )
```
